32 devices in a mesh: dp: 8 (over z, core), fsdp: 4 (over y, x).
Axes of the slice: x: 2, y: 2, z: 4, core: 2. Of those that a mesh axis runs over, the one named last changes fastest.
Arguments:
- tokens: bfloat16 [512, 196, 432], P(('dp', 'fsdp')), may hold values from -6 to 6
- keep_mask: int32 [512, 196], P(('dp', 'fsdp')), may hold values from 0 to 1, as said below
- cotangent: bfloat16 [512, 196, 432], P(('dp', 'fsdp')), may hold values from -6 to 6
- qk_weight: float32 [432, 864], P('dp', 'fsdp'), may hold values from -0.3125 to 0.3125
- qk_first: float32 [432, 864], P('dp', 'fsdp'), may hold values from -0.00390625 to 0.00390625
- qk_second: float32 [432, 864], P('dp', 'fsdp'), may hold values from 4.4653063e-07 to 1.7861225e-06
- value_weight: float32 [432, 432], P('fsdp', 'dp'), may hold values from -0.3125 to 0.3125
- value_first: float32 [432, 432], P('fsdp', 'dp'), may hold values from -0.00390625 to 0.00390625
- value_second: float32 [432, 432], P('fsdp', 'dp'), may hold values from 4.4653063e-07 to 1.7861225e-06
- out_weight: float32 [432, 432], P('fsdp', 'dp'), may hold values from -0.625 to 0.625
- out_first: float32 [432, 432], P('fsdp', 'dp'), may hold values from -0.00390625 to 0.00390625
- out_second: float32 [432, 432], P('fsdp', 'dp'), may hold values from 4.4653063e-07 to 1.7861225e-06
- up_weight: float32 [432, 1728], P('fsdp', 'dp'), may hold values from -0.3125 to 0.3125
- up_first: float32 [432, 1728], P('fsdp', 'dp'), may hold values from -0.00390625 to 0.00390625
- up_second: float32 [432, 1728], P('fsdp', 'dp'), may hold values from 4.4653063e-07 to 1.7861225e-06
- down_weight: float32 [1728, 432], P('dp', 'fsdp'), may hold values from -0.15625 to 0.15625
- down_first: float32 [1728, 432], P('dp', 'fsdp'), may hold values from -0.00390625 to 0.00390625
- down_second: float32 [1728, 432], P('dp', 'fsdp'), may hold values from 4.4653063e-07 to 1.7861225e-06
- vectors: float32 [6, 432], P(None, 'fsdp'), may hold values from -1.2 to 2.45
- vectors_first: float32 [6, 432], P(None, 'fsdp'), may hold values from -0.01171875 to 0.01171875
- vectors_second: float32 [6, 432], P(None, 'fsdp'), may hold values from 4.0187756e-06 to 1.6075102e-05
- up_bias: float32 [1728], P('fsdp'), may hold values from -1.5 to 1.5
- up_bias_first: float32 [1728], P('fsdp'), may hold values from -0.00390625 to 0.00390625
- up_bias_second: float32 [1728], P('fsdp'), may hold values from 4.4653063e-07 to 1.7861225e-06
- locality: float32 [4, 9], replicated, may hold values from -3 to 3
- locality_first: float32 [4, 9], replicated, may hold values from -0.125 to 0.125
- locality_second: float32 [4, 9], replicated, may hold values from 0.00040187757 to 0.0016075103
Outputs:
- result: bfloat16 [512, 196, 432], P(('dp', 'fsdp'))
- token_grad: bfloat16 [512, 196, 432], P(('dp', 'fsdp'))
- grad_norm: float32 [], replicated
- qk_new: float32 [432, 864], P('dp', 'fsdp')
- qk_copy: bfloat16 [432, 864], P('dp', 'fsdp')
- qk_moment: float32 [432, 864], P('dp', 'fsdp')
- qk_square: float32 [432, 864], P('dp', 'fsdp')
- value_new: float32 [432, 432], P('fsdp', 'dp')
- value_copy: bfloat16 [432, 432], P('fsdp', 'dp')
- value_moment: float32 [432, 432], P('fsdp', 'dp')
- value_square: float32 [432, 432], P('fsdp', 'dp')
- out_new: float32 [432, 432], P('fsdp', 'dp')
- out_copy: bfloat16 [432, 432], P('fsdp', 'dp')
- out_moment: float32 [432, 432], P('fsdp', 'dp')
- out_square: float32 [432, 432], P('fsdp', 'dp')
- up_new: float32 [432, 1728], P('fsdp', 'dp')
- up_copy: bfloat16 [432, 1728], P('fsdp', 'dp')
- up_moment: float32 [432, 1728], P('fsdp', 'dp')
- up_square: float32 [432, 1728], P('fsdp', 'dp')
- down_new: float32 [1728, 432], P('dp', 'fsdp')
- down_copy: bfloat16 [1728, 432], P('dp', 'fsdp')
- down_moment: float32 [1728, 432], P('dp', 'fsdp')
- down_square: float32 [1728, 432], P('dp', 'fsdp')
- vectors_new: float32 [6, 432], P(None, 'fsdp')
- vectors_moment: float32 [6, 432], P(None, 'fsdp')
- vectors_square: float32 [6, 432], P(None, 'fsdp')
- up_bias_new: float32 [1728], P('fsdp')
- up_bias_moment: float32 [1728], P('fsdp')
- up_bias_square: float32 [1728], P('fsdp')
- locality_new: float32 [4, 9], replicated
- locality_moment: float32 [4, 9], replicated
- locality_square: float32 [4, 9], replicated
The draws below stay inside these ranges and needn't reach their ends.
Inputs may be any that keep to these rules, and one draw needn't show every extreme that they name: `keep_mask`: every image keeps at least one of its 196 slots.
All inputs are finite; a program needn't handle non-finite values.
Results may differ from the reference program's by a relative error of at most 0.02.
Values may be sent and summed in bfloat16 or wider, within the bound.
A program may use at most 320 MiB of HBM per device.

```python
import math
import jax
import jax.numpy as jnp
from jax import lax

D = 432
HEADS = 9
FF = 1728
GRID = 14
STEP = 5
SLOTS = 196
IMAGES = 512


def draw_keep_mask(key, part):
    key = jax.random.fold_in(key, 11)
    first_key, second_key = jax.random.split(key)
    slot_count = GRID * GRID
    ranks = jax.random.randint(first_key, (IMAGES, slot_count), 0, 1000)
    image_index = jnp.arange(IMAGES, dtype=jnp.int32)[:, None]
    level = 300 + 600 * image_index // IMAGES
    forced = jax.random.randint(second_key, (IMAGES, 1), 0, slot_count)
    slot_index = jnp.arange(slot_count, dtype=jnp.int32)[None, :]
    return jnp.where((ranks < level) | (slot_index == forced), 1, 0).astype(jnp.int32)


def draw_vectors(key, part):
    key = jax.random.fold_in(key, 12)
    first_key, second_key = jax.random.split(key)
    column = jnp.arange(D, dtype=jnp.float32)[None, :] / D
    gains = (0.5 + column) * jax.random.uniform(first_key, (6, D), jnp.float32, 0.75, 1.25)
    shifts = 0.3 * jnp.clip(jax.random.normal(second_key, (6, D), jnp.float32), -4.0, 4.0)
    row_index = jnp.arange(6, dtype=jnp.int32)[:, None]
    return jnp.where((row_index == 0) | (row_index == 2), gains, shifts).astype(jnp.float32)


def draw_locality(key, part):
    key = jax.random.fold_in(key, 13)
    first_key, second_key, third_key = jax.random.split(key, 3)
    slopes = 0.25 * jnp.clip(jax.random.normal(first_key, (4, HEADS), jnp.float32), -4.0, 4.0)
    strength = jnp.exp(jax.random.uniform(second_key, (4, HEADS), jnp.float32, jnp.log(0.003), jnp.log(0.03)))
    gating = jnp.clip(jax.random.normal(third_key, (4, HEADS), jnp.float32), -3.0, 3.0)
    row_index = jnp.arange(4, dtype=jnp.int32)[:, None]
    picked = jnp.where(row_index == 2, -strength, slopes)
    return jnp.where(row_index == 3, gating, picked).astype(jnp.float32)


def levels(stream_key, shape, cuts, low, top_value):
    gain = 1.0
    for axis_at, parts in cuts:
        heights = jax.random.uniform(jax.random.fold_in(jax.random.fold_in(stream_key, 6), axis_at), (parts,), jnp.float32, low / len(cuts), top_value / len(cuts))
        gain = gain * jnp.repeat(jnp.exp(heights), shape[axis_at] // parts).reshape((-1,) + (1,) * (len(shape) - 1 - axis_at))
    return gain


def gaussian(stream_key, dims, width, bound, cuts=(), kind=jnp.bfloat16):
    values = jax.random.normal(stream_key, dims, jnp.float32) * width
    if len(cuts) > 0:
        values = levels(stream_key, dims, cuts, -0.22, 0.18) * values
    return jnp.clip(values, min=-bound, max=bound).astype(kind)


def setup_inputs(seed: int = 0) -> dict:
    streams_of = jax.random.split(jax.random.key(seed), 28)
    return {
        "tokens": gaussian(streams_of[0], (IMAGES, SLOTS, D), 1.0, 6.0, ((0, 32),)),
        "keep_mask": draw_keep_mask(jax.random.fold_in(streams_of[27], 71), 0),
        "cotangent": gaussian(streams_of[2], (IMAGES, SLOTS, D), 1.0, 6.0, ((0, 32),)),
        "qk_weight": gaussian(streams_of[3], (D, 2 * D), D ** -0.5, 0.3125, ((0, 8), (1, 4)), jnp.float32),
        "qk_first": gaussian(streams_of[4], (D, 2 * D), ((2 * D * (2 * D + FF)) ** -0.5), 0.00390625, ((0, 8), (1, 4)), jnp.float32),
        "qk_second": jnp.clip(jnp.exp(math.log(1.7861225387605373e-06) - 1.3862944 * jax.random.uniform(streams_of[5], (D, 2 * D), jnp.float32) ** levels(streams_of[5], (D, 2 * D), ((0, 8), (1, 4)), -0.2, 0.2)), 4.465306346901343e-07, 1.7861225387605373e-06),
        "value_weight": gaussian(streams_of[6], (D, D), D ** -0.5, 0.3125, ((0, 4), (1, 8)), jnp.float32),
        "value_first": gaussian(streams_of[7], (D, D), ((2 * D * (2 * D + FF)) ** -0.5), 0.00390625, ((0, 4), (1, 8)), jnp.float32),
        "value_second": jnp.clip(jnp.exp(math.log(1.7861225387605373e-06) - 1.3862944 * jax.random.uniform(streams_of[8], (D, D), jnp.float32) ** levels(streams_of[8], (D, D), ((0, 4), (1, 8)), -0.2, 0.2)), 4.465306346901343e-07, 1.7861225387605373e-06),
        "out_weight": gaussian(streams_of[9], (D, D), (D // 4) ** -0.5, 0.625, ((0, 4), (1, 8)), jnp.float32),
        "out_first": gaussian(streams_of[10], (D, D), ((2 * D * (2 * D + FF)) ** -0.5), 0.00390625, ((0, 4), (1, 8)), jnp.float32),
        "out_second": jnp.clip(jnp.exp(math.log(1.7861225387605373e-06) - 1.3862944 * jax.random.uniform(streams_of[11], (D, D), jnp.float32) ** levels(streams_of[11], (D, D), ((0, 4), (1, 8)), -0.2, 0.2)), 4.465306346901343e-07, 1.7861225387605373e-06),
        "up_weight": gaussian(streams_of[12], (D, FF), D ** -0.5, 0.3125, ((0, 4), (1, 8)), jnp.float32),
        "up_first": gaussian(streams_of[13], (D, FF), ((2 * D * (2 * D + FF)) ** -0.5), 0.00390625, ((0, 4), (1, 8)), jnp.float32),
        "up_second": jnp.clip(jnp.exp(math.log(1.7861225387605373e-06) - 1.3862944 * jax.random.uniform(streams_of[14], (D, FF), jnp.float32) ** levels(streams_of[14], (D, FF), ((0, 4), (1, 8)), -0.2, 0.2)), 4.465306346901343e-07, 1.7861225387605373e-06),
        "down_weight": gaussian(streams_of[15], (FF, D), FF ** -0.5, 0.15625, ((0, 8), (1, 4)), jnp.float32),
        "down_first": gaussian(streams_of[16], (FF, D), ((2 * D * (2 * D + FF)) ** -0.5), 0.00390625, ((0, 8), (1, 4)), jnp.float32),
        "down_second": jnp.clip(jnp.exp(math.log(1.7861225387605373e-06) - 1.3862944 * jax.random.uniform(streams_of[17], (FF, D), jnp.float32) ** levels(streams_of[17], (FF, D), ((0, 8), (1, 4)), -0.2, 0.2)), 4.465306346901343e-07, 1.7861225387605373e-06),
        "vectors": draw_vectors(jax.random.fold_in(streams_of[27], 71), 0),
        "vectors_first": gaussian(streams_of[19], (6, D), (3 * (2 * D * (2 * D + FF)) ** -0.5), 0.01171875, ((1, 4),), jnp.float32),
        "vectors_second": jnp.clip(jnp.exp(math.log(1.6075102394097485e-05) - 1.3862944 * jax.random.uniform(streams_of[20], (6, D), jnp.float32) ** levels(streams_of[20], (6, D), ((1, 4),), -0.2, 0.2)), 4.018775598524371e-06, 1.6075102394097485e-05),
        "up_bias": gaussian(streams_of[21], (FF,), 0.3, 1.5, ((0, 4),), jnp.float32),
        "up_bias_first": gaussian(streams_of[22], (FF,), ((2 * D * (2 * D + FF)) ** -0.5), 0.00390625, ((0, 4),), jnp.float32),
        "up_bias_second": jnp.clip(jnp.exp(math.log(1.7861225387605373e-06) - 1.3862944 * jax.random.uniform(streams_of[23], (FF,), jnp.float32) ** levels(streams_of[23], (FF,), ((0, 4),), -0.2, 0.2)), 4.465306346901343e-07, 1.7861225387605373e-06),
        "locality": draw_locality(jax.random.fold_in(streams_of[27], 71), 0),
        "locality_first": gaussian(streams_of[25], (4, HEADS), (30 * (2 * D * (2 * D + FF)) ** -0.5), 0.125, (), jnp.float32),
        "locality_second": jnp.clip(jnp.exp(jax.random.uniform(streams_of[26], (4, HEADS), jnp.float32, math.log(0.00040187757), math.log(0.0016075103))), 0.00040187757, 0.0016075103),
    }


@jax.custom_vjp
def low(v):
    return lax.optimization_barrier(v.astype(jnp.bfloat16)).astype(jnp.float32)

@jax.custom_vjp
def low_back(v):
    return v

def low_keep(v):
    return (low(v), None)

def low_pass(kept, grad):
    return (grad,)

def back_keep(v):
    return (v, None)

def back_low(kept, grad):
    return (low(grad),)
low.defvjp(low_keep, low_pass)
low_back.defvjp(back_keep, back_low)
highest = lax.Precision.HIGHEST
norm_eps = 1e-06
learn_rate = 0.03
small_rate = 0.3
beta_one = 0.5
beta_two = 0.5
adam_eps = 1e-08
weight_decay = 0.05
clip_limit = 1.0

def layer_norm(x, gain_vec, shift_vec):
    center = x - lax.optimization_barrier(jnp.mean(x, axis=-1, keepdims=True))
    spread = lax.optimization_barrier(jnp.mean(center * center, axis=-1, keepdims=True))
    return center * lax.rsqrt(spread + norm_eps) * gain_vec + shift_vec

def offsets_table():
    slot_index = jnp.arange(GRID * GRID, dtype=jnp.int32)
    row_place = (slot_index // GRID).astype(jnp.float32)
    col_place = (slot_index % GRID).astype(jnp.float32)
    horizontal = col_place[None, :] - col_place[:, None]
    vertical = row_place[None, :] - row_place[:, None]
    return jnp.stack([horizontal, vertical, horizontal * horizontal + vertical * vertical], axis=0)

def block(x, visible, params):
    qk_w, value_w, out_w, up_w, down_w, vectors, up_b, locality = params
    b, s, d = x.shape
    head_count = locality.shape[1]
    head_width = d // head_count
    offset_table = offsets_table()
    weight = visible[:, :, None]
    hidden = low(layer_norm(x, vectors[0], vectors[1]))
    joint_proj = low(low_back(jnp.einsum('bsd,de->bse', hidden, low(qk_w), precision=highest)))
    values = low(low_back(jnp.einsum('bsd,de->bse', hidden, low(value_w), precision=highest)))
    queries = joint_proj[..., :d].reshape(b, s, head_count, head_width)
    key_heads = joint_proj[..., d:].reshape(b, s, head_count, head_width)
    scores = low_back(jnp.einsum('bqhe,bkhe->bhqk', queries, key_heads, precision=highest) * head_width ** (-0.5))
    open_keys = visible[:, None, None, :] > 0
    content = jax.nn.softmax(jnp.where(open_keys, scores, -1e+30), axis=-1)
    placed = jnp.einsum('ch,cqk->hqk', locality[:3], offset_table, precision=highest)
    positional = jax.nn.softmax(jnp.where(open_keys, placed[None], -1e+30), axis=-1)
    gating = jax.nn.sigmoid(locality[3])[None, :, None, None]
    mixing = low((1.0 - gating) * content + gating * positional)
    mixture = jnp.einsum('bhqk,bkhe->bqhe', mixing, values.reshape(b, s, head_count, head_width), precision=highest)
    mixture = low(low_back(mixture.reshape(b, s, d)))
    branch = low_back(jnp.einsum('bsd,de->bse', mixture, low(out_w), precision=highest) + vectors[4])
    middle = x + weight * branch
    second = low(layer_norm(middle, vectors[2], vectors[3]))
    upward = low_back(jnp.einsum('bsd,df->bsf', second, low(up_w), precision=highest) + up_b)
    activated = low(jax.nn.gelu(upward, approximate=False))
    downward = jnp.einsum('bsf,fd->bsd', activated, low(down_w), precision=highest) + vectors[5]
    return middle + weight * downward

def adamw(parameter, moment_one, moment_two, gradient, rate, decay_rate):
    first_new = beta_one * moment_one + (1.0 - beta_one) * gradient
    second_new = beta_two * moment_two + (1.0 - beta_two) * gradient * gradient
    first_hat = first_new / (1.0 - beta_one ** STEP)
    second_hat = second_new / (1.0 - beta_two ** STEP)
    new_value = parameter - rate * (first_hat / (jnp.sqrt(second_hat) + adam_eps) + decay_rate * parameter)
    return (new_value, first_new, second_new)

def reference(tokens, keep_mask, cotangent, qk_weight, qk_first, qk_second, value_weight, value_first, value_second, out_weight, out_first, out_second, up_weight, up_first, up_second, down_weight, down_first, down_second, vectors, vectors_first, vectors_second, up_bias, up_bias_first, up_bias_second, locality, locality_first, locality_second):
    visible = keep_mask.astype(jnp.float32)
    group_size = math.gcd(IMAGES, 16)
    slot_count = GRID * GRID
    params = (qk_weight, value_weight, out_weight, up_weight, down_weight, vectors, up_bias, locality)
    checked = jax.checkpoint(block)

    def forward(x, weights):
        stacked = x.reshape(IMAGES // group_size, group_size, slot_count, D)
        mask_groups = visible.reshape(IMAGES // group_size, group_size, slot_count)
        outputs = lax.map(lambda pair_in: checked(pair_in[0], pair_in[1], weights), (stacked, mask_groups))
        return outputs.reshape(IMAGES, slot_count, D)
    result, pullback = jax.vjp(forward, tokens.astype(jnp.float32), params)
    token_grad, grads = pullback(cotangent.astype(jnp.float32))
    square_sum = jnp.float32(0.0)
    for gradient in grads:
        square_sum = square_sum + jnp.sum(gradient * gradient)
    grad_norm = jnp.sqrt(square_sum)
    factor = clip_limit / jnp.maximum(grad_norm, clip_limit)
    moments = ((qk_first, qk_second), (value_first, value_second), (out_first, out_second), (up_first, up_second), (down_first, down_second), (vectors_first, vectors_second), (up_bias_first, up_bias_second), (locality_first, locality_second))
    outputs = [result.astype(jnp.bfloat16), token_grad.astype(jnp.bfloat16), grad_norm]
    for position in range(8):
        decay_rate = weight_decay if position < 5 else 0.0
        rate = learn_rate if position < 5 else small_rate
        new_value, first_new, second_new = adamw(params[position], moments[position][0], moments[position][1], grads[position] * factor, rate, decay_rate)
        if position < 5:
            outputs.extend([new_value, new_value.astype(jnp.bfloat16), first_new, second_new])
        else:
            outputs.extend([new_value, first_new, second_new])
    return tuple(outputs)
```

```python
from functools import partial

import jax
import jax.numpy as jnp
from jax import lax
from jax.experimental import pallas as pl
from jax.experimental.pallas import tpu as pltpu
from jax.sharding import PartitionSpec as P

GRID = 14
STEP = 5
PITCH = 256

norm_eps = 1e-06
learn_rate = 0.03
small_rate = 0.3
beta_one = 0.5
beta_two = 0.5
adam_eps = 1e-08
weight_decay = 0.05
clip_limit = 1.0

LOG2E = 1.4426950408889634
ERF_P = 0.3275911 * 0.5**0.5
ERF_A = (0.254829592, -0.284496736, 1.421413741, -1.453152027, 1.061405429)
PHI_ZERO = 0.3989422804014327

f32 = jnp.float32
bf16 = jnp.bfloat16


def mm(a, b):
    return lax.dot_general(a, b, (((1,), (0,)), ((), ())), preferred_element_type=f32)


def mm_nt(a, b):
    return lax.dot_general(a, b, (((1,), (1,)), ((), ())), preferred_element_type=f32)


def gelu_parts(u):
    slope = 1.0 + ERF_P * jnp.abs(u)
    rough = pl.reciprocal(slope, approx=True)
    t = rough * (2.0 - slope * rough)
    poly = ERF_A[4] * 0.5
    for term in (ERF_A[3], ERF_A[2], ERF_A[1], ERF_A[0]):
        poly = poly * t + term * 0.5
    bell = jnp.exp2(u * u * (-0.5 * LOG2E))
    tail = poly * t * bell
    cdf = jnp.where(u >= 0, 1.0 - tail, tail)
    return u * cdf, cdf + u * bell * PHI_ZERO


def block_kernel(
    images,
    slots,
    heads,
    locality_ref,
    tok_ref,
    cot_ref,
    vis_ref,
    wqkvt_ref,
    wqkv_ref,
    woutt_ref,
    wout_ref,
    wupt_ref,
    wup_ref,
    wdownt_ref,
    wdown_ref,
    vec_ref,
    upb_ref,
    res_ref,
    tgrad_ref,
    gqkv_ref,
    gout_ref,
    gup_ref,
    gdown_ref,
    gvec_ref,
    gupb_ref,
    gloc_ref,
    eye,
    pad_in,
    placed,
    acc_qkv,
    acc_out,
    acc_up,
    acc_down,
    acc_vec,
    acc_upb,
    acc_place,
    acc_gate,
    x_s,
    hid_s,
    qkvt_s,
    kn_s,
    vn_s,
    win_s,
    winall_s,
    pa_s,
    pb_s,
    mix_s,
    ds_s,
    mixture_s,
    xh2_s,
    second_s,
    mid_s,
    cot_s,
    dlow_s,
    act_s,
    ug_s,
    dot_s,
    dqkv_s,
):
    d = tok_ref.shape[-1]
    ff = upb_ref.shape[0]
    hw = d // heads
    keys = placed.shape[1]
    n = images * PITCH
    scale = hw**-0.5
    step = pl.program_id(0)

    @pl.when(step == 0)
    def _():
        rows = lax.broadcasted_iota(jnp.int32, (PITCH, PITCH), 0)
        cols = lax.broadcasted_iota(jnp.int32, (PITCH, PITCH), 1)
        eye[...] = jnp.where(rows == cols, 1.0, 0.0).astype(bf16)
        pad_in[...] = jnp.zeros_like(pad_in)
        j = lax.broadcasted_iota(jnp.int32, (keys, PITCH), 0)
        i = lax.broadcasted_iota(jnp.int32, (keys, PITCH), 1)
        rj, ri = j // GRID, i // GRID
        dc = ((j - rj * GRID) - (i - ri * GRID)).astype(f32)
        dr = (rj - ri).astype(f32)
        far = dc * dc + dr * dr
        for h in range(heads):
            placed[h] = locality_ref[0, h] * dc + locality_ref[1, h] * dr + locality_ref[2, h] * far
        for ref in (acc_qkv, acc_out, acc_up, acc_down, acc_vec, acc_upb, acc_place, acc_gate, win_s, winall_s, mix_s, ds_s, qkvt_s):
            ref[...] = jnp.zeros_like(ref)

    def lanes(b):
        return pl.ds(b * PITCH, PITCH)

    def vec(k):
        return jnp.concatenate([vec_ref[k]] * (n // 128), axis=1)

    def fold(v):
        total = v[:, 0:128]
        for k in range(1, n // 128):
            total = total + v[:, 128 * k : 128 * (k + 1)]
        return total

    def turn_in(ref, b):
        pad_in[0:slots, 0:d] = ref[b]
        parts = []
        for lo in range(0, d, PITCH):
            hi = min(lo + PITCH, d)
            parts.append(mm_nt(eye[0 : hi - lo, 0 : hi - lo], pad_in[:, lo:hi]))
        return jnp.concatenate(parts, axis=0)

    visible = jnp.concatenate([vis_ref[b, 0:1, :] for b in range(images)], axis=1)

    for b in range(images):
        x_s[:, b * PITCH : (b + 1) * PITCH] = turn_in(tok_ref, b)
        cot_s[:, b * PITCH : (b + 1) * PITCH] = turn_in(cot_ref, b)
    dlow_s[...] = (cot_s[...] * visible).astype(bf16)
    acc_vec[5] += fold(cot_s[...] * visible)

    x = x_s[...]
    mean1 = jnp.mean(x, axis=0, keepdims=True)
    center = x - mean1
    rstd1 = lax.rsqrt(jnp.mean(center * center, axis=0, keepdims=True) + norm_eps)
    hid_s[...] = (center * rstd1 * vec(0) + vec(1)).astype(bf16)
    qkvt_s[...] = mm(wqkvt_ref[...], hid_s[...]).astype(bf16)

    sig, cosig = [], []
    for h in range(heads):
        gate = jnp.full((1, PITCH), locality_ref[3, h], f32)
        s = 1.0 / (1.0 + jnp.exp(-gate))
        sig.append(s)
        cosig.append(1.0 - s)

    wins = []
    for h in range(heads):
        lo = (h * hw) // 128 * 128
        wins.append((lo, min(lo + PITCH, d), h * hw - lo))

    for b in range(images):
        cols = slice(b * PITCH, (b + 1) * PITCH)
        kn_s[b] = mm_nt(eye[0:keys, :], qkvt_s[d : 2 * d, cols]).astype(bf16)
        vn_s[b] = mm_nt(eye[0:keys, :], qkvt_s[2 * d : 3 * d, cols]).astype(bf16)
        key_vis = mm_nt(eye[0:keys, :], jnp.broadcast_to(vis_ref[b, 0:1, :], (PITCH, PITCH)).astype(bf16))
        bias = jnp.where(key_vis > 0.5, 0.0, -1e30)
        for h in range(heads):
            lo, hi, at = wins[h]
            win_s[h, at : at + hw, :] = qkvt_s[h * hw : (h + 1) * hw, cols]
            scores = mm(kn_s[b, :, lo:hi], win_s[h, 0 : hi - lo, :]) * (scale * LOG2E) + bias
            p = jnp.exp2(scores - jnp.max(scores, axis=0, keepdims=True))
            pa = p * (cosig[h] / jnp.sum(p, axis=0, keepdims=True))
            z = placed[h] + bias
            e = jnp.exp(z - jnp.max(z, axis=0, keepdims=True))
            pb = e * (sig[h] / jnp.sum(e, axis=0, keepdims=True))
            pa_s[b, h] = pa
            pb_s[b, h] = pb
            mix_s[b, h, 0:keys, :] = (pa + pb).astype(bf16)
            mixture_s[h * hw : (h + 1) * hw, cols] = mm(
                qkvt_s[2 * d + h * hw : 2 * d + (h + 1) * hw, cols], mix_s[b, h]
            ).astype(bf16)

    branch = mm(woutt_ref[...], mixture_s[...]) + vec(4)
    middle = x_s[...] + visible * branch
    mid_s[...] = middle
    mean2 = jnp.mean(middle, axis=0, keepdims=True)
    center = middle - mean2
    rstd2 = lax.rsqrt(jnp.mean(center * center, axis=0, keepdims=True) + norm_eps)
    xh2_s[...] = center * rstd2
    second_s[...] = (xh2_s[...] * vec(2) + vec(3)).astype(bf16)

    chunk = d
    for c in range(0, ff, chunk):
        part = slice(c, c + chunk)
        up = mm(wupt_ref[part, :], second_s[...]) + jnp.concatenate([upb_ref[part, :]] * (n // 128), axis=1)
        back = mm(wdown_ref[part, :], dlow_s[...])
        act, slope = gelu_parts(up)
        act_s[part, :] = act.astype(bf16)
        ug = (back * slope).astype(bf16)
        ug_s[part, :] = ug
        acc_upb[part, :] += fold(ug.astype(f32))
        acc_down[part, :] += mm_nt(act_s[part, :], dlow_s[...])
        acc_up[part, :] += mm_nt(ug_s[part, :], second_s[...])

    result = mid_s[...] + visible * (mm(wdownt_ref[...], act_s[...]) + vec(5))
    result = result.astype(bf16)
    for b in range(images):
        res_ref[b] = mm_nt(eye[0:slots, :], result[:, b * PITCH : (b + 1) * PITCH]).astype(bf16)

    back = mm(wup_ref[...], ug_s[...])
    acc_vec[2] += fold(back * xh2_s[...])
    acc_vec[3] += fold(back)
    back = back * vec(2)
    m1 = jnp.mean(back, axis=0, keepdims=True)
    m2 = jnp.mean(back * xh2_s[...], axis=0, keepdims=True)
    middle_grad = cot_s[...] + rstd2 * (back - m1 - xh2_s[...] * m2)
    cot_s[...] = middle_grad
    blow = (visible * middle_grad).astype(bf16)
    dlow_s[...] = blow
    acc_vec[4] += fold(blow.astype(f32))
    acc_out[...] += mm_nt(mixture_s[...], dlow_s[...])
    dot_s[...] = mm(wout_ref[...], dlow_s[...]).astype(bf16)

    for b in range(images):
        cols = slice(b * PITCH, (b + 1) * PITCH)
        for h in range(heads):
            lo, hi, at = wins[h]
            rows = slice(h * hw, (h + 1) * hw)
            win_s[h, at : at + hw, :] = dot_s[rows, cols]
            g = mm(vn_s[b, :, lo:hi], win_s[h, 0 : hi - lo, :])
            pa = pa_s[b, h]
            pb = pb_s[b, h]
            pull_a = jnp.sum(g * pa, axis=0, keepdims=True) / cosig[h]
            pull_b = jnp.sum(g * pb, axis=0, keepdims=True) / sig[h]
            acc_gate[h : h + 1, :] += pull_b - pull_a
            acc_place[h] += pb * (g - pull_b)
            ds_s[h, 0:keys, :] = (pa * (g - pull_a)).astype(bf16)
            dqkv_s[rows, cols] = (mm(qkvt_s[d + h * hw : d + (h + 1) * hw, cols], ds_s[h]) * scale).astype(bf16)
            dqkv_s[d + h * hw : d + (h + 1) * hw, cols] = (
                mm_nt(qkvt_s[rows, cols], ds_s[h]) * scale
            ).astype(bf16)
            dqkv_s[2 * d + h * hw : 2 * d + (h + 1) * hw, cols] = mm_nt(dot_s[rows, cols], mix_s[b, h]).astype(bf16)

    acc_qkv[...] += mm_nt(dqkv_s[...], hid_s[...])
    back = mm(wqkv_ref[...], dqkv_s[...])
    xh1 = (x_s[...] - mean1) * rstd1
    acc_vec[0] += fold(back * xh1)
    acc_vec[1] += fold(back)
    back = back * vec(0)
    m1 = jnp.mean(back, axis=0, keepdims=True)
    m2 = jnp.mean(back * xh1, axis=0, keepdims=True)
    token_grad = (cot_s[...] + rstd1 * (back - m1 - xh1 * m2)).astype(bf16)
    for b in range(images):
        tgrad_ref[b] = mm_nt(eye[0:slots, :], token_grad[:, b * PITCH : (b + 1) * PITCH]).astype(bf16)

    @pl.when(step == pl.num_programs(0) - 1)
    def _():
        gqkv_ref[...] = acc_qkv[...].astype(bf16)
        gout_ref[...] = acc_out[...].astype(bf16)
        gup_ref[...] = acc_up[...].astype(bf16)
        gdown_ref[...] = acc_down[...].astype(bf16)
        for k in range(6):
            gvec_ref[k] = acc_vec[k]
        gupb_ref[...] = acc_upb[...]
        j = lax.broadcasted_iota(jnp.int32, (keys, PITCH), 0)
        i = lax.broadcasted_iota(jnp.int32, (keys, PITCH), 1)
        rj, ri = j // GRID, i // GRID
        dc = ((j - rj * GRID) - (i - ri * GRID)).astype(f32)
        dr = (rj - ri).astype(f32)
        far = dc * dc + dr * dr
        for h in range(heads):
            pg = acc_place[h]
            for c, off in enumerate((dc, dr, far)):
                gloc_ref[c, h : h + 1, :] = jnp.sum(pg * off, axis=0, keepdims=True)
            gloc_ref[3, h : h + 1, :] = acc_gate[h : h + 1, :] * (sig[h] * cosig[h])


def run_block(tokens, visible, cotangent, wqkv, wout, wup, wdown, vectors, up_bias, locality, images=2):
    b, slots, d = tokens.shape
    heads = locality.shape[1]
    ff = up_bias.shape[0]
    keys = -(-slots // 16) * 16
    n = images * PITCH
    vis = jnp.pad(visible, ((0, 0), (0, PITCH - slots)))[:, None, :]
    vec = jnp.broadcast_to(vectors[:, :, None], (6, d, 128))
    upb = jnp.broadcast_to(up_bias[:, None], (ff, 128))

    def whole(shape):
        return pl.BlockSpec(shape, lambda g: (0,) * len(shape), pipeline_mode=pl.Buffered(1))

    def per(shape):
        return pl.BlockSpec((images,) + shape, lambda g: (g,) + (0,) * len(shape))

    out_shapes = [
        jax.ShapeDtypeStruct((b, slots, d), bf16),
        jax.ShapeDtypeStruct((b, slots, d), bf16),
        jax.ShapeDtypeStruct((3 * d, d), bf16),
        jax.ShapeDtypeStruct((d, d), bf16),
        jax.ShapeDtypeStruct((ff, d), bf16),
        jax.ShapeDtypeStruct((ff, d), bf16),
        jax.ShapeDtypeStruct((6, d, 128), f32),
        jax.ShapeDtypeStruct((ff, 128), f32),
        jax.ShapeDtypeStruct((4, heads, PITCH), f32),
    ]
    scratch = [
        pltpu.VMEM((PITCH, PITCH), bf16),
        pltpu.VMEM((PITCH, d), bf16),
        pltpu.VMEM((heads, keys, PITCH), f32),
        pltpu.VMEM((3 * d, d), f32),
        pltpu.VMEM((d, d), f32),
        pltpu.VMEM((ff, d), f32),
        pltpu.VMEM((ff, d), f32),
        pltpu.VMEM((6, d, 128), f32),
        pltpu.VMEM((ff, 128), f32),
        pltpu.VMEM((heads, keys, PITCH), f32),
        pltpu.VMEM((-(-heads // 8) * 8, PITCH), f32),
        pltpu.VMEM((d, n), f32),
        pltpu.VMEM((d, n), bf16),
        pltpu.VMEM((3 * d, n), bf16),
        pltpu.VMEM((images, keys, d), bf16),
        pltpu.VMEM((images, keys, d), bf16),
        pltpu.VMEM((heads, PITCH, PITCH), bf16),
        pltpu.VMEM((8, 128), f32),
        pltpu.VMEM((images, heads, keys, PITCH), f32),
        pltpu.VMEM((images, heads, keys, PITCH), f32),
        pltpu.VMEM((images, heads, PITCH, PITCH), bf16),
        pltpu.VMEM((heads, PITCH, PITCH), bf16),
        pltpu.VMEM((d, n), bf16),
        pltpu.VMEM((d, n), f32),
        pltpu.VMEM((d, n), bf16),
        pltpu.VMEM((d, n), f32),
        pltpu.VMEM((d, n), f32),
        pltpu.VMEM((d, n), bf16),
        pltpu.VMEM((ff, n), bf16),
        pltpu.VMEM((ff, n), bf16),
        pltpu.VMEM((d, n), bf16),
        pltpu.VMEM((3 * d, n), bf16),
    ]
    outs = pl.pallas_call(
        partial(block_kernel, images, slots, heads),
        grid=(b // images,),
        out_shape=out_shapes,
        in_specs=[
            pl.BlockSpec(memory_space=pltpu.SMEM),
            per((slots, d)),
            per((slots, d)),
            per((1, PITCH)),
            whole((3 * d, d)),
            whole((d, 3 * d)),
            whole((d, d)),
            whole((d, d)),
            whole((ff, d)),
            whole((d, ff)),
            whole((d, ff)),
            whole((ff, d)),
            whole((6, d, 128)),
            whole((ff, 128)),
        ],
        out_specs=[
            per((slots, d)),
            per((slots, d)),
            whole((3 * d, d)),
            whole((d, d)),
            whole((ff, d)),
            whole((ff, d)),
            whole((6, d, 128)),
            whole((ff, 128)),
            whole((4, heads, PITCH)),
        ],
        scratch_shapes=scratch,
        compiler_params=pltpu.CompilerParams(
            dimension_semantics=("arbitrary",), vmem_limit_bytes=63 * 1024 * 1024
        ),
        cost_estimate=pl.CostEstimate(flops=90_000_000_000, bytes_accessed=30_000_000, transcendentals=0),
    )(
        locality,
        tokens,
        cotangent,
        vis,
        wqkv.T,
        wqkv,
        wout.T,
        wout,
        wup.T,
        wup,
        wdown.T,
        wdown,
        vec,
        upb,
    )
    result, token_grad, gqkv, gout, gup, gdown, gvec, gupb, gloc = outs
    return result, token_grad, gqkv, gout, gup, gdown, gvec.sum(-1), gupb.sum(-1), gloc.sum(-1)


def collect(shards):
    partly = (
        lax.all_gather(shards[0], "fsdp", axis=1, tiled=True),
        lax.all_gather(shards[1], "fsdp", axis=0, tiled=True),
        lax.all_gather(shards[2], "fsdp", axis=0, tiled=True),
        lax.all_gather(shards[3], "fsdp", axis=0, tiled=True),
        lax.all_gather(shards[4], "fsdp", axis=1, tiled=True),
    )
    return (
        lax.all_gather(partly[0], "dp", axis=0, tiled=True),
        lax.all_gather(partly[1], "dp", axis=1, tiled=True),
        lax.all_gather(partly[2], "dp", axis=1, tiled=True),
        lax.all_gather(partly[3], "dp", axis=1, tiled=True),
        lax.all_gather(partly[4], "dp", axis=0, tiled=True),
    )


def spread_back(partials):
    partly = (
        lax.psum_scatter(
            partials[0].astype(jnp.bfloat16), "dp", scatter_dimension=0, tiled=True
        ).astype(jnp.float32),
        lax.psum_scatter(
            partials[1].astype(jnp.bfloat16), "dp", scatter_dimension=1, tiled=True
        ).astype(jnp.float32),
        lax.psum_scatter(
            partials[2].astype(jnp.bfloat16), "dp", scatter_dimension=1, tiled=True
        ).astype(jnp.float32),
        lax.psum_scatter(
            partials[3].astype(jnp.bfloat16), "dp", scatter_dimension=1, tiled=True
        ).astype(jnp.float32),
        lax.psum_scatter(
            partials[4].astype(jnp.bfloat16), "dp", scatter_dimension=0, tiled=True
        ).astype(jnp.float32),
    )
    return (
        lax.psum_scatter(
            partly[0].astype(jnp.bfloat16), "fsdp", scatter_dimension=1, tiled=True
        ).astype(jnp.float32),
        lax.psum_scatter(
            partly[1].astype(jnp.bfloat16), "fsdp", scatter_dimension=0, tiled=True
        ).astype(jnp.float32),
        lax.psum_scatter(
            partly[2].astype(jnp.bfloat16), "fsdp", scatter_dimension=0, tiled=True
        ).astype(jnp.float32),
        lax.psum_scatter(
            partly[3].astype(jnp.bfloat16), "fsdp", scatter_dimension=0, tiled=True
        ).astype(jnp.float32),
        lax.psum_scatter(
            partly[4].astype(jnp.bfloat16), "fsdp", scatter_dimension=1, tiled=True
        ).astype(jnp.float32),
    )


def adamw(parameter, moment_one, moment_two, gradient, rate, decay_rate):
    first_new = beta_one * moment_one + (1.0 - beta_one) * gradient
    second_new = beta_two * moment_two + (1.0 - beta_two) * gradient * gradient
    first_hat = first_new / (1.0 - beta_one**STEP)
    second_hat = second_new / (1.0 - beta_two**STEP)
    new_value = parameter - rate * (
        first_hat / (jnp.sqrt(second_hat) + adam_eps) + decay_rate * parameter
    )
    return (new_value, first_new, second_new)


def body(
    tokens,
    keep_mask,
    cotangent,
    qk_weight,
    qk_first,
    qk_second,
    value_weight,
    value_first,
    value_second,
    out_weight,
    out_first,
    out_second,
    up_weight,
    up_first,
    up_second,
    down_weight,
    down_first,
    down_second,
    vectors,
    vectors_first,
    vectors_second,
    up_bias,
    up_bias_first,
    up_bias_second,
    locality,
    locality_first,
    locality_second,
):
    d = tokens.shape[-1]
    masters = (qk_weight, value_weight, out_weight, up_weight, down_weight)
    gathered = collect(tuple(matrix.astype(jnp.bfloat16) for matrix in masters))
    vectors_all = lax.all_gather(vectors, "fsdp", axis=1, tiled=True)
    up_bias_all = lax.all_gather(up_bias, "fsdp", axis=0, tiled=True)
    qk_full, value_full, out_full, up_full, down_full = gathered
    result, token_grad, gqkv, gout, gup, gdown, vectors_grad, grad_up_bias, locality_grad = run_block(
        tokens,
        keep_mask.astype(f32),
        cotangent,
        jnp.concatenate([qk_full, value_full], axis=1),
        out_full,
        up_full,
        down_full,
        vectors_all,
        up_bias_all,
        locality,
    )
    owned_grads = spread_back((gqkv[: 2 * d].T, gqkv[2 * d :].T, gout, gup.T, gdown))
    local_squares = jnp.float32(0.0)
    for gradient in owned_grads:
        local_squares = local_squares + jnp.sum(gradient * gradient)
    matrix_squares, vectors_sum, up_bias_sum, locality_sum = lax.psum(
        (local_squares, vectors_grad, grad_up_bias, locality_grad), ("dp", "fsdp")
    )
    small_squares = (
        jnp.sum(vectors_sum * vectors_sum)
        + jnp.sum(up_bias_sum * up_bias_sum)
        + jnp.sum(locality_sum * locality_sum)
    )
    grad_norm = jnp.sqrt(matrix_squares + small_squares)
    factor = clip_limit / jnp.maximum(grad_norm, clip_limit)
    share_width = vectors.shape[1]
    up_share = up_bias.shape[0]
    outer_place = lax.axis_index("fsdp")
    vectors_own = lax.dynamic_slice_in_dim(vectors_sum, outer_place * share_width, share_width, 1)
    up_bias_own = lax.dynamic_slice_in_dim(up_bias_sum, outer_place * up_share, up_share, 0)
    outputs = [result, token_grad, grad_norm]
    matrix_states = (
        (qk_first, qk_second),
        (value_first, value_second),
        (out_first, out_second),
        (up_first, up_second),
        (down_first, down_second),
    )
    for position in range(5):
        new_value, first_new, second_new = adamw(
            masters[position],
            matrix_states[position][0],
            matrix_states[position][1],
            owned_grads[position] * factor,
            learn_rate,
            weight_decay,
        )
        outputs.extend([new_value, new_value.astype(jnp.bfloat16), first_new, second_new])
    small_params = (
        (vectors, vectors_first, vectors_second, vectors_own),
        (up_bias, up_bias_first, up_bias_second, up_bias_own),
        (locality, locality_first, locality_second, locality_sum),
    )
    for parameter, moment_one, moment_two, gradient in small_params:
        new_value, first_new, second_new = adamw(
            parameter, moment_one, moment_two, gradient * factor, small_rate, 0.0
        )
        outputs.extend([new_value, first_new, second_new])
    return tuple(outputs)


def solution(mesh):
    placed = (
        P(("dp", "fsdp"), None, None),
        P(("dp", "fsdp"), None),
        P(("dp", "fsdp"), None, None),
        P("dp", "fsdp"),
        P("dp", "fsdp"),
        P("dp", "fsdp"),
        P("fsdp", "dp"),
        P("fsdp", "dp"),
        P("fsdp", "dp"),
        P("fsdp", "dp"),
        P("fsdp", "dp"),
        P("fsdp", "dp"),
        P("fsdp", "dp"),
        P("fsdp", "dp"),
        P("fsdp", "dp"),
        P("dp", "fsdp"),
        P("dp", "fsdp"),
        P("dp", "fsdp"),
        P(None, "fsdp"),
        P(None, "fsdp"),
        P(None, "fsdp"),
        P("fsdp"),
        P("fsdp"),
        P("fsdp"),
        P(),
        P(),
        P(),
    )
    return jax.shard_map(
        body,
        mesh=mesh,
        in_specs=placed,
        out_specs=(
            P(("dp", "fsdp"), None, None),
            P(("dp", "fsdp"), None, None),
            P(),
            P("dp", "fsdp"),
            P("dp", "fsdp"),
            P("dp", "fsdp"),
            P("dp", "fsdp"),
            P("fsdp", "dp"),
            P("fsdp", "dp"),
            P("fsdp", "dp"),
            P("fsdp", "dp"),
            P("fsdp", "dp"),
            P("fsdp", "dp"),
            P("fsdp", "dp"),
            P("fsdp", "dp"),
            P("fsdp", "dp"),
            P("fsdp", "dp"),
            P("fsdp", "dp"),
            P("fsdp", "dp"),
            P("dp", "fsdp"),
            P("dp", "fsdp"),
            P("dp", "fsdp"),
            P("dp", "fsdp"),
            P(None, "fsdp"),
            P(None, "fsdp"),
            P(None, "fsdp"),
            P("fsdp"),
            P("fsdp"),
            P("fsdp"),
            P(),
            P(),
            P(),
        ),
        check_vma=False,
    )
```

```python
from functools import partial

import jax
import jax.numpy as jnp
from jax import lax
from jax.experimental import pallas as pl
from jax.experimental.pallas import tpu as pltpu
from jax.sharding import PartitionSpec as P

GRID = 14
STEP = 5
PITCH = 256

norm_eps = 1e-06
learn_rate = 0.03
small_rate = 0.3
beta_one = 0.5
beta_two = 0.5
adam_eps = 1e-08
weight_decay = 0.05
clip_limit = 1.0

LOG2E = 1.4426950408889634
ERF_P = 0.3275911 * 0.5**0.5
ERF_A = (0.254829592, -0.284496736, 1.421413741, -1.453152027, 1.061405429)
PHI_ZERO = 0.3989422804014327

f32 = jnp.float32
bf16 = jnp.bfloat16


def mm(a, b):
    return lax.dot_general(a, b, (((1,), (0,)), ((), ())), preferred_element_type=f32)


def mm_nt(a, b):
    return lax.dot_general(a, b, (((1,), (1,)), ((), ())), preferred_element_type=f32)


def gelu_parts(u):
    slope = 1.0 + ERF_P * jnp.abs(u)
    rough = pl.reciprocal(slope, approx=True)
    t = rough * (2.0 - slope * rough)
    poly = ERF_A[4] * 0.5
    for term in (ERF_A[3], ERF_A[2], ERF_A[1], ERF_A[0]):
        poly = poly * t + term * 0.5
    bell = jnp.exp2(u * u * (-0.5 * LOG2E))
    tail = poly * t * bell
    cdf = jnp.where(u >= 0, 1.0 - tail, tail)
    return u * cdf, cdf + u * bell * PHI_ZERO


def block_kernel(
    images,
    slots,
    heads,
    locality_ref,
    tok_ref,
    cot_ref,
    vis_ref,
    all_ref,
    small_ref,
    res_ref,
    tgrad_ref,
    part_ref,
    gsmall_ref,
    eye,
    pick,
    pick_a,
    pick_b,
    cat_s,
    chunk_s,
    chunk_sem,
    wqkvt_s,
    wqk_s,
    wv_s,
    wot_s,
    wo_s,
    wupt_s,
    wup_s,
    wdnt_s,
    wdn_s,
    vec_s,
    upb_s,
    pad_in,
    placed,
    acc_qk,
    acc_v,
    acc_out,
    acc_up,
    acc_down,
    acc_vec,
    acc_upb,
    acc_place,
    acc_gate,
    x_s,
    hid_s,
    qkvt_s,
    kn_s,
    vn_s,
    win_s,
    pa_s,
    pb_s,
    mix_s,
    ds_s,
    mixture_s,
    xh2_s,
    second_s,
    mid_s,
    cot_s,
    dlow_s,
    act_s,
    ug_s,
    dot_s,
    dqkv_s,
):
    d = tok_ref.shape[-1]
    ff = upb_s.shape[0]
    dp, fsdp, rows_all, _ = all_ref.shape
    u, w = d // dp, d // fsdp
    fu = ff // dp
    base = up16(2 * fu)
    rest = rows_all - base
    hw = d // heads
    keys = placed.shape[1]
    n = images * PITCH
    scale = hw**-0.5
    step = pl.program_id(0)

    @pl.when(step == 0)
    def _():
        rows = lax.broadcasted_iota(jnp.int32, (PITCH, PITCH), 0)
        cols = lax.broadcasted_iota(jnp.int32, (PITCH, PITCH), 1)
        eye[...] = jnp.where(rows == cols, 1.0, 0.0).astype(bf16)
        pad_in[...] = jnp.zeros_like(pad_in)
        j = lax.broadcasted_iota(jnp.int32, (keys, PITCH), 0)
        i = lax.broadcasted_iota(jnp.int32, (keys, PITCH), 1)
        rj, ri = j // GRID, i // GRID
        dc = ((j - rj * GRID) - (i - ri * GRID)).astype(f32)
        dr = (rj - ri).astype(f32)
        far = dc * dc + dr * dr
        for h in range(heads):
            placed[h] = locality_ref[0, h] * dc + locality_ref[1, h] * dr + locality_ref[2, h] * far

        def one_hot(shape, goal):
            r = lax.broadcasted_iota(jnp.int32, shape, 0)
            c = lax.broadcasted_iota(jnp.int32, shape, 1)
            block, lane = r // 128, r % 128
            return jnp.where((c == goal(block, lane)) & (lane < w), 1.0, 0.0).astype(bf16)

        pick[...] = one_hot(pick.shape, lambda block, lane: block * w + lane)
        pick_a[...] = one_hot(pick_a.shape, lambda block, lane: block * (2 * w) + lane)
        pick_b[...] = one_hot(pick_b.shape, lambda block, lane: block * (2 * w) + w + lane)

        def fetch(k):
            return pltpu.make_async_copy(all_ref.at[k, :, pl.ds(0, base)], chunk_s.at[k % 2], chunk_sem.at[k % 2])

        def fetch_rest(k):
            return pltpu.make_async_copy(
                all_ref.at[k, :, pl.ds(base, rest)], chunk_s.at[k % 2, :, pl.ds(0, rest)], chunk_sem.at[k % 2]
            )

        fetch(0).start()

        def unpack(k, cat):
            fetch(k).wait()

            @pl.when(k + 1 < dp)
            def _():
                fetch(k + 1).start()

            for f in range(fsdp):
                cat_s[0:base, 128 * f : 128 * (f + 1)] = chunk_s[k % 2, f].astype(f32)
            big = pl.ds(pl.multiple_of(fu * k, 8), fu) if fu % 8 == 0 else pl.ds(fu * k, fu)
            acc_up[big, :] = mm(cat_s[0:fu, :].astype(bf16), pick[...])
            acc_down[big, :] = mm(cat_s[fu : 2 * fu, :].astype(bf16), pick[...])
            return 0

        if fu % 8 == 0:
            lax.fori_loop(0, dp, unpack, 0)
        else:
            for k in range(dp):
                unpack(k, 0)
        fetch_rest(0).start()
        for k in range(dp):
            fetch_rest(k).wait()
            if k + 1 < dp:
                fetch_rest(k + 1).start()
            for f in range(fsdp):
                cat_s[0:rest, 128 * f : 128 * (f + 1)] = chunk_s[k % 2, f, 0:rest].astype(f32)

            def wide(at):
                return cat_s[at : at + u, :].astype(bf16)

            acc_v[u * k : u * (k + 1), :] = mm(wide(0), pick[...])
            acc_out[u * k : u * (k + 1), :] = mm(wide(u), pick[...])
            acc_qk[u * k : u * (k + 1), :] = mm(wide(2 * u), pick_a[...]) + mm(wide(3 * u), pick_b[...])

        def turned(ref, out_ref, row=0):
            for lo in range(0, ref.shape[1], PITCH):
                hi = min(lo + PITCH, ref.shape[1])
                out_ref[row + lo : row + hi, :] = mm_nt(eye[0 : hi - lo, 0 : hi - lo], ref[:, lo:hi]).astype(bf16)

        wupt_s[...] = acc_up[...].astype(bf16)
        turned(wupt_s, wup_s)
        wdn_s[...] = acc_down[...].astype(bf16)
        turned(wdn_s, wdnt_s)
        wot_s[...] = acc_out[...].astype(bf16)
        turned(wot_s, wo_s)
        wqk_s[...] = acc_qk[...].astype(bf16)
        turned(wqk_s, wqkvt_s)
        wqkvt_s[2 * d : 3 * d, :] = acc_v[...].astype(bf16)
        turned(wqkvt_s.at[2 * d : 3 * d], wv_s)
        for f in range(fsdp):
            for r in range(6):
                vec_s[r, w * f : w * (f + 1), :] = jnp.broadcast_to(small_ref[f, r : r + 1, :], (128, 128)).T[0:w]
            for r in range(ff // d):
                upb_s[(f * (ff // d) + r) * w : (f * (ff // d) + r + 1) * w, :] = jnp.broadcast_to(
                    small_ref[f, 6 + r : 7 + r, :], (128, 128)
                ).T[0:w]
        for ref in (acc_qk, acc_v, acc_out, acc_up, acc_down, acc_vec, acc_upb, acc_place, acc_gate, win_s, mix_s, ds_s, qkvt_s):
            ref[...] = jnp.zeros_like(ref)

    def lanes(b):
        return pl.ds(b * PITCH, PITCH)

    def vec(k):
        return jnp.concatenate([vec_s[k]] * (n // 128), axis=1)

    def fold(v):
        total = v[:, 0:128]
        for k in range(1, n // 128):
            total = total + v[:, 128 * k : 128 * (k + 1)]
        return total

    def turn_in(ref, b):
        pad_in[0:slots, 0:d] = ref[b]
        parts = []
        for lo in range(0, d, PITCH):
            hi = min(lo + PITCH, d)
            parts.append(mm_nt(eye[0 : hi - lo, 0 : hi - lo], pad_in[:, lo:hi]))
        return jnp.concatenate(parts, axis=0)

    visible = jnp.concatenate([vis_ref[b, 0:1, :] for b in range(images)], axis=1)

    def enter(b, _):
        cols = pl.ds(pl.multiple_of(b * PITCH, PITCH), PITCH)
        x_s[:, cols] = turn_in(tok_ref, b)
        cot_s[:, cols] = turn_in(cot_ref, b)
        return 0

    lax.fori_loop(0, images, enter, 0)
    dlow_s[...] = (cot_s[...] * visible).astype(bf16)
    acc_vec[5] += fold(cot_s[...] * visible)

    x = x_s[...]
    mean1 = jnp.mean(x, axis=0, keepdims=True)
    center = x - mean1
    rstd1 = lax.rsqrt(jnp.mean(center * center, axis=0, keepdims=True) + norm_eps)
    hid_s[...] = (center * rstd1 * vec(0) + vec(1)).astype(bf16)
    qkvt_s[...] = mm(wqkvt_s[...], hid_s[...]).astype(bf16)

    sig, cosig = [], []
    for h in range(heads):
        gate = jnp.full((1, PITCH), locality_ref[3, h], f32)
        s = 1.0 / (1.0 + jnp.exp(-gate))
        sig.append(s)
        cosig.append(1.0 - s)

    wins = []
    for h in range(heads):
        lo = (h * hw) // 128 * 128
        wins.append((lo, min(lo + PITCH, d), h * hw - lo))

    def forward(b, _):
        cols = pl.ds(pl.multiple_of(b * PITCH, PITCH), PITCH)
        kn_s[b] = mm_nt(eye[0:keys, :], qkvt_s[d : 2 * d, cols]).astype(bf16)
        vn_s[b] = mm_nt(eye[0:keys, :], qkvt_s[2 * d : 3 * d, cols]).astype(bf16)
        key_vis = mm_nt(eye[0:keys, :], jnp.broadcast_to(vis_ref[b, 0:1, :], (PITCH, PITCH)).astype(bf16))
        bias = jnp.where(key_vis > 0.5, 0.0, -1e30)
        for h in range(heads):
            lo, hi, at = wins[h]
            win_s[h, at : at + hw, :] = qkvt_s[h * hw : (h + 1) * hw, cols]
            scores = mm(kn_s[b, :, lo:hi], win_s[h, 0 : hi - lo, :]) * (scale * LOG2E) + bias
            p = jnp.exp2(scores - jnp.max(scores, axis=0, keepdims=True))
            pa = p * (cosig[h] / jnp.sum(p, axis=0, keepdims=True))
            z = placed[h] + bias
            e = jnp.exp(z - jnp.max(z, axis=0, keepdims=True))
            pb = e * (sig[h] / jnp.sum(e, axis=0, keepdims=True))
            pa_s[b, h] = pa.astype(bf16)
            pb_s[b, h] = pb.astype(bf16)
            mix_s[h, 0:keys, :] = (pa + pb).astype(bf16)
            mixture_s[h * hw : (h + 1) * hw, cols] = mm(
                qkvt_s[2 * d + h * hw : 2 * d + (h + 1) * hw, cols], mix_s[h]
            ).astype(bf16)
        return 0

    lax.fori_loop(0, images, forward, 0)

    branch = mm(wot_s[...], mixture_s[...]) + vec(4)
    middle = x_s[...] + visible * branch
    mid_s[...] = middle
    mean2 = jnp.mean(middle, axis=0, keepdims=True)
    center = middle - mean2
    rstd2 = lax.rsqrt(jnp.mean(center * center, axis=0, keepdims=True) + norm_eps)
    xh2_s[...] = center * rstd2
    second_s[...] = (xh2_s[...] * vec(2) + vec(3)).astype(bf16)

    chunk = d
    def feed(c, _):
        part = pl.ds(pl.multiple_of(c * chunk, chunk), chunk)
        up = mm(wupt_s[part, :], second_s[...]) + jnp.concatenate([upb_s[part, :]] * (n // 128), axis=1)
        back = mm(wdn_s[part, :], dlow_s[...])
        act, slope = gelu_parts(up)
        act_s[part, :] = act.astype(bf16)
        ug = (back * slope).astype(bf16)
        ug_s[part, :] = ug
        acc_upb[part, :] += fold(ug.astype(f32))
        acc_down[part, :] += mm_nt(act_s[part, :], dlow_s[...])
        acc_up[part, :] += mm_nt(ug_s[part, :], second_s[...])
        return 0

    lax.fori_loop(0, ff // chunk, feed, 0)

    result = mid_s[...] + visible * (mm(wdnt_s[...], act_s[...]) + vec(5))
    result = result.astype(bf16)
    for b in range(images):
        res_ref[b] = mm_nt(eye[0:slots, :], result[:, b * PITCH : (b + 1) * PITCH]).astype(bf16)

    back = mm(wup_s[...], ug_s[...])
    acc_vec[2] += fold(back * xh2_s[...])
    acc_vec[3] += fold(back)
    back = back * vec(2)
    m1 = jnp.mean(back, axis=0, keepdims=True)
    m2 = jnp.mean(back * xh2_s[...], axis=0, keepdims=True)
    middle_grad = cot_s[...] + rstd2 * (back - m1 - xh2_s[...] * m2)
    cot_s[...] = middle_grad
    blow = (visible * middle_grad).astype(bf16)
    dlow_s[...] = blow
    acc_vec[4] += fold(blow.astype(f32))
    acc_out[...] += mm_nt(dlow_s[...], mixture_s[...])
    dot_s[...] = mm(wo_s[...], dlow_s[...]).astype(bf16)

    def backward(b, _):
        cols = pl.ds(pl.multiple_of(b * PITCH, PITCH), PITCH)
        for h in range(heads):
            lo, hi, at = wins[h]
            rows = slice(h * hw, (h + 1) * hw)
            win_s[h, at : at + hw, :] = dot_s[rows, cols]
            g = mm(vn_s[b, :, lo:hi], win_s[h, 0 : hi - lo, :])
            pa = pa_s[b, h].astype(f32)
            pb = pb_s[b, h].astype(f32)
            mix_s[h, 0:keys, :] = (pa + pb).astype(bf16)
            pull_a = jnp.sum(g * pa, axis=0, keepdims=True) / cosig[h]
            pull_b = jnp.sum(g * pb, axis=0, keepdims=True) / sig[h]
            acc_gate[h : h + 1, :] += pull_b - pull_a
            acc_place[h] += pb * (g - pull_b)
            ds_s[h, 0:keys, :] = (pa * (g - pull_a)).astype(bf16)
            dqkv_s[rows, cols] = (mm(qkvt_s[d + h * hw : d + (h + 1) * hw, cols], ds_s[h]) * scale).astype(bf16)
            dqkv_s[d + h * hw : d + (h + 1) * hw, cols] = (
                mm_nt(qkvt_s[rows, cols], ds_s[h]) * scale
            ).astype(bf16)
            dqkv_s[2 * d + h * hw : 2 * d + (h + 1) * hw, cols] = mm_nt(dot_s[rows, cols], mix_s[h]).astype(bf16)
        return 0

    lax.fori_loop(0, images, backward, 0)

    acc_qk[...] += mm_nt(hid_s[...], dqkv_s[0 : 2 * d, :])
    acc_v[...] += mm_nt(dqkv_s[2 * d : 3 * d, :], hid_s[...])
    back = mm(wqk_s[...], dqkv_s[0 : 2 * d, :]) + mm(wv_s[...], dqkv_s[2 * d : 3 * d, :])
    xh1 = (x_s[...] - mean1) * rstd1
    acc_vec[0] += fold(back * xh1)
    acc_vec[1] += fold(back)
    back = back * vec(0)
    m1 = jnp.mean(back, axis=0, keepdims=True)
    m2 = jnp.mean(back * xh1, axis=0, keepdims=True)
    token_grad = (cot_s[...] + rstd1 * (back - m1 - xh1 * m2)).astype(bf16)
    for b in range(images):
        tgrad_ref[b] = mm_nt(eye[0:slots, :], token_grad[:, b * PITCH : (b + 1) * PITCH]).astype(bf16)

    @pl.when(step == pl.num_programs(0) - 1)
    def _():
        def put_rest(k):
            return pltpu.make_async_copy(
                chunk_s.at[k % 2, :, pl.ds(0, rest)], part_ref.at[k, :, pl.ds(base, rest)], chunk_sem.at[k % 2]
            )

        cat_s[...] = jnp.zeros_like(cat_s)
        for k in range(dp):
            cat_s[0:u, :] = mm_nt(acc_v[u * k : u * (k + 1), :].astype(bf16), pick[...])
            cat_s[u : 2 * u, :] = mm_nt(acc_out[u * k : u * (k + 1), :].astype(bf16), pick[...])
            piece = acc_qk[u * k : u * (k + 1), :].astype(bf16)
            cat_s[2 * u : 3 * u, :] = mm_nt(piece, pick_a[...])
            cat_s[3 * u : 4 * u, :] = mm_nt(piece, pick_b[...])
            if k >= 2:
                put_rest(k - 2).wait()
            for f in range(fsdp):
                chunk_s[k % 2, f, 0:rest] = cat_s[0:rest, 128 * f : 128 * (f + 1)].astype(bf16)
            put_rest(k).start()
        for k in range(max(dp - 2, 0), dp):
            put_rest(k).wait()
        if base > 2 * fu:
            cat_s[2 * fu : base, :] = jnp.zeros((base - 2 * fu, fsdp * 128), f32)

        def put(k):
            return pltpu.make_async_copy(chunk_s.at[k % 2], part_ref.at[k, :, pl.ds(0, base)], chunk_sem.at[k % 2])

        def pack(k, _):
            big = pl.ds(pl.multiple_of(fu * k, 8), fu) if fu % 8 == 0 else pl.ds(fu * k, fu)
            cat_s[0:fu, :] = mm_nt(acc_up[big, :].astype(bf16), pick[...])
            cat_s[fu : 2 * fu, :] = mm_nt(acc_down[big, :].astype(bf16), pick[...])

            @pl.when(k >= 2)
            def _():
                put(k - 2).wait()

            for f in range(fsdp):
                chunk_s[k % 2, f] = cat_s[0:base, 128 * f : 128 * (f + 1)].astype(bf16)
            put(k).start()
            return 0

        if fu % 8 == 0:
            lax.fori_loop(0, dp, pack, 0)
        else:
            for k in range(dp):
                pack(k, 0)
        for k in range(max(dp - 2, 0), dp):
            put(k).wait()

        def lane_sums(v):
            ones = jnp.ones((8, v.shape[1]), f32)
            return lax.dot_general(
                ones, v, (((1,), (1,)), ((), ())), preferred_element_type=f32, precision=lax.Precision.HIGHEST
            )[0:1]

        gsmall_ref[...] = jnp.zeros_like(gsmall_ref)
        for f in range(fsdp):
            for r in range(6):
                gsmall_ref[f, r : r + 1, 0:w] = lane_sums(acc_vec[r, w * f : w * (f + 1), :])
            for r in range(ff // d):
                lo = (f * (ff // d) + r) * w
                gsmall_ref[f, 6 + r : 7 + r, 0:w] = lane_sums(acc_upb[lo : lo + w, :])
        j = lax.broadcasted_iota(jnp.int32, (keys, PITCH), 0)
        i = lax.broadcasted_iota(jnp.int32, (keys, PITCH), 1)
        rj, ri = j // GRID, i // GRID
        dc = ((j - rj * GRID) - (i - ri * GRID)).astype(f32)
        dr = (rj - ri).astype(f32)
        far = dc * dc + dr * dr
        at = 6 + ff // d
        wide_rows = [[], [], []]
        for h in range(heads):
            pg = acc_place[h]
            for c, off in enumerate((dc, dr, far)):
                wide_rows[c].append(jnp.sum(pg * off, axis=0, keepdims=True))
        for h in range(heads):
            acc_gate[h : h + 1, :] = acc_gate[h : h + 1, :] * (sig[h] * cosig[h])
        gsmall_ref[0, at + 3 : at + 4, 0 : acc_gate.shape[0]] = lane_sums(acc_gate[...])
        for c in range(3):
            for h in range(heads):
                acc_gate[h : h + 1, :] = wide_rows[c][h]
            gsmall_ref[0, at + c : at + c + 1, 0 : acc_gate.shape[0]] = lane_sums(acc_gate[...])


def run_block(tokens, visible, cotangent, everything, small, locality, ff, images=2):
    b, slots, d = tokens.shape
    heads = locality.shape[1]
    keys = -(-slots // 16) * 16
    n = images * PITCH
    dp, fsdp, rows, _ = everything.shape
    base = up16(2 * ff // dp)
    vis = jnp.pad(visible, ((0, 0), (0, PITCH - slots)))[:, None, :]

    def whole(shape):
        return pl.BlockSpec(shape, lambda g: (0,) * len(shape), pipeline_mode=pl.Buffered(1))

    def per(shape):
        return pl.BlockSpec((images,) + shape, lambda g: (g,) + (0,) * len(shape))

    out_shapes = [
        jax.ShapeDtypeStruct((b, slots, d), bf16),
        jax.ShapeDtypeStruct((b, slots, d), bf16),
        jax.ShapeDtypeStruct((dp, fsdp, rows, 128), bf16),
        jax.ShapeDtypeStruct((fsdp, 16, 128), f32),
    ]
    scratch = [
        ((PITCH, PITCH), bf16),
        ((fsdp * 128, d), bf16),
        ((fsdp * 128, 2 * d), bf16),
        ((fsdp * 128, 2 * d), bf16),
        ((base, fsdp * 128), f32),
        ((2, fsdp, base, 128), bf16),
        None,
        ((3 * d, d), bf16),
        ((d, 2 * d), bf16),
        ((d, d), bf16),
        ((d, d), bf16),
        ((d, d), bf16),
        ((ff, d), bf16),
        ((d, ff), bf16),
        ((d, ff), bf16),
        ((ff, d), bf16),
        ((6, d, 128), f32),
        ((ff, 128), f32),
        ((PITCH, d), bf16),
        ((heads, keys, PITCH), f32),
        ((d, 2 * d), f32),
        ((d, d), f32),
        ((d, d), f32),
        ((ff, d), f32),
        ((ff, d), f32),
        ((6, d, 128), f32),
        ((ff, 128), f32),
        ((heads, keys, PITCH), f32),
        ((-(-heads // 8) * 8, PITCH), f32),
        ((d, n), f32),
        ((d, n), bf16),
        ((3 * d, n), bf16),
        ((images, keys, d), bf16),
        ((images, keys, d), bf16),
        ((heads, PITCH, PITCH), bf16),
        ((images, heads, keys, PITCH), bf16),
        ((images, heads, keys, PITCH), bf16),
        ((heads, PITCH, PITCH), bf16),
        ((heads, PITCH, PITCH), bf16),
        ((d, n), bf16),
        ((d, n), f32),
        ((d, n), bf16),
        ((d, n), f32),
        ((d, n), f32),
        ((d, n), bf16),
        ((ff, n), bf16),
        ((ff, n), bf16),
        ((d, n), bf16),
        ((3 * d, n), bf16),
    ]
    scratch = [pltpu.SemaphoreType.DMA((3,)) if entry is None else pltpu.VMEM(*entry) for entry in scratch]
    return pl.pallas_call(
        partial(block_kernel, images, slots, heads),
        grid=(b // images,),
        out_shape=out_shapes,
        in_specs=[
            pl.BlockSpec(memory_space=pltpu.SMEM),
            per((slots, d)),
            per((slots, d)),
            per((1, PITCH)),
            pl.BlockSpec(memory_space=pl.ANY),
            whole((fsdp, 16, 128)),
        ],
        out_specs=[
            per((slots, d)),
            per((slots, d)),
            pl.BlockSpec(memory_space=pl.ANY),
            whole((fsdp, 16, 128)),
        ],
        scratch_shapes=scratch,
        compiler_params=pltpu.CompilerParams(
            dimension_semantics=("arbitrary",), vmem_limit_bytes=63 * 1024 * 1024
        ),
        cost_estimate=pl.CostEstimate(flops=90_000_000_000, bytes_accessed=30_000_000, transcendentals=0),
    )(locality, tokens, cotangent, vis, everything, small)


MESH = pl.DeviceIdType.MESH


def up16(v):
    return -(-v // 16) * 16


class Place:
    def __init__(self, dp, fsdp):
        self.cores = 2 if dp % 2 == 0 else 1
        self.zs = dp // self.cores
        self.ys = max(v for v in range(1, fsdp + 1) if fsdp % v == 0 and v * v <= fsdp)
        self.xs = fsdp // self.ys
        self.fs = fsdp
        at_dp, at_f = lax.axis_index("dp"), lax.axis_index("fsdp")
        self.z, self.c = at_dp // self.cores, at_dp % self.cores
        self.y, self.x = at_f // self.xs, at_f % self.xs

    def to(self, dz=0, dc=0, dy=0, dx=0):
        z = lax.rem(self.z + dz, self.zs)
        c = lax.rem(self.c + dc, self.cores)
        y = lax.rem(self.y + dy, self.ys)
        x = lax.rem(self.x + dx, self.xs)
        return (z * self.cores + c, y * self.xs + x)


def greet(peers):
    barrier = pltpu.get_barrier_semaphore()
    for peer in peers:
        pl.semaphore_signal(barrier, inc=1, device_id=peer, device_id_type=MESH)
    pl.semaphore_wait(barrier, len(peers))


def gather_kernel(dp, fsdp, rows, qk_ref, vt_ref, ot_ref, upt_ref, dn_ref, vec_ref, upb_ref, all_ref, small_ref, wide, block, part, send, recv, small_send, small_recv, local):
    here = Place(dp, fsdp)
    zs, ys, xs, cores = here.zs, here.ys, here.xs, here.cores
    u, w = vt_ref.shape
    half = rows // 32 * 16
    segs = (pl.ds(0, half), pl.ds(half, rows - half))
    me = here.to()

    peers = [here.to(dz=k) for k in range(1, zs)] + [here.to(dc=k) for k in range(1, cores)]
    peers += [here.to(dy=a, dx=b) for a in range(ys) for b in range(xs) if a or b]

    wide[...] = jnp.zeros_like(wide)
    at = 0
    for ref in (upt_ref, dn_ref, vt_ref, ot_ref):
        wide[at : at + ref.shape[0], 0:w] = ref[...]
        at += ref.shape[0]
        if ref is dn_ref:
            at = up16(at)
    for k in range(qk_ref.shape[1] // w):
        wide[at : at + u, 0:w] = qk_ref[:, k * w : (k + 1) * w]
        at += u
    block[...] = wide[...].astype(bf16)
    part[...] = jnp.zeros_like(part)
    part[0:6, 0:w] = vec_ref[...]
    part[6 : 6 + upb_ref.shape[0], 0:w] = upb_ref[...]

    greet(peers)
    count = [0]
    sent = []

    def push(owner, seg, target, own=False):
        slot = all_ref.at[owner[0], owner[1], segs[seg]]
        flat = owner[0] * here.fs + owner[1]
        copy = pltpu.make_async_remote_copy(
            src_ref=block.at[segs[seg]] if own else slot,
            dst_ref=slot,
            send_sem=send.at[count[0]],
            recv_sem=recv.at[flat, seg],
            device_id=target,
            device_id_type=MESH,
        )
        count[0] += 1
        copy.start()
        sent.append(copy)

    def arrive(owner, seg):
        slot = all_ref.at[owner[0], owner[1], segs[seg]]
        flat = owner[0] * here.fs + owner[1]
        pltpu.make_async_remote_copy(
            src_ref=slot, dst_ref=slot, send_sem=send.at[0], recv_sem=recv.at[flat, seg], device_id=me, device_id_type=MESH
        ).wait_recv()

    own_copy = pltpu.make_async_copy(block, all_ref.at[me[0], me[1]], local.at[0])
    own_copy.start()
    small_copy = pltpu.make_async_copy(part, small_ref.at[me[1]], local.at[1])
    small_copy.start()
    for k in range(1, zs):
        for seg in (0, 1):
            push(me, seg, here.to(dz=k), own=True)
    smalls = []
    for a in range(ys):
        for b in range(xs):
            if a or b:
                n = len(smalls)
                copy = pltpu.make_async_remote_copy(
                    src_ref=part,
                    dst_ref=small_ref.at[me[1]],
                    send_sem=small_send.at[n],
                    recv_sem=small_recv.at[me[1]],
                    device_id=here.to(dy=a, dx=b),
                    device_id_type=MESH,
                )
                copy.start()
                smalls.append(copy)

    def spread(owner, own=False):
        for seg in (0, 1):
            for k in range(1, ys):
                push(owner, seg, here.to(dy=k), own)
            for k in range(1, xs):
                push(owner, seg, here.to(dx=k), own)
        for seg in (0, 1):
            for k in range(1, cores):
                push(owner, seg, here.to(dc=k), own)

    def relay(k):
        for a in range(1, ys):
            owner = here.to(dz=k, dy=a)
            arrive(owner, 0)
            for b in range(1, xs):
                push(owner, 0, here.to(dx=b))
        for b in range(1, xs):
            owner = here.to(dz=k, dx=b)
            arrive(owner, 1)
            for a in range(1, ys):
                push(owner, 1, here.to(dy=a))
        for a in range(1, ys):
            owner = here.to(dz=k, dy=a)
            arrive(owner, 1)
            for seg in (0, 1):
                for c in range(1, cores):
                    push(owner, seg, here.to(dc=c))
        for b in range(1, xs):
            owner = here.to(dz=k, dx=b)
            arrive(owner, 0)
            for seg in (0, 1):
                for c in range(1, cores):
                    push(owner, seg, here.to(dc=c))

    order = [0] + sorted(range(1, zs), key=lambda k: min(k, zs - k))
    spread(me, own=True)
    for n, k in enumerate(order[1:]):
        owner = here.to(dz=k)
        for seg in (0, 1):
            arrive(owner, seg)
        spread(owner)
        relay(order[n])
    relay(order[-1])
    for k in order:
        for a in range(1, ys):
            for b in range(1, xs):
                owner = here.to(dz=k, dy=a, dx=b)
                for seg in (0, 1):
                    arrive(owner, seg)
                    for c in range(1, cores):
                        push(owner, seg, here.to(dc=c))
    for c in range(1, cores):
        for k in order:
            for a in range(ys):
                for b in range(xs):
                    for seg in (0, 1):
                        arrive(here.to(dz=k, dy=a, dx=b, dc=c), seg)
    for a in range(ys):
        for b in range(xs):
            if a or b:
                peer = here.to(dy=a, dx=b)
                pltpu.make_async_remote_copy(
                    src_ref=part,
                    dst_ref=small_ref.at[peer[1]],
                    send_sem=small_send.at[0],
                    recv_sem=small_recv.at[peer[1]],
                    device_id=me,
                    device_id_type=MESH,
                ).wait_recv()
    for copy in sent + smalls:
        copy.wait_send()
    own_copy.wait()
    small_copy.wait()


def gather_sends(dp, fsdp):
    here = Place.__new__(Place)
    cores = 2 if dp % 2 == 0 else 1
    zs = dp // cores
    ys = max(v for v in range(1, fsdp + 1) if fsdp % v == 0 and v * v <= fsdp)
    xs = fsdp // ys
    n = 2 * (zs - 1) + zs * 2 * (ys - 1 + xs - 1) + 2 * zs * (ys - 1) * (xs - 1)
    return n + zs * ys * xs * 2 * (cores - 1)


def gather_all(dp, fsdp, rows, qk, vt, ot, upt, dn, vectors, up_bias):
    return pl.pallas_call(
        partial(gather_kernel, dp, fsdp, rows),
        out_shape=[
            jax.ShapeDtypeStruct((dp, fsdp, rows, 128), bf16),
            jax.ShapeDtypeStruct((fsdp, 16, 128), f32),
        ],
        in_specs=[pl.BlockSpec(memory_space=pltpu.VMEM)] * 7,
        out_specs=[pl.BlockSpec(memory_space=pl.ANY)] * 2,
        scratch_shapes=[
            pltpu.VMEM((rows, 128), f32),
            pltpu.VMEM((rows, 128), bf16),
            pltpu.VMEM((16, 128), f32),
            pltpu.SemaphoreType.DMA((gather_sends(dp, fsdp),)),
            pltpu.SemaphoreType.DMA((dp * fsdp, 2)),
            pltpu.SemaphoreType.DMA((fsdp,)),
            pltpu.SemaphoreType.DMA((fsdp,)),
            pltpu.SemaphoreType.DMA((2,)),
        ],
        compiler_params=pltpu.CompilerParams(collective_id=0, has_side_effects=True, vmem_limit_bytes=32 * 1024 * 1024),
    )(qk, vt, ot, upt, dn, vectors, up_bias.reshape(-1, vt.shape[1]))


def reduce_kernel(dp, fsdp, rows, part_ref, small_in, grad_ref, small_ref, norm_ref, mine, other, got_x, got_y, got_x2, got_y2, got_z, small_buf, norm_buf, load, send, recv, sm_send, sm_recv, nm_send, nm_recv):
    here = Place(dp, fsdp)
    zs, ys, xs, cores = here.zs, here.ys, here.xs, here.cores
    half = rows // 32 * 16
    segs = (pl.ds(0, half), pl.ds(half, rows - half))
    peers = [here.to(dz=k) for k in range(1, zs)] + [here.to(dc=k) for k in range(1, cores)]
    peers += [here.to(dy=a, dx=b) for a in range(ys) for b in range(xs) if a or b]
    peers += [here.to(dz=k, dc=c) for k in range(1, zs) for c in range(1, cores)]
    order = sorted(range(1, zs), key=lambda k: min(k, zs - k)) + [0]

    loads = []
    for n, k in enumerate(order):
        at = here.to(dz=k)
        copy = pltpu.make_async_copy(part_ref.at[at[0]], mine.at[n], load.at[n])
        copy.start()
        loads.append(copy)
    small_ref[...] = small_in[...]
    greet(peers)
    count = [0]
    sent = []

    def push(src, dst, target):
        n = count[0]
        count[0] += 1
        copy = pltpu.make_async_remote_copy(
            src_ref=src, dst_ref=dst, send_sem=send.at[n], recv_sem=recv.at[n], device_id=target, device_id_type=MESH
        )
        copy.start()
        sent.append(copy)
        return copy

    slots = [0]

    def small_round(coordinate, size, targets):
        base = slots[0]
        slots[0] += size
        small_buf[base + coordinate] = small_ref[...]
        copies = []
        for target in targets:
            copy = pltpu.make_async_remote_copy(
                src_ref=small_ref,
                dst_ref=small_buf.at[base + coordinate],
                send_sem=sm_send.at[base + len(copies)],
                recv_sem=sm_recv.at[base + coordinate],
                device_id=target,
                device_id_type=MESH,
            )
            copy.start()
            copies.append(copy)
        return base, coordinate, size, copies

    def small_add(state):
        base, coordinate, size, copies = state
        for copy in copies:
            copy.wait_send()
        for k in range(1, size):
            at = base + lax.rem(coordinate + k, size)
            pltpu.make_async_remote_copy(
                src_ref=small_ref,
                dst_ref=small_buf.at[at],
                send_sem=sm_send.at[base],
                recv_sem=sm_recv.at[at],
                device_id=here.to(),
                device_id_type=MESH,
            ).wait_recv()
        total = small_buf[base]
        for k in range(1, size):
            total = total + small_buf[base + k]
        small_ref[...] = total

    pair = []
    for n, k in enumerate(order):
        at = here.to(dz=k, dc=1)
        if cores > 1:
            pair.append(push(part_ref.at[at[0]], other.at[n], here.to(dc=1)))
    pending = small_round(here.c, cores, [here.to(dc=k) for k in range(1, cores)])

    def f_at(dy, dx):
        return here.to(dy=dy, dx=dx)[1]

    def add(n, f, seg, got):
        mine[n, f, segs[seg]] = (mine[n, f, segs[seg]].astype(f32) + got.astype(f32)).astype(bf16)

    first_a, first_b = {}, {}
    for n, k in enumerate(order):
        loads[n].wait()
        if cores > 1:
            pair[n].wait_recv()

            def body(f, _, n=n):
                mine[n, f] = (mine[n, f].astype(f32) + other[n, f].astype(f32)).astype(bf16)
                return 0

            lax.fori_loop(0, fsdp, body, 0)
        for b in range(1, xs):
            for a in range(ys):
                first_a[n, a, b] = push(mine.at[n, f_at(a, b), segs[0]], got_x.at[n, a, b - 1], here.to(dx=b))
        for a in range(1, ys):
            for b in range(xs):
                first_b[n, a, b] = push(mine.at[n, f_at(a, b), segs[1]], got_y.at[n, b, a - 1], here.to(dy=a))
        if n == 0:
            small_add(pending)
            pending = small_round(here.x, xs, [here.to(dx=b) for b in range(1, xs)])
    second_a, second_b = {}, {}
    for n, k in enumerate(order):
        for a in list(range(1, ys)) + [0]:
            for b in range(1, xs):
                first_a[n, a, b].wait_recv()
                add(n, f_at(a, 0), 0, got_x[n, a, b - 1])
            if a:
                second_a[n, a] = push(mine.at[n, f_at(a, 0), segs[0]], got_y2.at[n, a - 1], here.to(dy=a))
        for b in list(range(1, xs)) + [0]:
            for a in range(1, ys):
                first_b[n, a, b].wait_recv()
                add(n, f_at(0, b), 1, got_y[n, b, a - 1])
            if b:
                second_b[n, b] = push(mine.at[n, f_at(0, b), segs[1]], got_x2.at[n, b - 1], here.to(dx=b))
        if n == 0:
            small_add(pending)
            pending = small_round(here.y, ys, [here.to(dy=a) for a in range(1, ys)])
    third = {}
    for n, k in enumerate(order):
        for a in range(1, ys):
            second_a[n, a].wait_recv()
            add(n, f_at(0, 0), 0, got_y2[n, a - 1])
        for b in range(1, xs):
            second_b[n, b].wait_recv()
            add(n, f_at(0, 0), 1, got_x2[n, b - 1])
        if k:
            for seg in (0, 1):
                third[n, seg] = push(mine.at[n, f_at(0, 0), segs[seg]], got_z.at[n, segs[seg]], here.to(dz=k))
        if n == 0:
            small_add(pending)
            pending = small_round(here.z, zs, [here.to(dz=q) for q in range(1, zs)])
    small_add(pending)
    total = mine[zs - 1, f_at(0, 0)].astype(f32)
    for n, k in enumerate(order):
        if k:
            for seg in (0, 1):
                third[n, seg].wait_recv()
            total = total + got_z[n].astype(f32)
    grad_ref[...] = total
    squares = jnp.sum((total * total).reshape(rows // 8, 8, 128), axis=0)
    norm_ref[...] = squares
    def norm_round(base, coordinate, size, targets):
        norm_buf[base + coordinate] = norm_ref[...]
        copies = []
        for target in targets:
            copy = pltpu.make_async_remote_copy(
                src_ref=norm_ref,
                dst_ref=norm_buf.at[base + coordinate],
                send_sem=nm_send.at[base + len(copies)],
                recv_sem=nm_recv.at[base + coordinate],
                device_id=target,
                device_id_type=MESH,
            )
            copy.start()
            copies.append(copy)
        for copy in copies:
            copy.wait_send()
        for k in range(1, size):
            at = base + lax.rem(coordinate + k, size)
            pltpu.make_async_remote_copy(
                src_ref=norm_ref,
                dst_ref=norm_buf.at[at],
                send_sem=nm_send.at[base],
                recv_sem=nm_recv.at[at],
                device_id=here.to(),
                device_id_type=MESH,
            ).wait_recv()
        got = norm_buf[base]
        for k in range(1, size):
            got = got + norm_buf[base + k]
        norm_ref[...] = got

    norm_round(0, here.to()[1], fsdp, [here.to(dy=a, dx=b) for a in range(ys) for b in range(xs) if a or b])
    norm_round(fsdp, here.to()[0], dp, [here.to(dz=k, dc=c) for k in range(zs) for c in range(cores) if k or c])
    for copy in sent:
        copy.wait_send()


def reduce_all(dp, fsdp, rows, parts, small):
    cores = 2 if dp % 2 == 0 else 1
    zs = dp // cores
    ys = max(v for v in range(1, fsdp + 1) if fsdp % v == 0 and v * v <= fsdp)
    xs = fsdp // ys
    half = rows // 32 * 16
    rest = rows - half
    sends = zs * (cores - 1) + zs * (xs - 1) * ys + zs * (ys - 1) * xs + zs * (ys - 1) + zs * (xs - 1) + 2 * (zs - 1)
    rounds = cores + xs + ys + zs
    norms = fsdp + dp
    return pl.pallas_call(
        partial(reduce_kernel, dp, fsdp, rows),
        out_shape=[
            jax.ShapeDtypeStruct((rows, 128), f32),
            jax.ShapeDtypeStruct(small.shape, f32),
            jax.ShapeDtypeStruct((8, 128), f32),
        ],
        in_specs=[pl.BlockSpec(memory_space=pl.ANY), pl.BlockSpec(memory_space=pltpu.VMEM)],
        out_specs=[pl.BlockSpec(memory_space=pltpu.VMEM)] * 3,
        scratch_shapes=[
            pltpu.VMEM((zs, fsdp, rows, 128), bf16),
            pltpu.VMEM((zs, fsdp, rows, 128), bf16),
            pltpu.VMEM((zs, ys, max(xs - 1, 1), half, 128), bf16),
            pltpu.VMEM((zs, xs, max(ys - 1, 1), rest, 128), bf16),
            pltpu.VMEM((zs, max(xs - 1, 1), rest, 128), bf16),
            pltpu.VMEM((zs, max(ys - 1, 1), half, 128), bf16),
            pltpu.VMEM((zs, rows, 128), bf16),
            pltpu.VMEM((rounds,) + small.shape, f32),
            pltpu.VMEM((norms, 8, 128), f32),
            pltpu.SemaphoreType.DMA((zs,)),
            pltpu.SemaphoreType.DMA((sends,)),
            pltpu.SemaphoreType.DMA((sends,)),
            pltpu.SemaphoreType.DMA((rounds,)),
            pltpu.SemaphoreType.DMA((rounds,)),
            pltpu.SemaphoreType.DMA((norms,)),
            pltpu.SemaphoreType.DMA((norms,)),
        ],
        compiler_params=pltpu.CompilerParams(collective_id=1, has_side_effects=True, vmem_limit_bytes=60 * 1024 * 1024),
    )(parts, small)


def adamw(parameter, moment_one, moment_two, gradient, rate, decay_rate):
    first_new = beta_one * moment_one + (1.0 - beta_one) * gradient
    second_new = beta_two * moment_two + (1.0 - beta_two) * gradient * gradient
    first_hat = first_new / (1.0 - beta_one**STEP)
    second_hat = second_new / (1.0 - beta_two**STEP)
    new_value = parameter - rate * (
        first_hat / (jnp.sqrt(second_hat) + adam_eps) + decay_rate * parameter
    )
    return (new_value, first_new, second_new)


def update_kernel(heads, *refs):
    grad_ref, small_ref, norm_ref = refs[0:3]
    states = [refs[3 + 3 * k : 6 + 3 * k] for k in range(8)]
    outs = refs[27:]
    small = small_ref[...]
    norm = jnp.sqrt(jnp.sum(norm_ref[...], keepdims=True) + jnp.sum(small * small, keepdims=True)[0])
    factor = clip_limit / jnp.maximum(norm, clip_limit)
    outs[0][...] = norm
    u, w = states[1][0].shape
    fu = states[3][0].shape[0]
    base = up16(2 * fu)
    starts = {1: base, 2: base + u, 3: 0, 4: fu}

    def matrix(k, state, gradient, place):
        new_value, first_new, second_new = adamw(
            state[0][place], state[1][place], state[2][place], gradient * factor, learn_rate, weight_decay
        )
        outs[1 + 4 * k][place] = new_value
        outs[2 + 4 * k][place] = new_value.astype(bf16)
        outs[3 + 4 * k][place] = first_new
        outs[4 + 4 * k][place] = second_new

    at = base + 2 * u
    gradient = jnp.concatenate([grad_ref[at : at + u, 0:w], grad_ref[at + u : at + 2 * u, 0:w]], axis=1)
    matrix(0, states[0], gradient, ...)
    for k in (1, 2, 3, 4):
        rows = states[k][0].shape[0]
        matrix(k, states[k], grad_ref[starts[k] : starts[k] + rows, 0:w], ...)
    mine = small_ref[lax.axis_index("fsdp")]
    share = states[6][0].shape[0]
    gradients = (mine[0:6, 0:w], mine[6 : 6 + share, 0:w], small_ref[0, 6 + share : 10 + share, 0:heads])
    for k in range(3):
        state = states[5 + k]
        new_value, first_new, second_new = adamw(
            state[0][...], state[1][...], state[2][...], gradients[k] * factor, small_rate, 0.0
        )
        outs[21 + 3 * k][...] = new_value
        outs[22 + 3 * k][...] = first_new
        outs[23 + 3 * k][...] = second_new


def update(heads, grad, small, norm, states):
    shapes = [jax.ShapeDtypeStruct((1, 1), f32)]
    for k in range(5):
        shape = states[3 * k].shape
        shapes += [jax.ShapeDtypeStruct(shape, kind) for kind in (f32, bf16, f32, f32)]
    for k in range(5, 8):
        shapes += [jax.ShapeDtypeStruct(states[3 * k].shape, f32)] * 3
    return pl.pallas_call(
        partial(update_kernel, heads),
        out_shape=shapes,
        in_specs=[pl.BlockSpec(memory_space=pltpu.VMEM)] * 27,
        out_specs=[pl.BlockSpec(memory_space=pltpu.VMEM)] * len(shapes),
        compiler_params=pltpu.CompilerParams(vmem_limit_bytes=32 * 1024 * 1024),
    )(grad, small, norm, *states)


def body(
    dp,
    fsdp,
    tokens,
    keep_mask,
    cotangent,
    qk_weight,
    qk_first,
    qk_second,
    value_weight,
    value_first,
    value_second,
    out_weight,
    out_first,
    out_second,
    up_weight,
    up_first,
    up_second,
    down_weight,
    down_first,
    down_second,
    vectors,
    vectors_first,
    vectors_second,
    up_bias,
    up_bias_first,
    up_bias_second,
    locality,
    locality_first,
    locality_second,
):
    d = tokens.shape[-1]
    heads = locality.shape[1]
    ff = up_bias.shape[0] * fsdp
    rows = up16(2 * ff // dp) + up16(4 * d // dp)
    everything, small = gather_all(
        dp, fsdp, rows, qk_weight, value_weight.T, out_weight.T, up_weight.T, down_weight, vectors, up_bias
    )
    result, token_grad, parts, small_part = run_block(
        tokens, keep_mask.astype(f32), cotangent, everything, small, locality, ff, 2 if fsdp <= 4 else 1
    )
    grad, small_sum, norm = reduce_all(dp, fsdp, rows, parts, small_part)

    def flat(v):
        return v.reshape(-1, vectors.shape[1])

    states = [qk_weight, qk_first, qk_second]
    states += [v.T for v in (value_weight, value_first, value_second, out_weight, out_first, out_second)]
    states += [v.T for v in (up_weight, up_first, up_second)]
    states += [down_weight, down_first, down_second, vectors, vectors_first, vectors_second]
    states += [flat(up_bias), flat(up_bias_first), flat(up_bias_second), locality, locality_first, locality_second]
    outs = list(update(heads, grad, small_sum, norm, states))
    for k in range(5, 17):
        outs[k] = outs[k].T
    for k in (24, 25, 26):
        outs[k] = outs[k].reshape(up_bias.shape)
    outs[0] = outs[0].reshape(())
    return (result, token_grad, *outs)


def solution(mesh):
    placed = (
        P(("dp", "fsdp"), None, None),
        P(("dp", "fsdp"), None),
        P(("dp", "fsdp"), None, None),
        P("dp", "fsdp"),
        P("dp", "fsdp"),
        P("dp", "fsdp"),
        P("fsdp", "dp"),
        P("fsdp", "dp"),
        P("fsdp", "dp"),
        P("fsdp", "dp"),
        P("fsdp", "dp"),
        P("fsdp", "dp"),
        P("fsdp", "dp"),
        P("fsdp", "dp"),
        P("fsdp", "dp"),
        P("dp", "fsdp"),
        P("dp", "fsdp"),
        P("dp", "fsdp"),
        P(None, "fsdp"),
        P(None, "fsdp"),
        P(None, "fsdp"),
        P("fsdp"),
        P("fsdp"),
        P("fsdp"),
        P(),
        P(),
        P(),
    )
    return jax.shard_map(
        partial(body, mesh.shape["dp"], mesh.shape["fsdp"]),
        mesh=mesh,
        in_specs=placed,
        out_specs=(
            P(("dp", "fsdp"), None, None),
            P(("dp", "fsdp"), None, None),
            P(),
            P("dp", "fsdp"),
            P("dp", "fsdp"),
            P("dp", "fsdp"),
            P("dp", "fsdp"),
            P("fsdp", "dp"),
            P("fsdp", "dp"),
            P("fsdp", "dp"),
            P("fsdp", "dp"),
            P("fsdp", "dp"),
            P("fsdp", "dp"),
            P("fsdp", "dp"),
            P("fsdp", "dp"),
            P("fsdp", "dp"),
            P("fsdp", "dp"),
            P("fsdp", "dp"),
            P("fsdp", "dp"),
            P("dp", "fsdp"),
            P("dp", "fsdp"),
            P("dp", "fsdp"),
            P("dp", "fsdp"),
            P(None, "fsdp"),
            P(None, "fsdp"),
            P(None, "fsdp"),
            P("fsdp"),
            P("fsdp"),
            P("fsdp"),
            P(),
            P(),
            P(),
        ),
        check_vma=False,
    )
```

```python
from functools import partial

import jax
import jax.numpy as jnp
from jax import lax
from jax.experimental import pallas as pl
from jax.experimental.pallas import tpu as pltpu
from jax.sharding import PartitionSpec as P

GRID = 14
STEP = 5
PITCH = 256

norm_eps = 1e-06
learn_rate = 0.03
small_rate = 0.3
beta_one = 0.5
beta_two = 0.5
adam_eps = 1e-08
weight_decay = 0.05
clip_limit = 1.0

LOG2E = 1.4426950408889634
PHI_ZERO = 0.3989422804014327

f32 = jnp.float32
bf16 = jnp.bfloat16


def mm(a, b):
    return lax.dot_general(a, b, (((1,), (0,)), ((), ())), preferred_element_type=f32)


def mm_nt(a, b):
    return lax.dot_general(a, b, (((1,), (1,)), ((), ())), preferred_element_type=f32)


def gelu_parts(u):
    v = u * 0.5**0.5
    cdf = 0.5 * lax.erf(v) + 0.5
    bell = jnp.exp2(v * v * -LOG2E)
    return u * cdf, cdf + (v * (PHI_ZERO * 2**0.5)) * bell


MESH = pl.DeviceIdType.MESH


def up16(v):
    return -(-v // 16) * 16


class Place:
    def __init__(self, dp, fsdp):
        self.cores = 2 if dp % 2 == 0 else 1
        self.zs = dp // self.cores
        self.ys = max(v for v in range(1, fsdp + 1) if fsdp % v == 0 and v * v <= fsdp)
        self.xs = fsdp // self.ys
        self.fs = fsdp
        at_dp, at_f = lax.axis_index("dp"), lax.axis_index("fsdp")
        self.z, self.c = at_dp // self.cores, at_dp % self.cores
        self.y, self.x = at_f // self.xs, at_f % self.xs

    def to(self, dz=0, dc=0, dy=0, dx=0):
        z = lax.rem(self.z + dz, self.zs)
        c = lax.rem(self.c + dc, self.cores)
        y = lax.rem(self.y + dy, self.ys)
        x = lax.rem(self.x + dx, self.xs)
        return (z * self.cores + c, y * self.xs + x)


def greet(peers):
    barrier = pltpu.get_barrier_semaphore()
    for peer in peers:
        pl.semaphore_signal(barrier, inc=1, device_id=peer, device_id_type=MESH)
    pl.semaphore_wait(barrier, len(peers))


def row_plan(fu, u):
    o_at = up16(2 * fu)
    split = up16(o_at + u)
    return o_at, split, split + up16(3 * u)


def gather_kernel(dp, fsdp, rows, qk_ref, vt_ref, ot_ref, upt_ref, dn_ref, vec_ref, upb_ref, tok_ref, cot_ref, all_ref, small_ref, tok_out, cot_out, wide, block, part, slab, rows_s, turned_s, in_qk, in_vt, in_ot, in_upt, in_dn, in_vec, in_upb, in_sem, send, recv, small_send, small_recv, local, turn_sem):
    here = Place(dp, fsdp)
    zs, ys, xs, cores = here.zs, here.ys, here.xs, here.cores
    u, w = vt_ref.shape
    half = rows // 32 * 16
    segs = (pl.ds(0, half), pl.ds(half, rows - half))
    me = here.to()

    peers = [here.to(dz=k) for k in range(1, zs)] + [here.to(dc=k) for k in range(1, cores)]
    peers += [here.to(dy=a, dx=b) for a in range(ys) for b in range(xs) if a or b]

    loads = []
    for ref, into in (
        (qk_ref, in_qk),
        (vt_ref, in_vt),
        (ot_ref, in_ot),
        (upt_ref, in_upt),
        (dn_ref, in_dn),
        (vec_ref, in_vec),
        (upb_ref, in_upb),
    ):
        loads.append(pltpu.make_async_copy(ref, into, in_sem.at[len(loads)]))
        loads[-1].start()
    slots, images, d = tok_ref.shape
    spans = [(lo, min(lo + 128, d)) for lo in range(0, d, 128)]
    arrivals = [pltpu.make_async_copy(ref, slab.at[n], turn_sem.at[n]) for n, ref in enumerate((tok_ref, cot_ref))]
    for copy in arrivals:
        copy.start()

    def turn(n, out):
        arrivals[n].wait()

        def widen(k, _):
            for c, (lo, hi) in enumerate(spans):
                rows_s[c, pl.ds(pl.multiple_of(k * images, 8), images), 0 : hi - lo] = slab[n, k, :, lo:hi].astype(f32)
            return 0

        lax.fori_loop(0, slots, widen, 0, unroll=4)

        def pick(k, _):
            for c, (lo, hi) in enumerate(spans):
                turned_s[n, k, :, lo:hi] = rows_s[c, pl.ds(k, slots, stride=images), :][:, 0 : hi - lo].astype(bf16)
            return 0

        lax.fori_loop(0, images, pick, 0)
        copy = pltpu.make_async_copy(turned_s.at[n], out, turn_sem.at[n])
        copy.start()
        return copy

    wide[...] = jnp.zeros_like(wide)
    part[...] = jnp.zeros_like(part)
    for copy in loads:
        copy.wait()
    fu = in_upt.shape[0]
    o_at, split, _ = row_plan(fu, u)
    wide[0:fu, 0:w] = in_upt[...]
    wide[fu : 2 * fu, 0:w] = in_dn[...]
    wide[o_at : o_at + u, 0:w] = in_ot[...]
    wide[split : split + u, 0:w] = in_vt[...]
    for k in range(in_qk.shape[1] // w):
        at = split + (k + 1) * u
        wide[at : at + u, 0:w] = in_qk[:, k * w : (k + 1) * w]
    block[...] = wide[...].astype(bf16)
    part[0:6, 0:w] = in_vec[...]
    part[6 : 6 + in_upb.shape[0], 0:w] = in_upb[...]

    greet(peers)
    count = [0]
    sent = []

    def push(owner, seg, target, own=False):
        slot = all_ref.at[owner[0], owner[1], segs[seg]]
        flat = owner[0] * here.fs + owner[1]
        copy = pltpu.make_async_remote_copy(
            src_ref=block.at[segs[seg]] if own else slot,
            dst_ref=slot,
            send_sem=send.at[count[0]],
            recv_sem=recv.at[flat, seg],
            device_id=target,
            device_id_type=MESH,
        )
        count[0] += 1
        copy.start()
        sent.append(copy)

    def arrive(owner, seg):
        slot = all_ref.at[owner[0], owner[1], segs[seg]]
        flat = owner[0] * here.fs + owner[1]
        pltpu.make_async_remote_copy(
            src_ref=slot, dst_ref=slot, send_sem=send.at[0], recv_sem=recv.at[flat, seg], device_id=me, device_id_type=MESH
        ).wait_recv()

    own_copy = pltpu.make_async_copy(block, all_ref.at[me[0], me[1]], local.at[0])
    own_copy.start()
    small_copy = pltpu.make_async_copy(part, small_ref.at[me[1]], local.at[1])
    small_copy.start()
    for k in range(1, zs):
        for seg in (0, 1):
            push(me, seg, here.to(dz=k), own=True)
    smalls = []
    for a in range(ys):
        for b in range(xs):
            if a or b:
                n = len(smalls)
                copy = pltpu.make_async_remote_copy(
                    src_ref=part,
                    dst_ref=small_ref.at[me[1]],
                    send_sem=small_send.at[n],
                    recv_sem=small_recv.at[me[1]],
                    device_id=here.to(dy=a, dx=b),
                    device_id_type=MESH,
                )
                copy.start()
                smalls.append(copy)

    def spread(owner, own=False):
        for seg in (0, 1):
            for k in range(1, ys):
                push(owner, seg, here.to(dy=k), own)
            for k in range(1, xs):
                push(owner, seg, here.to(dx=k), own)
        for seg in (0, 1):
            for k in range(1, cores):
                push(owner, seg, here.to(dc=k), own)

    def relay(k):
        for a in range(1, ys):
            owner = here.to(dz=k, dy=a)
            arrive(owner, 0)
            for b in range(1, xs):
                push(owner, 0, here.to(dx=b))
        for b in range(1, xs):
            owner = here.to(dz=k, dx=b)
            arrive(owner, 1)
            for a in range(1, ys):
                push(owner, 1, here.to(dy=a))
        for a in range(1, ys):
            owner = here.to(dz=k, dy=a)
            arrive(owner, 1)
            for seg in (0, 1):
                for c in range(1, cores):
                    push(owner, seg, here.to(dc=c))
        for b in range(1, xs):
            owner = here.to(dz=k, dx=b)
            arrive(owner, 0)
            for seg in (0, 1):
                for c in range(1, cores):
                    push(owner, seg, here.to(dc=c))

    order = [0] + sorted(range(1, zs), key=lambda k: min(k, zs - k))
    spread(me, own=True)
    turns = [turn(0, tok_out), turn(1, cot_out)]
    for n, k in enumerate(order[1:]):
        owner = here.to(dz=k)
        for seg in (0, 1):
            arrive(owner, seg)
        spread(owner)
        relay(order[n])
    relay(order[-1])
    for k in order:
        for a in range(1, ys):
            for b in range(1, xs):
                owner = here.to(dz=k, dy=a, dx=b)
                for seg in (0, 1):
                    arrive(owner, seg)
                    for c in range(1, cores):
                        push(owner, seg, here.to(dc=c))
    for c in range(1, cores):
        for k in order:
            for a in range(ys):
                for b in range(xs):
                    for seg in (0, 1):
                        arrive(here.to(dz=k, dy=a, dx=b, dc=c), seg)
    for a in range(ys):
        for b in range(xs):
            if a or b:
                peer = here.to(dy=a, dx=b)
                pltpu.make_async_remote_copy(
                    src_ref=part,
                    dst_ref=small_ref.at[peer[1]],
                    send_sem=small_send.at[0],
                    recv_sem=small_recv.at[peer[1]],
                    device_id=me,
                    device_id_type=MESH,
                ).wait_recv()
    for copy in sent + smalls:
        copy.wait_send()
    own_copy.wait()
    small_copy.wait()
    for copy in turns:
        copy.wait()


def gather_sends(dp, fsdp):
    here = Place.__new__(Place)
    cores = 2 if dp % 2 == 0 else 1
    zs = dp // cores
    ys = max(v for v in range(1, fsdp + 1) if fsdp % v == 0 and v * v <= fsdp)
    xs = fsdp // ys
    n = 2 * (zs - 1) + zs * 2 * (ys - 1 + xs - 1) + 2 * zs * (ys - 1) * (xs - 1)
    return n + zs * ys * xs * 2 * (cores - 1)


def gather_all(dp, fsdp, rows, qk, vt, ot, upt, dn, vectors, up_bias, tokens, cotangent):
    images, slots, d = tokens.shape
    flat_bias = up_bias.reshape(-1, vt.shape[1])
    return pl.pallas_call(
        partial(gather_kernel, dp, fsdp, rows),
        out_shape=[
            jax.ShapeDtypeStruct((dp, fsdp, rows, 128), bf16),
            jax.ShapeDtypeStruct((fsdp, 16, 128), f32),
            jax.ShapeDtypeStruct((images, slots, d), bf16),
            jax.ShapeDtypeStruct((images, slots, d), bf16),
        ],
        in_specs=[pl.BlockSpec(memory_space=pl.ANY)] * 9,
        out_specs=[pl.BlockSpec(memory_space=pl.ANY)] * 4,
        scratch_shapes=[
            pltpu.VMEM((rows, 128), f32),
            pltpu.VMEM((rows, 128), bf16),
            pltpu.VMEM((16, 128), f32),
            pltpu.VMEM((2, slots, images, d), bf16),
            pltpu.VMEM((-(-d // 128), slots * images, 128), f32),
            pltpu.VMEM((2, images, slots, d), bf16),
            *[pltpu.VMEM(v.shape, f32) for v in (qk, vt, ot, upt, dn, vectors, flat_bias)],
            pltpu.SemaphoreType.DMA((7,)),
            pltpu.SemaphoreType.DMA((gather_sends(dp, fsdp),)),
            pltpu.SemaphoreType.DMA((dp * fsdp, 2)),
            pltpu.SemaphoreType.DMA((fsdp,)),
            pltpu.SemaphoreType.DMA((fsdp,)),
            pltpu.SemaphoreType.DMA((2,)),
            pltpu.SemaphoreType.DMA((2,)),
        ],
        compiler_params=pltpu.CompilerParams(collective_id=0, has_side_effects=True, vmem_limit_bytes=62 * 1024 * 1024),
    )(qk, vt, ot, upt, dn, vectors, flat_bias, tokens.transpose(1, 0, 2), cotangent.transpose(1, 0, 2))


def identity():
    rows = lax.broadcasted_iota(jnp.int32, (PITCH, PITCH), 0)
    cols = lax.broadcasted_iota(jnp.int32, (PITCH, PITCH), 1)
    return jnp.where(rows == cols, 1.0, 0.0).astype(bf16)


def one_hot(shape, w, goal):
    r = lax.broadcasted_iota(jnp.int32, shape, 0)
    c = lax.broadcasted_iota(jnp.int32, shape, 1)
    block, lane = r // 128, r % 128
    return jnp.where((c == goal(block, lane)) & (lane < w), 1.0, 0.0).astype(bf16)


def offset_planes(keys):
    j = lax.broadcasted_iota(jnp.int32, (keys, PITCH), 0)
    i = lax.broadcasted_iota(jnp.int32, (keys, PITCH), 1)
    rj, ri = j // GRID, i // GRID
    dc = ((j - rj * GRID) - (i - ri * GRID)).astype(f32)
    dr = (rj - ri).astype(f32)
    return dc, dr, dc * dc + dr * dr


def gates(locality_ref, heads):
    sig, cosig = [], []
    for h in range(heads):
        s = 1.0 / (1.0 + jnp.exp(-jnp.full((1, PITCH), locality_ref[3, h], f32)))
        sig.append(s)
        cosig.append(1.0 - s)
    return sig, cosig


def windows(heads, hw, d):
    wins = []
    for h in range(heads):
        lo = (h * hw) // 128 * 128
        wins.append((lo, min(lo + PITCH, d), h * hw - lo))
    return wins


def lane_sums(v):
    return lax.dot_general(
        jnp.ones((8, v.shape[1]), f32),
        v,
        (((1,), (1,)), ((), ())),
        preferred_element_type=f32,
        precision=lax.Precision.HIGHEST,
    )[0:1]


def column(row):
    return jnp.broadcast_to(row, (128, 128)).T


def norm_stats(x):
    d = x.shape[0]
    mean = jnp.sum(x, axis=0, keepdims=True) * (1.0 / d)
    center = x - mean
    rstd = lax.rsqrt(jnp.sum(center * center, axis=0, keepdims=True) * (1.0 / d) + norm_eps)
    return center * rstd, rstd


def norm_back(grad, gain, normal, rstd):
    d = grad.shape[0]
    pull = grad * gain
    m1 = jnp.sum(pull, axis=0, keepdims=True) * (1.0 / d)
    m2 = jnp.sum(pull * normal, axis=0, keepdims=True) * (1.0 / d)
    return rstd * (pull - m1 - normal * m2)


def forward_kernel(
    images,
    slots,
    heads,
    locality_ref,
    tok_ref,
    cot_ref,
    vis_ref,
    all_ref,
    small_ref,
    res_ref,
    xt_ref,
    qkvt_ref,
    pa_ref,
    pb_ref,
    dot_ref,
    mg_ref,
    part_ref,
    gsmall_ref,
    wqk_ref,
    wv_ref,
    eye,
    pick,
    pick_a,
    pick_b,
    cat_s,
    chunk_s,
    chunk_sem,
    wqkvt_s,
    wot_s,
    wo_s,
    wupt_s,
    wup_s,
    wdnt_s,
    wdn_s,
    vec_s,
    upb_s,
    pad_in,
    placed,
    acc_out,
    acc_up,
    acc_down,
    acc_vec,
    acc_upb,
    hid_s,
    kn_s,
    win_s,
    sc_s,
    mix_s,
    mixture_s,
    xh2_s,
    rstd_s,
    second_s,
    mid_s,
    cot_s,
    dlow_s,
    up_s,
    back_s,
    act_s,
    ug_s,
    blow_s,
):
    d = tok_ref.shape[-1]
    ff = upb_s.shape[0]
    dp, fsdp, rows_all, _ = all_ref.shape
    u, w = d // dp, d // fsdp
    fu = ff // dp
    o_at, split, _ = row_plan(fu, u)
    rest = rows_all - o_at
    hw = d // heads
    keys = placed.shape[1]
    n = images * PITCH
    scale = hw**-0.5
    step = pl.program_id(0)

    @pl.when(step == 0)
    def _():
        eye[...] = identity()
        pad_in[...] = jnp.zeros_like(pad_in)
        dc, dr, far = offset_planes(keys)
        for h in range(heads):
            placed[h] = (locality_ref[0, h] * dc + locality_ref[1, h] * dr + locality_ref[2, h] * far) * LOG2E

        pick[...] = one_hot(pick.shape, w, lambda block, lane: block * w + lane)
        pick_a[...] = one_hot(pick_a.shape, w, lambda block, lane: block * (2 * w) + lane)
        pick_b[...] = one_hot(pick_b.shape, w, lambda block, lane: block * (2 * w) + w + lane)

        def fetch(k):
            return pltpu.make_async_copy(all_ref.at[k, :, pl.ds(0, o_at)], chunk_s.at[k % 2], chunk_sem.at[k % 2])

        def fetch_rest(k):
            return pltpu.make_async_copy(
                all_ref.at[k, :, pl.ds(o_at, rest)], chunk_s.at[k % 2, :, pl.ds(0, rest)], chunk_sem.at[k % 2]
            )

        fetch(0).start()

        def unpack(k, _):
            fetch(k).wait()

            @pl.when(k + 1 < dp)
            def _():
                fetch(k + 1).start()

            for f in range(fsdp):
                cat_s[0:o_at, 128 * f : 128 * (f + 1)] = chunk_s[k % 2, f].astype(f32)
            big = pl.ds(pl.multiple_of(fu * k, 8), fu) if fu % 8 == 0 else pl.ds(fu * k, fu)
            acc_up[big, :] = mm(cat_s[0:fu, :].astype(bf16), pick[...])
            acc_down[big, :] = mm(cat_s[fu : 2 * fu, :].astype(bf16), pick[...])
            return 0

        if fu % 8 == 0:
            lax.fori_loop(0, dp, unpack, 0)
        else:
            for k in range(dp):
                unpack(k, 0)

        def turned(ref, out_ref, row=0):
            for lo in range(0, ref.shape[1], PITCH):
                hi = min(lo + PITCH, ref.shape[1])
                out_ref[row + lo : row + hi, :] = mm_nt(eye[0 : hi - lo, 0 : hi - lo], ref[:, lo:hi]).astype(bf16)

        wupt_s[...] = acc_up[...].astype(bf16)
        turned(wupt_s, wup_s)
        wdn_s[...] = acc_down[...].astype(bf16)
        turned(wdn_s, wdnt_s)
        fetch_rest(0).start()
        for k in range(dp):
            fetch_rest(k).wait()
            if k + 1 < dp:
                fetch_rest(k + 1).start()
            for f in range(fsdp):
                cat_s[0:rest, 128 * f : 128 * (f + 1)] = chunk_s[k % 2, f, 0:rest].astype(f32)

            def wide(at):
                return cat_s[at : at + u, :].astype(bf16)

            acc_out[u * k : u * (k + 1), :] = mm(wide(0), pick[...])
            acc_up[u * k : u * (k + 1), :] = mm(wide(split - o_at), pick[...])
            both = mm(wide(split - o_at + u), pick_a[...]) + mm(wide(split - o_at + 2 * u), pick_b[...])
            acc_down[u * k : u * (k + 1), :] = both[:, 0:d]
            acc_down[d + u * k : d + u * (k + 1), :] = both[:, d : 2 * d]
        wot_s[...] = acc_out[...].astype(bf16)
        turned(wot_s, wo_s)
        wqkvt_s[2 * d : 3 * d, :] = acc_up[0:d, :].astype(bf16)
        turned(wqkvt_s.at[2 * d : 3 * d], wv_ref)
        wqk_ref[0] = acc_down[0:d, :].astype(bf16)
        wqk_ref[1] = acc_down[d : 2 * d, :].astype(bf16)
        turned(wqk_ref.at[0], wqkvt_s)
        turned(wqk_ref.at[1], wqkvt_s, d)
        for f in range(fsdp):
            for r in range(6):
                vec_s[r, w * f : w * (f + 1), :] = column(small_ref[f, r : r + 1, :])[0:w]
            for r in range(ff // d):
                at = (f * (ff // d) + r) * w
                upb_s[at : at + w, :] = column(small_ref[f, 6 + r : 7 + r, :])[0:w]
        for ref in (acc_out, acc_up, acc_down, acc_vec, acc_upb, win_s, mix_s):
            ref[...] = jnp.zeros_like(ref)

    tiles = [slice(128 * k, 128 * (k + 1)) for k in range(n // 128)]

    def seen(t):
        at = 128 * t
        return vis_ref[at // PITCH, 0:1, at % PITCH : at % PITCH + 128]

    def fold(v):
        total = v[:, 0:128]
        for k in range(1, n // 128):
            total = total + v[:, 128 * k : 128 * (k + 1)]
        return total

    def turn_in(ref, b, out):
        pad_in[0:slots, 0:d] = ref[b]
        for lo in range(0, d, PITCH):
            hi = min(lo + PITCH, d)
            out[lo:hi, :] = mm_nt(eye[0 : hi - lo, 0 : hi - lo], pad_in[:, lo:hi]).astype(bf16)

    def enter(b, _):
        cols = pl.ds(pl.multiple_of(b * PITCH, PITCH), PITCH)
        turn_in(tok_ref, b, xt_ref.at[b])
        turn_in(cot_ref, b, cot_s.at[:, cols])
        return 0

    lax.fori_loop(0, images, enter, 0)

    def x_tile(t):
        at = 128 * t
        return xt_ref[at // PITCH, :, at % PITCH : at % PITCH + 128].astype(f32)

    for t, tile in enumerate(tiles):
        normal, _ = norm_stats(x_tile(t))
        hid_s[:, tile] = (normal * vec_s[0] + vec_s[1]).astype(bf16)
        down = cot_s[:, tile].astype(f32) * seen(t)
        dlow_s[:, tile] = down.astype(bf16)
        acc_vec[3] += down
    joint = mm(wqkvt_s[...], hid_s[...]).astype(bf16)
    for b in range(images):
        qkvt_ref[b] = joint[:, PITCH * b : PITCH * (b + 1)]

    sig, cosig = gates(locality_ref, heads)
    wins = windows(heads, hw, d)

    def forward(b, _):
        cols = pl.ds(pl.multiple_of(b * PITCH, PITCH), PITCH)
        kn_s[...] = mm_nt(eye[0:keys, :], qkvt_ref[b, d : 2 * d, :]).astype(bf16)
        key_vis = mm_nt(eye[0:keys, :], jnp.broadcast_to(vis_ref[b, 0:1, :], (PITCH, PITCH)).astype(bf16))
        bias = jnp.where(key_vis > 0.5, 0.0, -1e30)

        def fa(h):
            lo, hi, at = wins[h]
            win_s[h, at : at + hw, :] = qkvt_ref[b, h * hw : (h + 1) * hw, :]
            sc_s[h % 2] = mm(kn_s[:, lo:hi], win_s[h, 0 : hi - lo, :])

        def fb(h):
            scores = sc_s[h % 2] * (scale * LOG2E) + bias
            p = jnp.exp2(scores - jnp.max(scores, axis=0, keepdims=True))
            pa = p * (cosig[h] / jnp.sum(p, axis=0, keepdims=True))
            z = placed[h] + bias
            e = jnp.exp2(z - jnp.max(z, axis=0, keepdims=True))
            pb = e * (sig[h] / jnp.sum(e, axis=0, keepdims=True))
            pa_ref[b, h] = pa.astype(bf16)
            pb_ref[b, h] = pb.astype(bf16)
            mix_s[h, 0:keys, :] = (pa + pb).astype(bf16)

        def fc(h):
            mixture_s[h * hw : (h + 1) * hw, cols] = mm(
                qkvt_ref[b, 2 * d + h * hw : 2 * d + (h + 1) * hw, :], mix_s[h]
            ).astype(bf16)

        for t in range(heads + 2):
            if t < heads:
                fa(t)
            if t >= 2:
                fc(t - 2)
            if 1 <= t <= heads:
                fb(t - 1)
        return 0

    lax.fori_loop(0, images, forward, 0)

    mid_s[...] = mm(wot_s[...], mixture_s[...])
    for t, tile in enumerate(tiles):
        middle = x_tile(t) + seen(t) * (mid_s[:, tile] + vec_s[4])
        mid_s[:, tile] = middle
        normal, rstd = norm_stats(middle)
        xh2_s[:, tile] = normal
        rstd_s[0:1, tile] = rstd
        second_s[:, tile] = (normal * vec_s[2] + vec_s[3]).astype(bf16)

    chunk = up_s.shape[1]
    steps = ff // chunk

    def feed_start(c):
        part = slice(c * chunk, (c + 1) * chunk)
        up_s[c % 2] = mm(wupt_s[part, :], second_s[...])
        back_s[c % 2] = mm(wdn_s[part, :], dlow_s[...])

    feed_start(0)
    for c in range(steps):
        if c + 1 < steps:
            feed_start(c + 1)
        part = slice(c * chunk, (c + 1) * chunk)
        act, slope = gelu_parts(up_s[c % 2] + jnp.concatenate([upb_s[part, :]] * (n // 128), axis=1))
        act_s[part, :] = act.astype(bf16)
        ug = (back_s[c % 2] * slope).astype(bf16)
        ug_s[part, :] = ug
        acc_upb[part, :] += fold(ug.astype(f32))

    second_grad = mm(wup_s[...], ug_s[...])
    acc_up[...] += mm_nt(ug_s[...], second_s[...])
    for t, tile in enumerate(tiles):
        grad = second_grad[:, tile]
        normal = xh2_s[:, tile]
        acc_vec[0] += grad * normal
        acc_vec[1] += grad
        middle_grad = cot_s[:, tile].astype(f32) + norm_back(grad, vec_s[2], normal, rstd_s[0:1, tile])
        at = 128 * t
        mg_ref[at // PITCH, :, at % PITCH : at % PITCH + 128] = middle_grad.astype(bf16)
        low = (seen(t) * middle_grad).astype(bf16)
        blow_s[:, tile] = low
        acc_vec[2] += low.astype(f32)
    acc_down[...] += mm_nt(act_s[...], dlow_s[...])
    mixture_grad = mm(wo_s[...], blow_s[...]).astype(bf16)
    for b in range(images):
        dot_ref[b] = mixture_grad[:, PITCH * b : PITCH * (b + 1)]
    acc_out[...] += mm_nt(blow_s[...], mixture_s[...])
    downward = mm(wdnt_s[...], act_s[...])
    for t, tile in enumerate(tiles):
        dlow_s[:, tile] = (mid_s[:, tile] + seen(t) * (downward[:, tile] + vec_s[5])).astype(bf16)
    for b in range(images):
        res_ref[b] = mm_nt(eye[0:slots, :], dlow_s[:, b * PITCH : (b + 1) * PITCH]).astype(bf16)

    @pl.when(step == pl.num_programs(0) - 1)
    def _():
        def put_rest(k):
            return pltpu.make_async_copy(
                chunk_s.at[k % 2, :, pl.ds(0, split - o_at)],
                part_ref.at[k, :, pl.ds(o_at, split - o_at)],
                chunk_sem.at[k % 2],
            )

        cat_s[...] = jnp.zeros_like(cat_s)
        for k in range(dp):
            cat_s[0:u, :] = mm_nt(acc_out[u * k : u * (k + 1), :].astype(bf16), pick[...])
            if k >= 2:
                put_rest(k - 2).wait()
            for f in range(fsdp):
                chunk_s[k % 2, f, 0 : split - o_at] = cat_s[0 : split - o_at, 128 * f : 128 * (f + 1)].astype(bf16)
            put_rest(k).start()
        for k in range(max(dp - 2, 0), dp):
            put_rest(k).wait()
        if o_at > 2 * fu:
            cat_s[2 * fu : o_at, :] = jnp.zeros((o_at - 2 * fu, fsdp * 128), f32)

        def put(k):
            return pltpu.make_async_copy(chunk_s.at[k % 2], part_ref.at[k, :, pl.ds(0, o_at)], chunk_sem.at[k % 2])

        def pack(k, _):
            big = pl.ds(pl.multiple_of(fu * k, 8), fu) if fu % 8 == 0 else pl.ds(fu * k, fu)
            cat_s[0:fu, :] = mm_nt(acc_up[big, :].astype(bf16), pick[...])
            cat_s[fu : 2 * fu, :] = mm_nt(acc_down[big, :].astype(bf16), pick[...])

            @pl.when(k >= 2)
            def _():
                put(k - 2).wait()

            for f in range(fsdp):
                chunk_s[k % 2, f] = cat_s[0:o_at, 128 * f : 128 * (f + 1)].astype(bf16)
            put(k).start()
            return 0

        if fu % 8 == 0:
            lax.fori_loop(0, dp, pack, 0)
        else:
            for k in range(dp):
                pack(k, 0)
        for k in range(max(dp - 2, 0), dp):
            put(k).wait()

        gsmall_ref[...] = jnp.zeros_like(gsmall_ref)
        for f in range(fsdp):
            for r in range(4):
                gsmall_ref[f, 2 + r : 3 + r, 0:w] = lane_sums(acc_vec[r, w * f : w * (f + 1), :])
            for r in range(ff // d):
                lo = (f * (ff // d) + r) * w
                gsmall_ref[f, 6 + r : 7 + r, 0:w] = lane_sums(acc_upb[lo : lo + w, :])


def run_forward(tokens, visible, cotangent, everything, small, locality, ff, images):
    b, slots, d = tokens.shape
    heads = locality.shape[1]
    keys = up16(slots)
    n = images * PITCH
    dp, fsdp, _, _ = everything.shape
    o_at, split, _ = row_plan(ff // dp, d // dp)
    vis = jnp.pad(visible, ((0, 0), (0, PITCH - slots)))[:, None, :]

    def whole(shape):
        return pl.BlockSpec(shape, lambda g: (0,) * len(shape), pipeline_mode=pl.Buffered(1))

    def per(shape):
        return pl.BlockSpec((images,) + shape, lambda g: (g,) + (0,) * len(shape))

    kept_shapes = [(d, PITCH), (3 * d, PITCH), (heads, keys, PITCH), (heads, keys, PITCH), (d, PITCH), (d, PITCH)]
    out_shapes = [jax.ShapeDtypeStruct((b, slots, d), bf16)]
    out_shapes += [jax.ShapeDtypeStruct((b,) + shape, bf16) for shape in kept_shapes]
    out_shapes += [
        jax.ShapeDtypeStruct((dp, fsdp, split, 128), bf16),
        jax.ShapeDtypeStruct((fsdp, 16, 128), f32),
        jax.ShapeDtypeStruct((2, d, d), bf16),
        jax.ShapeDtypeStruct((d, d), bf16),
    ]
    scratch = [
        ((PITCH, PITCH), bf16),
        ((fsdp * 128, d), bf16),
        ((fsdp * 128, 2 * d), bf16),
        ((fsdp * 128, 2 * d), bf16),
        ((o_at, fsdp * 128), f32),
        ((2, fsdp, o_at, 128), bf16),
        None,
        ((3 * d, d), bf16),
        ((d, d), bf16),
        ((d, d), bf16),
        ((ff, d), bf16),
        ((d, ff), bf16),
        ((d, ff), bf16),
        ((ff, d), bf16),
        ((6, d, 128), f32),
        ((ff, 128), f32),
        ((PITCH, d), bf16),
        ((heads, keys, PITCH), f32),
        ((d, d), f32),
        ((ff, d), f32),
        ((ff, d), f32),
        ((4, d, 128), f32),
        ((ff, 128), f32),
        ((d, n), bf16),
        ((keys, d), bf16),
        ((heads, PITCH, PITCH), bf16),
        ((2, keys, PITCH), f32),
        ((heads, PITCH, PITCH), bf16),
        ((d, n), bf16),
        ((d, n), f32),
        ((8, n), f32),
        ((d, n), bf16),
        ((d, n), f32),
        ((d, n), bf16),
        ((d, n), bf16),
        ((2, ff // 6, n), f32),
        ((2, ff // 6, n), f32),
        ((ff, n), bf16),
        ((ff, n), bf16),
        ((d, n), bf16),
    ]
    scratch = [pltpu.SemaphoreType.DMA((2,)) if entry is None else pltpu.VMEM(*entry) for entry in scratch]
    outs = pl.pallas_call(
        partial(forward_kernel, images, slots, heads),
        grid=(b // images,),
        out_shape=out_shapes,
        in_specs=[
            pl.BlockSpec(memory_space=pltpu.SMEM),
            per((slots, d)),
            per((slots, d)),
            per((1, PITCH)),
            pl.BlockSpec(memory_space=pl.ANY),
            whole((fsdp, 16, 128)),
        ],
        out_specs=[per((slots, d))]
        + [per(shape) for shape in kept_shapes]
        + [pl.BlockSpec(memory_space=pl.ANY), whole((fsdp, 16, 128)), whole((2, d, d)), whole((d, d))],
        scratch_shapes=scratch,
        compiler_params=pltpu.CompilerParams(
            dimension_semantics=("arbitrary",), vmem_limit_bytes=63 * 1024 * 1024
        ),
        cost_estimate=pl.CostEstimate(flops=60_000_000_000, bytes_accessed=90_000_000, transcendentals=0),
    )(locality, tokens, cotangent, vis, everything, small)
    return outs[0], outs[7], outs[8], outs[9], outs[10], outs[1:7]


class Reducer:
    def __init__(self, here, rows, mine, theirs, other, bufs, send, recv):
        self.here, self.mine, self.theirs, self.other = here, mine, theirs, other
        self.got_x, self.got_y, self.got_x2, self.got_y2, self.got_z = bufs
        self.send, self.recv = send, recv
        half = rows // 32 * 16
        self.segs = (pl.ds(0, half), pl.ds(half, rows - half))
        self.order = z_order(here.zs)
        self.keys = reducer_keys(here.zs, here.ys, here.xs, here.cores)

    def f_at(self, dy, dx):
        return self.here.to(dy=dy, dx=dx)[1]

    def copy(self, key):
        here, segs, n = self.here, self.segs, key[1]
        if key[0] == "pair":
            src, dst, target = self.theirs(n), self.other.at[n], here.to(dc=1)
        elif key[0] == "a1":
            _, _, a, b = key
            src, dst, target = self.mine(n).at[self.f_at(a, b), segs[0]], self.got_x.at[n, a, b - 1], here.to(dx=b)
        elif key[0] == "b1":
            _, _, a, b = key
            src, dst, target = self.mine(n).at[self.f_at(a, b), segs[1]], self.got_y.at[n, b, a - 1], here.to(dy=a)
        elif key[0] == "a2":
            src, dst, target = self.mine(n).at[self.f_at(key[2], 0), segs[0]], self.got_y2.at[n, key[2] - 1], here.to(dy=key[2])
        elif key[0] == "b2":
            src, dst, target = self.mine(n).at[self.f_at(0, key[2]), segs[1]], self.got_x2.at[n, key[2] - 1], here.to(dx=key[2])
        else:
            seg = segs[key[2]]
            src, dst, target = self.mine(n).at[self.f_at(0, 0), seg], self.got_z.at[n, seg], here.to(dz=self.order[n])
        at = self.keys.index(key)
        return pltpu.make_async_remote_copy(
            src_ref=src, dst_ref=dst, send_sem=self.send.at[at], recv_sem=self.recv.at[at], device_id=target, device_id_type=MESH
        )

    def add(self, n, f, seg, got):
        ref = self.mine(n)
        ref[f, self.segs[seg]] = (ref[f, self.segs[seg]].astype(f32) + got.astype(f32)).astype(bf16)

    def begin(self):
        if self.here.cores > 1:
            for n in range(self.here.zs):
                self.copy(("pair", n)).start()

    def stage_one(self, n):
        here = self.here
        if here.cores > 1:
            self.copy(("pair", n)).wait_recv()
            ref = self.mine(n)

            def body(f, _):
                ref[f] = (ref[f].astype(f32) + self.other[n, f].astype(f32)).astype(bf16)
                return 0

            lax.fori_loop(0, here.fs, body, 0)
        for a in list(range(1, here.ys)) + [0]:
            for b in range(1, here.xs):
                self.copy(("a1", n, a, b)).start()
        for b in list(range(1, here.xs)) + [0]:
            for a in range(1, here.ys):
                self.copy(("b1", n, a, b)).start()

    def stage_two(self, n):
        here = self.here
        for a in list(range(1, here.ys)) + [0]:
            for b in range(1, here.xs):
                self.copy(("a1", n, a, b)).wait_recv()
                self.add(n, self.f_at(a, 0), 0, self.got_x[n, a, b - 1])
            if a:
                self.copy(("a2", n, a)).start()
        for b in list(range(1, here.xs)) + [0]:
            for a in range(1, here.ys):
                self.copy(("b1", n, a, b)).wait_recv()
                self.add(n, self.f_at(0, b), 1, self.got_y[n, b, a - 1])
            if b:
                self.copy(("b2", n, b)).start()

    def stage_three(self, n):
        here = self.here
        for a in range(1, here.ys):
            self.copy(("a2", n, a)).wait_recv()
            self.add(n, self.f_at(0, 0), 0, self.got_y2[n, a - 1])
        for b in range(1, here.xs):
            self.copy(("b2", n, b)).wait_recv()
            self.add(n, self.f_at(0, 0), 1, self.got_x2[n, b - 1])
        if self.order[n]:
            for seg in (0, 1):
                self.copy(("z", n, seg)).start()

    def turn(self, t):
        zs = self.here.zs
        if t < zs:
            self.stage_one(t)
        if 1 <= t <= zs:
            self.stage_two(t - 1)
        if 2 <= t < zs + 2:
            self.stage_three(t - 2)

    def total(self):
        zs = self.here.zs
        total = self.mine(zs - 1)[self.f_at(0, 0)].astype(f32)
        for n in range(zs - 1):
            for seg in (0, 1):
                self.copy(("z", n, seg)).wait_recv()
            total = total + self.got_z[n].astype(f32)
        return total

    def finish(self):
        for key in self.keys:
            self.copy(key).wait_send()


def z_order(zs):
    return sorted(range(1, zs), key=lambda k: min(k, zs - k)) + [0]


def reducer_keys(zs, ys, xs, cores):
    keys = []
    for n in range(zs):
        if cores > 1:
            keys.append(("pair", n))
        keys += [("a1", n, a, b) for a in range(ys) for b in range(1, xs)]
        keys += [("b1", n, a, b) for a in range(1, ys) for b in range(xs)]
        keys += [("a2", n, a) for a in range(1, ys)] + [("b2", n, b) for b in range(1, xs)]
        if n < zs - 1:
            keys += [("z", n, 0), ("z", n, 1)]
    return keys


def reducer_buffers(zs, ys, xs, rows):
    half = rows // 32 * 16
    rest = rows - half
    return [
        pltpu.VMEM((zs, ys, max(xs - 1, 1), half, 128), bf16),
        pltpu.VMEM((zs, xs, max(ys - 1, 1), rest, 128), bf16),
        pltpu.VMEM((zs, max(xs - 1, 1), rest, 128), bf16),
        pltpu.VMEM((zs, max(ys - 1, 1), half, 128), bf16),
        pltpu.VMEM((zs, rows, 128), bf16),
    ]


def exchange(here, ref, buf, send, recv, base, coordinate, size, targets):
    buf[base + coordinate] = ref[...]
    for k, target in enumerate(targets):
        pltpu.make_async_remote_copy(
            src_ref=ref,
            dst_ref=buf.at[base + coordinate],
            send_sem=send.at[base + k],
            recv_sem=recv.at[base + coordinate],
            device_id=target,
            device_id_type=MESH,
        ).start()

    def add():
        for k in range(1, size):
            pltpu.make_async_remote_copy(
                src_ref=ref,
                dst_ref=buf.at[base + coordinate],
                send_sem=send.at[base + k - 1],
                recv_sem=recv.at[base],
                device_id=here.to(),
                device_id_type=MESH,
            ).wait_send()
        for k in range(1, size):
            at = base + lax.rem(coordinate + k, size)
            pltpu.make_async_remote_copy(
                src_ref=ref,
                dst_ref=buf.at[at],
                send_sem=send.at[base],
                recv_sem=recv.at[at],
                device_id=here.to(),
                device_id_type=MESH,
            ).wait_recv()
        total = buf[base]
        for k in range(1, size):
            total = total + buf[base + k]
        ref[...] = total

    return add


def backward_kernel(
    images,
    slots,
    heads,
    dp,
    fsdp,
    ff,
    total_steps,
    locality_ref,
    xt_ref,
    qkvt_ref,
    pa_ref,
    pb_ref,
    dot_ref,
    mg_ref,
    small_ref,
    gsmall_ref,
    wqk_ref,
    wv_ref,
    part_ref,
    tgrad_ref,
    grad_ref,
    sum_ref,
    norm_ref,
    eye,
    pick,
    perm,
    cat_s,
    vec_s,
    acc_qk,
    acc_v,
    acc_vec,
    acc_place,
    acc_gate,
    hid_s,
    xh_s,
    rstd_s,
    vn_s,
    win_s,
    sc_s,
    mix_s,
    ds_s,
    dqkv_s,
    tg_s,
    last_s,
    a_mine,
    a_other,
    a_x,
    a_y,
    a_x2,
    a_y2,
    a_z,
    b_other,
    b_x,
    b_y,
    b_x2,
    b_y2,
    b_z,
    small_buf,
    norm_buf,
    load,
    a_send,
    a_recv,
    b_send,
    b_recv,
    sm_send,
    sm_recv,
    nm_send,
    nm_recv,
):
    d = xt_ref.shape[1]
    u, w = d // dp, d // fsdp
    _, split, rows_all = row_plan(ff // dp, u)
    hw = d // heads
    keys = acc_place.shape[1]
    n = images * PITCH
    scale = hw**-0.5
    step = pl.program_id(0)
    count = pl.num_programs(0)
    here = Place(dp, fsdp)
    zs, ys, xs, cores = here.zs, here.ys, here.xs, here.cores
    order = z_order(zs)

    def plane(k, dc=0):
        return here.to(dz=order[k], dc=dc)[0]

    first = Reducer(
        here,
        split,
        lambda k: a_mine.at[k],
        lambda k: part_ref.at[plane(k, 1)],
        a_other,
        (a_x, a_y, a_x2, a_y2, a_z),
        a_send,
        a_recv,
    )
    last = Reducer(
        here,
        rows_all - split,
        lambda k: last_s.at[plane(k)],
        lambda k: last_s.at[plane(k, 1)],
        b_other,
        (b_x, b_y, b_x2, b_y2, b_z),
        b_send,
        b_recv,
    )

    def loading(k):
        return pltpu.make_async_copy(part_ref.at[plane(k)], a_mine.at[k], load.at[k])

    @pl.when(step == 0)
    def _():
        for k in range(zs):
            loading(k).start()
        peers = [here.to(dz=k) for k in range(1, zs)] + [here.to(dc=k) for k in range(1, cores)]
        peers += [here.to(dy=a, dx=b) for a in range(ys) for b in range(xs) if a or b]
        peers += [here.to(dz=k, dc=c) for k in range(1, zs) for c in range(1, cores)]
        greet(peers)
        first.begin()
        eye[...] = identity()
        pick[...] = one_hot(pick.shape, w, lambda block, lane: block * w + lane)
        e = lax.broadcasted_iota(jnp.int32, (2 * d, 1), 0)
        goal = (e % (2 * w)) // w * d + e // (2 * w) * w + e % w
        perm[...] = jnp.where(lax.broadcasted_iota(jnp.int32, perm.shape, 1) == goal, 1.0, 0.0).astype(bf16)
        for f in range(fsdp):
            for r in range(2):
                vec_s[r, w * f : w * (f + 1), :] = column(small_ref[f, r : r + 1, :])[0:w]
        for ref in (acc_qk, acc_v, acc_vec, acc_place, acc_gate, win_s, mix_s, ds_s):
            ref[...] = jnp.zeros_like(ref)
        for k in range(zs):
            loading(k).wait()

    spread = total_steps
    for t in range(zs + 2):

        @pl.when(step == min(t + 1, spread - 1))
        def _(t=t):
            first.turn(t)

    sig, cosig = gates(locality_ref, heads)
    wins = windows(heads, hw, d)
    tiles = [slice(128 * k, 128 * (k + 1)) for k in range(n // 128)]

    def place_of(t):
        at = 128 * t
        return at // PITCH, slice(at % PITCH, at % PITCH + 128)

    for t, tile in enumerate(tiles):
        b, lane = place_of(t)
        normal, rstd = norm_stats(xt_ref[b, :, lane].astype(f32))
        xh_s[:, tile] = normal
        rstd_s[0:1, tile] = rstd
        hid_s[:, tile] = (normal * vec_s[0] + vec_s[1]).astype(bf16)

    def backward(b, _):
        cols = pl.ds(pl.multiple_of(b * PITCH, PITCH), PITCH)
        vn_s[...] = mm_nt(eye[0:keys, :], qkvt_ref[b, 2 * d : 3 * d, :]).astype(bf16)

        def ba(h):
            lo, hi, at = wins[h]
            win_s[h, at : at + hw, :] = dot_ref[b, h * hw : (h + 1) * hw, :]
            sc_s[h % 2] = mm(vn_s[:, lo:hi], win_s[h, 0 : hi - lo, :])

        def bb(h):
            g = sc_s[h % 2]
            pa = pa_ref[b, h].astype(f32)
            pb = pb_ref[b, h].astype(f32)
            mix_s[h, 0:keys, :] = (pa + pb).astype(bf16)
            pull_a = jnp.sum(g * pa, axis=0, keepdims=True) / cosig[h]
            pull_b = jnp.sum(g * pb, axis=0, keepdims=True) / sig[h]
            acc_gate[h : h + 1, :] += pull_b - pull_a
            acc_place[h] += pb * (g - pull_b)
            ds_s[h, 0:keys, :] = (pa * (g - pull_a)).astype(bf16)

        def bc(h):
            rows = slice(h * hw, (h + 1) * hw)
            dqkv_s[rows, cols] = (mm(qkvt_ref[b, d + h * hw : d + (h + 1) * hw, :], ds_s[h]) * scale).astype(bf16)
            dqkv_s[d + h * hw : d + (h + 1) * hw, cols] = (mm_nt(qkvt_ref[b, rows, :], ds_s[h]) * scale).astype(bf16)
            dqkv_s[2 * d + h * hw : 2 * d + (h + 1) * hw, cols] = mm_nt(dot_ref[b, rows, :], mix_s[h]).astype(bf16)

        for t in range(heads + 2):
            if t < heads:
                ba(t)
            if t >= 2:
                bc(t - 2)
            if 1 <= t <= heads:
                bb(t - 1)
        return 0

    lax.fori_loop(0, images, backward, 0)

    back = mm(wqk_ref[0], dqkv_s[0:d, :]) + mm(wqk_ref[1], dqkv_s[d : 2 * d, :]) + mm(wv_ref[...], dqkv_s[2 * d : 3 * d, :])
    acc_qk[...] += mm_nt(hid_s[...], dqkv_s[0 : 2 * d, :])
    for t, tile in enumerate(tiles):
        b, lane = place_of(t)
        grad = back[:, tile]
        normal = xh_s[:, tile]
        acc_vec[0] += grad * normal
        acc_vec[1] += grad
        pulled = norm_back(grad, vec_s[0], normal, rstd_s[0:1, tile])
        tg_s[:, tile] = (mg_ref[b, :, lane].astype(f32) + pulled).astype(bf16)
    acc_v[...] += mm_nt(dqkv_s[2 * d : 3 * d, :], hid_s[...])
    for b in range(images):
        tgrad_ref[b] = mm_nt(eye[0:slots, :], tg_s[:, b * PITCH : (b + 1) * PITCH]).astype(bf16)

    @pl.when(step == count - 1)
    def _():
        sum_ref[...] = gsmall_ref[...]
        for f in range(fsdp):
            for r in range(2):
                sum_ref[f, r : r + 1, 0:w] = lane_sums(acc_vec[r, w * f : w * (f + 1), :])
        at = 6 + ff // d
        dc, dr, far = offset_planes(keys)
        rows = [[], [], []]
        for h in range(heads):
            pg = acc_place[h]
            for c, off in enumerate((dc, dr, far)):
                rows[c].append(jnp.sum(pg * off, axis=0, keepdims=True))
            acc_gate[h : h + 1, :] = acc_gate[h : h + 1, :] * (sig[h] * cosig[h])
        sum_ref[0, at + 3 : at + 4, 0 : acc_gate.shape[0]] = lane_sums(acc_gate[...])
        for c in range(3):
            for h in range(heads):
                acc_gate[h : h + 1, :] = rows[c][h]
            sum_ref[0, at + c : at + c + 1, 0 : acc_gate.shape[0]] = lane_sums(acc_gate[...])

        cat_s[...] = jnp.zeros_like(cat_s)
        acc_qk[...] = mm(acc_qk[...].astype(bf16), perm[...])
        for k in range(dp):
            cat_s[0:u, :] = mm_nt(acc_v[u * k : u * (k + 1), :].astype(bf16), pick[...])
            cat_s[u : 2 * u, :] = mm_nt(acc_qk[u * k : u * (k + 1), 0:d].astype(bf16), pick[...])
            cat_s[2 * u : 3 * u, :] = mm_nt(acc_qk[u * k : u * (k + 1), d : 2 * d].astype(bf16), pick[...])
            for f in range(fsdp):
                last_s[k, f] = cat_s[:, 128 * f : 128 * (f + 1)].astype(bf16)
        last.begin()

        def small_round(base, coordinate, size, targets):
            return exchange(here, sum_ref, small_buf, sm_send, sm_recv, base, coordinate, size, targets)

        pending = small_round(0, here.c, cores, [here.to(dc=k) for k in range(1, cores)])
        total = first.total()
        grad_ref[0:split, :] = total
        squares = jnp.sum((total * total).reshape(split // 8, 8, 128), axis=0)
        for t in range(zs + 2):
            last.turn(t)
            if t == 0:
                pending()
                pending = small_round(cores, here.x, xs, [here.to(dx=b) for b in range(1, xs)])
            if t == 1:
                pending()
                pending = small_round(cores + xs, here.y, ys, [here.to(dy=a) for a in range(1, ys)])
            if t == 2:
                pending()
                pending = small_round(cores + xs + ys, here.z, zs, [here.to(dz=q) for q in range(1, zs)])
        pending()
        total = last.total()
        grad_ref[split:rows_all, :] = total
        norm_ref[...] = squares + jnp.sum((total * total).reshape((rows_all - split) // 8, 8, 128), axis=0)
        everyone = [here.to(dy=a, dx=b) for a in range(ys) for b in range(xs) if a or b]
        exchange(here, norm_ref, norm_buf, nm_send, nm_recv, 0, here.to()[1], fsdp, everyone)()
        everyone = [here.to(dz=k, dc=c) for k in range(zs) for c in range(cores) if k or c]
        exchange(here, norm_ref, norm_buf, nm_send, nm_recv, fsdp, here.to()[0], dp, everyone)()
        first.finish()
        last.finish()


def run_backward(dp, fsdp, slots, kept, small, small_part, wqk, wv, first_part, locality, ff, images):
    b, d, _ = kept[0].shape
    heads = locality.shape[1]
    keys = kept[2].shape[2]
    n = images * PITCH
    _, split, rows = row_plan(ff // dp, d // dp)
    more = rows - split
    cores = 2 if dp % 2 == 0 else 1
    zs = dp // cores
    ys = max(v for v in range(1, fsdp + 1) if fsdp % v == 0 and v * v <= fsdp)
    xs = fsdp // ys
    copies = len(reducer_keys(zs, ys, xs, cores))
    rounds = cores + xs + ys + zs

    def whole(shape):
        return pl.BlockSpec(shape, lambda g: (0,) * len(shape), pipeline_mode=pl.Buffered(1))

    def per(shape):
        mode = pl.Buffered(1) if fsdp > 4 and shape[-1] == PITCH else None
        return pl.BlockSpec((images,) + shape, lambda g: (g,) + (0,) * len(shape), pipeline_mode=mode)

    scratch = [
        pltpu.VMEM((PITCH, PITCH), bf16),
        pltpu.VMEM((fsdp * 128, d), bf16),
        pltpu.VMEM((2 * d, 2 * d), bf16),
        pltpu.VMEM((more, fsdp * 128), f32),
        pltpu.VMEM((2, d, 128), f32),
        pltpu.VMEM((d, 2 * d), f32),
        pltpu.VMEM((d, d), f32),
        pltpu.VMEM((2, d, 128), f32),
        pltpu.VMEM((heads, keys, PITCH), f32),
        pltpu.VMEM((-(-heads // 8) * 8, PITCH), f32),
        pltpu.VMEM((d, n), bf16),
        pltpu.VMEM((d, n), f32),
        pltpu.VMEM((8, n), f32),
        pltpu.VMEM((keys, d), bf16),
        pltpu.VMEM((heads, PITCH, PITCH), bf16),
        pltpu.VMEM((2, keys, PITCH), f32),
        pltpu.VMEM((heads, PITCH, PITCH), bf16),
        pltpu.VMEM((heads, PITCH, PITCH), bf16),
        pltpu.VMEM((3 * d, n), bf16),
        pltpu.VMEM((d, n), bf16),
        pltpu.VMEM((dp, fsdp, more, 128), bf16),
        pltpu.VMEM((zs, fsdp, split, 128), bf16),
        pltpu.VMEM((zs, fsdp, split, 128), bf16),
        *reducer_buffers(zs, ys, xs, split),
        pltpu.VMEM((zs, fsdp, more, 128), bf16),
        *reducer_buffers(zs, ys, xs, more),
        pltpu.VMEM((rounds,) + small.shape, f32),
        pltpu.VMEM((fsdp + dp, 8, 128), f32),
        pltpu.SemaphoreType.DMA((zs,)),
        pltpu.SemaphoreType.DMA((copies,)),
        pltpu.SemaphoreType.DMA((copies,)),
        pltpu.SemaphoreType.DMA((copies,)),
        pltpu.SemaphoreType.DMA((copies,)),
        pltpu.SemaphoreType.DMA((rounds,)),
        pltpu.SemaphoreType.DMA((rounds,)),
        pltpu.SemaphoreType.DMA((fsdp + dp,)),
        pltpu.SemaphoreType.DMA((fsdp + dp,)),
    ]
    return pl.pallas_call(
        partial(backward_kernel, images, slots, heads, dp, fsdp, ff, b // images),
        grid=(b // images,),
        out_shape=[
            jax.ShapeDtypeStruct((b, slots, d), bf16),
            jax.ShapeDtypeStruct((rows, 128), f32),
            jax.ShapeDtypeStruct(small.shape, f32),
            jax.ShapeDtypeStruct((8, 128), f32),
        ],
        in_specs=[pl.BlockSpec(memory_space=pltpu.SMEM)]
        + [per(v.shape[1:]) for v in kept]
        + [whole(small.shape), whole(small.shape), whole((2, d, d)), whole((d, d)), pl.BlockSpec(memory_space=pl.ANY)],
        out_specs=[per((slots, d)), whole((rows, 128)), whole(small.shape), whole((8, 128))],
        scratch_shapes=scratch,
        compiler_params=pltpu.CompilerParams(
            dimension_semantics=("arbitrary",),
            collective_id=1,
            has_side_effects=True,
            vmem_limit_bytes=63 * 1024 * 1024,
        ),
        cost_estimate=pl.CostEstimate(flops=25_000_000_000, bytes_accessed=70_000_000, transcendentals=0),
    )(locality, *kept, small, small_part, wqk, wv, first_part)


def adamw(parameter, moment_one, moment_two, gradient, rate, decay_rate):
    first_new = beta_one * moment_one + (1.0 - beta_one) * gradient
    second_new = beta_two * moment_two + (1.0 - beta_two) * gradient * gradient
    first_hat = first_new / (1.0 - beta_one**STEP)
    second_hat = second_new / (1.0 - beta_two**STEP)
    new_value = parameter - rate * (
        first_hat / (jnp.sqrt(second_hat) + adam_eps) + decay_rate * parameter
    )
    return (new_value, first_new, second_new)


def update_kernel(heads, *refs):
    grad_ref, small_ref, norm_ref = refs[0:3]
    states = [refs[3 + 3 * k : 6 + 3 * k] for k in range(8)]
    outs = refs[27:]
    small = small_ref[...]
    norm = jnp.sqrt(jnp.sum(norm_ref[...], keepdims=True) + jnp.sum(small * small, keepdims=True)[0])
    factor = clip_limit / jnp.maximum(norm, clip_limit)
    outs[0][...] = norm
    u, w = states[1][0].shape
    fu = states[3][0].shape[0]
    o_at, split, _ = row_plan(fu, u)
    starts = {1: split, 2: o_at, 3: 0, 4: fu}

    def matrix(k, state, gradient, place):
        new_value, first_new, second_new = adamw(
            state[0][place], state[1][place], state[2][place], gradient * factor, learn_rate, weight_decay
        )
        outs[1 + 4 * k][place] = new_value
        outs[2 + 4 * k][place] = new_value.astype(bf16)
        outs[3 + 4 * k][place] = first_new
        outs[4 + 4 * k][place] = second_new

    at = split + u
    gradient = jnp.concatenate([grad_ref[at : at + u, 0:w], grad_ref[at + u : at + 2 * u, 0:w]], axis=1)
    matrix(0, states[0], gradient, ...)
    for k in (1, 2, 3, 4):
        rows = states[k][0].shape[0]
        matrix(k, states[k], grad_ref[starts[k] : starts[k] + rows, 0:w], ...)
    mine = small_ref[lax.axis_index("fsdp")]
    share = states[6][0].shape[0]
    gradients = (mine[0:6, 0:w], mine[6 : 6 + share, 0:w], small_ref[0, 6 + share : 10 + share, 0:heads])
    for k in range(3):
        state = states[5 + k]
        new_value, first_new, second_new = adamw(
            state[0][...], state[1][...], state[2][...], gradients[k] * factor, small_rate, 0.0
        )
        outs[21 + 3 * k][...] = new_value
        outs[22 + 3 * k][...] = first_new
        outs[23 + 3 * k][...] = second_new


def update(heads, grad, small, norm, states):
    shapes = [jax.ShapeDtypeStruct((1, 1), f32)]
    for k in range(5):
        shape = states[3 * k].shape
        shapes += [jax.ShapeDtypeStruct(shape, kind) for kind in (f32, bf16, f32, f32)]
    for k in range(5, 8):
        shapes += [jax.ShapeDtypeStruct(states[3 * k].shape, f32)] * 3
    return pl.pallas_call(
        partial(update_kernel, heads),
        out_shape=shapes,
        in_specs=[pl.BlockSpec(memory_space=pltpu.VMEM)] * 27,
        out_specs=[pl.BlockSpec(memory_space=pltpu.VMEM)] * len(shapes),
        compiler_params=pltpu.CompilerParams(vmem_limit_bytes=32 * 1024 * 1024),
    )(grad, small, norm, *states)


def body(
    dp,
    fsdp,
    tokens,
    keep_mask,
    cotangent,
    qk_weight,
    qk_first,
    qk_second,
    value_weight,
    value_first,
    value_second,
    out_weight,
    out_first,
    out_second,
    up_weight,
    up_first,
    up_second,
    down_weight,
    down_first,
    down_second,
    vectors,
    vectors_first,
    vectors_second,
    up_bias,
    up_bias_first,
    up_bias_second,
    locality,
    locality_first,
    locality_second,
):
    d = tokens.shape[-1]
    heads = locality.shape[1]
    ff = up_bias.shape[0] * fsdp
    rows = row_plan(ff // dp, d // dp)[2]
    images = 2 if fsdp <= 4 else 1
    everything, small, tokens, cotangent = gather_all(
        dp,
        fsdp,
        rows,
        qk_weight,
        value_weight.T,
        out_weight.T,
        up_weight.T,
        down_weight,
        vectors,
        up_bias,
        tokens,
        cotangent,
    )
    result, first_part, small_part, wqk, wv, kept = run_forward(
        tokens, keep_mask.astype(f32), cotangent, everything, small, locality, ff, images
    )
    token_grad, grad, small_sum, norm = run_backward(
        dp, fsdp, tokens.shape[1], kept, small, small_part, wqk, wv, first_part, locality, ff, images
    )

    def flat(v):
        return v.reshape(-1, vectors.shape[1])

    states = [qk_weight, qk_first, qk_second]
    states += [v.T for v in (value_weight, value_first, value_second, out_weight, out_first, out_second)]
    states += [v.T for v in (up_weight, up_first, up_second)]
    states += [down_weight, down_first, down_second, vectors, vectors_first, vectors_second]
    states += [flat(up_bias), flat(up_bias_first), flat(up_bias_second), locality, locality_first, locality_second]
    outs = list(update(heads, grad, small_sum, norm, states))
    for k in range(5, 17):
        outs[k] = outs[k].T
    for k in (24, 25, 26):
        outs[k] = outs[k].reshape(up_bias.shape)
    outs[0] = outs[0].reshape(())
    return (result, token_grad, *outs)


def solution(mesh):
    placed = (
        P(("dp", "fsdp"), None, None),
        P(("dp", "fsdp"), None),
        P(("dp", "fsdp"), None, None),
        P("dp", "fsdp"),
        P("dp", "fsdp"),
        P("dp", "fsdp"),
        P("fsdp", "dp"),
        P("fsdp", "dp"),
        P("fsdp", "dp"),
        P("fsdp", "dp"),
        P("fsdp", "dp"),
        P("fsdp", "dp"),
        P("fsdp", "dp"),
        P("fsdp", "dp"),
        P("fsdp", "dp"),
        P("dp", "fsdp"),
        P("dp", "fsdp"),
        P("dp", "fsdp"),
        P(None, "fsdp"),
        P(None, "fsdp"),
        P(None, "fsdp"),
        P("fsdp"),
        P("fsdp"),
        P("fsdp"),
        P(),
        P(),
        P(),
    )
    return jax.shard_map(
        partial(body, mesh.shape["dp"], mesh.shape["fsdp"]),
        mesh=mesh,
        in_specs=placed,
        out_specs=(
            P(("dp", "fsdp"), None, None),
            P(("dp", "fsdp"), None, None),
            P(),
            P("dp", "fsdp"),
            P("dp", "fsdp"),
            P("dp", "fsdp"),
            P("dp", "fsdp"),
            P("fsdp", "dp"),
            P("fsdp", "dp"),
            P("fsdp", "dp"),
            P("fsdp", "dp"),
            P("fsdp", "dp"),
            P("fsdp", "dp"),
            P("fsdp", "dp"),
            P("fsdp", "dp"),
            P("fsdp", "dp"),
            P("fsdp", "dp"),
            P("fsdp", "dp"),
            P("fsdp", "dp"),
            P("dp", "fsdp"),
            P("dp", "fsdp"),
            P("dp", "fsdp"),
            P("dp", "fsdp"),
            P(None, "fsdp"),
            P(None, "fsdp"),
            P(None, "fsdp"),
            P("fsdp"),
            P("fsdp"),
            P("fsdp"),
            P(),
            P(),
            P(),
        ),
        check_vma=False,
    )
```

```python
from functools import partial

import jax
import jax.numpy as jnp
from jax import lax
from jax.experimental import pallas as pl
from jax.experimental.pallas import tpu as pltpu
from jax.sharding import PartitionSpec as P

GRID = 14
STEP = 5
PITCH = 256

norm_eps = 1e-06
learn_rate = 0.03
small_rate = 0.3
beta_one = 0.5
beta_two = 0.5
adam_eps = 1e-08
weight_decay = 0.05
clip_limit = 1.0

LOG2E = 1.4426950408889634
PHI_ZERO = 0.3989422804014327

f32 = jnp.float32
bf16 = jnp.bfloat16


def mm(a, b):
    return lax.dot_general(a, b, (((1,), (0,)), ((), ())), preferred_element_type=f32)


def mm_nt(a, b):
    return lax.dot_general(a, b, (((1,), (1,)), ((), ())), preferred_element_type=f32)


def gelu_parts(u):
    v = u * 0.5**0.5
    cdf = 0.5 * lax.erf(v) + 0.5
    bell = jnp.exp2(v * v * -LOG2E)
    return u * cdf, cdf + (v * (PHI_ZERO * 2**0.5)) * bell


MESH = pl.DeviceIdType.MESH


def up16(v):
    return -(-v // 16) * 16


class Place:
    def __init__(self, dp, fsdp):
        self.cores = 2 if dp % 2 == 0 else 1
        self.zs = dp // self.cores
        self.ys = max(v for v in range(1, fsdp + 1) if fsdp % v == 0 and v * v <= fsdp)
        self.xs = fsdp // self.ys
        self.fs = fsdp
        at_dp, at_f = lax.axis_index("dp"), lax.axis_index("fsdp")
        self.z, self.c = at_dp // self.cores, at_dp % self.cores
        self.y, self.x = at_f // self.xs, at_f % self.xs

    def to(self, dz=0, dc=0, dy=0, dx=0):
        z = lax.rem(self.z + dz, self.zs)
        c = lax.rem(self.c + dc, self.cores)
        y = lax.rem(self.y + dy, self.ys)
        x = lax.rem(self.x + dx, self.xs)
        return (z * self.cores + c, y * self.xs + x)


def greet(peers):
    barrier = pltpu.get_barrier_semaphore()
    for peer in peers:
        pl.semaphore_signal(barrier, inc=1, device_id=peer, device_id_type=MESH)
    pl.semaphore_wait(barrier, len(peers))


def row_plan(fu, u):
    o_at = up16(2 * fu)
    split = up16(o_at + u)
    return o_at, split, split + up16(3 * u)


class Gatherer:
    def __init__(self, here, rows, block, slots, send, recv):
        self.here, self.block, self.slots, self.send, self.recv = here, block, slots, send, recv
        half = rows // 32 * 16
        self.segs = (pl.ds(0, half), pl.ds(half, rows - half))
        self.keys = gatherer_keys(here.zs, here.ys, here.xs, here.cores)
        self.order = [0] + z_order(here.zs)[:-1]

    def slot(self, owner, seg):
        return self.slots.at[owner[0], owner[1], self.segs[seg]]

    def copy(self, key):
        here, kind, k, a, b, seg, to = self.here, *key
        owner = here.to(dz=k, dy=a, dx=b)
        own = (k, a, b) == (0, 0, 0)
        target = {"z": here.to(dz=to), "y": here.to(dy=to), "x": here.to(dx=to), "c": here.to(dc=to)}[kind]
        return pltpu.make_async_remote_copy(
            src_ref=self.block.at[self.segs[seg]] if own else self.slot(owner, seg),
            dst_ref=self.slot(owner, seg),
            send_sem=self.send.at[self.keys.index(key)],
            recv_sem=self.recv.at[owner[0] * here.fs + owner[1], seg],
            device_id=target,
            device_id_type=MESH,
        )

    def push(self, kind, k, a, b, seg):
        for key in self.keys:
            if key[:5] == (kind, k, a, b, seg):
                self.copy(key).start()

    def arrive(self, k, a, b, seg, dc=0):
        owner = self.here.to(dz=k, dy=a, dx=b, dc=dc)
        slot = self.slot(owner, seg)
        pltpu.make_async_remote_copy(
            src_ref=slot,
            dst_ref=slot,
            send_sem=self.send.at[0],
            recv_sem=self.recv.at[owner[0] * self.here.fs + owner[1], seg],
            device_id=self.here.to(),
            device_id_type=MESH,
        ).wait_recv()

    def spread(self, k):
        for kind in "yxc":
            for seg in (0, 1):
                self.push(kind, k, 0, 0, seg)

    def relay(self, k):
        here = self.here
        for a in range(1, here.ys):
            self.arrive(k, a, 0, 0)
            self.push("x", k, a, 0, 0)
        for b in range(1, here.xs):
            self.arrive(k, 0, b, 1)
            self.push("y", k, 0, b, 1)
        for a in range(1, here.ys):
            self.arrive(k, a, 0, 1)
            for seg in (0, 1):
                self.push("c", k, a, 0, seg)
        for b in range(1, here.xs):
            self.arrive(k, 0, b, 0)
            for seg in (0, 1):
                self.push("c", k, 0, b, seg)

    def corner(self, k):
        for a in range(1, self.here.ys):
            for b in range(1, self.here.xs):
                for seg in (0, 1):
                    self.arrive(k, a, b, seg)
                    self.push("c", k, a, b, seg)

    def twin(self, k):
        here = self.here
        for c in range(1, here.cores):
            for a in range(here.ys):
                for b in range(here.xs):
                    for seg in (0, 1):
                        self.arrive(k, a, b, seg, c)

    def events(self):
        return self.here.zs + 3

    def event(self, t):
        zs = self.here.zs
        if t == 0:
            for seg in (0, 1):
                self.push("z", 0, 0, 0, seg)
            self.spread(0)
        elif t < zs:
            for seg in (0, 1):
                self.arrive(self.order[t], 0, 0, seg)
            self.spread(self.order[t])
            self.relay(self.order[t - 1])
        elif t == zs:
            self.relay(self.order[zs - 1])
            for k in self.order[: zs // 2]:
                self.corner(k)
        elif t == zs + 1:
            for k in self.order[zs // 2 :]:
                self.corner(k)
        else:
            for k in self.order:
                self.twin(k)

    def finish(self):
        for key in self.keys:
            self.copy(key).wait_send()


def gatherer_keys(zs, ys, xs, cores):
    keys = [("z", 0, 0, 0, seg, k) for seg in (0, 1) for k in range(1, zs)]
    for k in range(zs):
        for seg in (0, 1):
            keys += [("y", k, 0, 0, seg, a) for a in range(1, ys)]
            keys += [("x", k, 0, 0, seg, b) for b in range(1, xs)]
        keys += [("x", k, a, 0, 0, b) for a in range(1, ys) for b in range(1, xs)]
        keys += [("y", k, 0, b, 1, a) for a in range(1, ys) for b in range(1, xs)]
        keys += [("c", k, a, b, seg, c) for a in range(ys) for b in range(xs) for seg in (0, 1) for c in range(1, cores)]
    return keys


def gather_kernel(dp, fsdp, rows, qk_ref, vt_ref, ot_ref, vec_ref, upb_ref, tok_ref, cot_ref, all_ref, small_ref, tok_out, cot_out, wide, block, part, slab, rows_s, turned_s, in_qk, in_vt, in_ot, in_vec, in_upb, in_sem, send, recv, small_send, small_recv, local, turn_sem):
    here = Place(dp, fsdp)
    zs, ys, xs, cores = here.zs, here.ys, here.xs, here.cores
    u, w = vt_ref.shape
    me = here.to()
    peers = [here.to(dz=k) for k in range(1, zs)] + [here.to(dc=k) for k in range(1, cores)]
    peers += [here.to(dy=a, dx=b) for a in range(ys) for b in range(xs) if a or b]

    loads = []
    for ref, into in ((qk_ref, in_qk), (vt_ref, in_vt), (ot_ref, in_ot), (vec_ref, in_vec), (upb_ref, in_upb)):
        loads.append(pltpu.make_async_copy(ref, into, in_sem.at[len(loads)]))
        loads[-1].start()
    slots, images, d = tok_ref.shape
    spans = [(lo, min(lo + 128, d)) for lo in range(0, d, 128)]
    arrivals = [pltpu.make_async_copy(ref, slab.at[n], turn_sem.at[n]) for n, ref in enumerate((tok_ref, cot_ref))]
    for copy in arrivals:
        copy.start()

    def widen_all(n):
        arrivals[n].wait()

        def widen(k, _):
            for c, (lo, hi) in enumerate(spans):
                rows_s[c, pl.ds(pl.multiple_of(k * images, 8), images), 0 : hi - lo] = slab[n, k, :, lo:hi].astype(f32)
            return 0

        lax.fori_loop(0, slots, widen, 0, unroll=4)

    def pick_all(n, out, first, count):
        def pick(k, _):
            for c, (lo, hi) in enumerate(spans):
                turned_s[n, k, :, lo:hi] = rows_s[c, pl.ds(k, slots, stride=images), :][:, 0 : hi - lo].astype(bf16)
            return 0

        lax.fori_loop(first, first + count, pick, 0)
        copy = pltpu.make_async_copy(turned_s.at[n, pl.ds(first, count)], out.at[pl.ds(first, count)], turn_sem.at[n])
        copy.start()
        return copy

    wide[...] = jnp.zeros_like(wide)
    part[...] = jnp.zeros_like(part)
    for copy in loads:
        copy.wait()
    wide[0:u, 0:w] = in_ot[...]
    wide[u : 2 * u, 0:w] = in_vt[...]
    for k in range(in_qk.shape[1] // w):
        wide[(k + 2) * u : (k + 3) * u, 0:w] = in_qk[:, k * w : (k + 1) * w]
    block[...] = wide[...].astype(bf16)
    part[0:6, 0:w] = in_vec[...]
    for r in range(in_upb.shape[1] // w):
        part[6 + r : 7 + r, 0:w] = in_upb[:, r * w : (r + 1) * w]

    greet(peers)
    gatherer = Gatherer(here, rows, block, all_ref, send, recv)
    gatherer.event(0)
    own_copy = pltpu.make_async_copy(block, all_ref.at[me[0], me[1]], local.at[0])
    own_copy.start()
    small_copy = pltpu.make_async_copy(part, small_ref.at[me[1]], local.at[1])
    small_copy.start()
    smalls = []
    for a in range(ys):
        for b in range(xs):
            if a or b:
                n = len(smalls)
                copy = pltpu.make_async_remote_copy(
                    src_ref=part,
                    dst_ref=small_ref.at[me[1]],
                    send_sem=small_send.at[n],
                    recv_sem=small_recv.at[me[1]],
                    device_id=here.to(dy=a, dx=b),
                    device_id_type=MESH,
                )
                copy.start()
                smalls.append(copy)
    turns = []
    jobs = [
        lambda: widen_all(0),
        lambda: turns.append(pick_all(0, tok_out, 0, images)),
        lambda: widen_all(1),
        lambda: turns.append(pick_all(1, cot_out, 0, images)),
    ]
    for t in range(1, gatherer.events()):
        if jobs:
            jobs.pop(0)()
        gatherer.event(t)
    for job in jobs:
        job()
    for a in range(ys):
        for b in range(xs):
            if a or b:
                peer = here.to(dy=a, dx=b)
                pltpu.make_async_remote_copy(
                    src_ref=part,
                    dst_ref=small_ref.at[peer[1]],
                    send_sem=small_send.at[0],
                    recv_sem=small_recv.at[peer[1]],
                    device_id=me,
                    device_id_type=MESH,
                ).wait_recv()
    gatherer.finish()
    for copy in smalls:
        copy.wait_send()
    own_copy.wait()
    small_copy.wait()
    for copy in turns:
        copy.wait()


def shape_of(dp, fsdp):
    cores = 2 if dp % 2 == 0 else 1
    ys = max(v for v in range(1, fsdp + 1) if fsdp % v == 0 and v * v <= fsdp)
    return dp // cores, ys, fsdp // ys, cores


def gather_all(dp, fsdp, rows, qk, vt, ot, vectors, up_bias, tokens, cotangent):
    images, slots, d = tokens.shape
    flat_bias = up_bias.reshape(1, -1)
    shards = (qk, vt, ot, vectors, flat_bias)
    return pl.pallas_call(
        partial(gather_kernel, dp, fsdp, rows),
        out_shape=[
            jax.ShapeDtypeStruct((dp, fsdp, rows, 128), bf16),
            jax.ShapeDtypeStruct((fsdp, 16, 128), f32),
            jax.ShapeDtypeStruct((images, slots, d), bf16),
            jax.ShapeDtypeStruct((images, slots, d), bf16),
        ],
        in_specs=[pl.BlockSpec(memory_space=pl.ANY)] * 7,
        out_specs=[pl.BlockSpec(memory_space=pl.ANY)] * 4,
        scratch_shapes=[
            pltpu.VMEM((rows, 128), f32),
            pltpu.VMEM((rows, 128), bf16),
            pltpu.VMEM((16, 128), f32),
            pltpu.VMEM((2, slots, images, d), bf16),
            pltpu.VMEM((-(-d // 128), slots * images, 128), f32),
            pltpu.VMEM((2, images, slots, d), bf16),
            *[pltpu.VMEM(v.shape, f32) for v in shards],
            pltpu.SemaphoreType.DMA((len(shards),)),
            pltpu.SemaphoreType.DMA((len(gatherer_keys(*shape_of(dp, fsdp))),)),
            pltpu.SemaphoreType.DMA((dp * fsdp, 2)),
            pltpu.SemaphoreType.DMA((fsdp,)),
            pltpu.SemaphoreType.DMA((fsdp,)),
            pltpu.SemaphoreType.DMA((2,)),
            pltpu.SemaphoreType.DMA((2,)),
        ],
        compiler_params=pltpu.CompilerParams(collective_id=0, has_side_effects=True, vmem_limit_bytes=62 * 1024 * 1024),
    )(*shards, tokens.transpose(1, 0, 2), cotangent.transpose(1, 0, 2))


def identity():
    rows = lax.broadcasted_iota(jnp.int32, (PITCH, PITCH), 0)
    cols = lax.broadcasted_iota(jnp.int32, (PITCH, PITCH), 1)
    return jnp.where(rows == cols, 1.0, 0.0).astype(bf16)


def one_hot(shape, w, goal):
    r = lax.broadcasted_iota(jnp.int32, shape, 0)
    c = lax.broadcasted_iota(jnp.int32, shape, 1)
    block, lane = r // 128, r % 128
    return jnp.where((c == goal(block, lane)) & (lane < w), 1.0, 0.0).astype(bf16)


def offset_planes(keys):
    j = lax.broadcasted_iota(jnp.int32, (keys, PITCH), 0)
    i = lax.broadcasted_iota(jnp.int32, (keys, PITCH), 1)
    rj, ri = j // GRID, i // GRID
    dc = ((j - rj * GRID) - (i - ri * GRID)).astype(f32)
    dr = (rj - ri).astype(f32)
    return dc, dr, dc * dc + dr * dr


def gates(locality_ref, heads):
    sig, cosig = [], []
    for h in range(heads):
        s = 1.0 / (1.0 + jnp.exp(-jnp.full((1, PITCH), locality_ref[3, h], f32)))
        sig.append(s)
        cosig.append(1.0 - s)
    return sig, cosig


def windows(heads, hw, d):
    wins = []
    for h in range(heads):
        lo = (h * hw) // 128 * 128
        wins.append((lo, min(lo + PITCH, d), h * hw - lo))
    return wins


def lane_sums(v):
    return lax.dot_general(
        jnp.ones((8, v.shape[1]), f32),
        v,
        (((1,), (1,)), ((), ())),
        preferred_element_type=f32,
        precision=lax.Precision.HIGHEST,
    )[0:1]


def column(row):
    return jnp.broadcast_to(row, (128, 128)).T


def norm_stats(x):
    d = x.shape[0]
    mean = jnp.sum(x, axis=0, keepdims=True) * (1.0 / d)
    center = x - mean
    rstd = lax.rsqrt(jnp.sum(center * center, axis=0, keepdims=True) * (1.0 / d) + norm_eps)
    return center * rstd, rstd


def norm_back(grad, gain, normal, rstd):
    d = grad.shape[0]
    pull = grad * gain
    m1 = jnp.sum(pull, axis=0, keepdims=True) * (1.0 / d)
    m2 = jnp.sum(pull * normal, axis=0, keepdims=True) * (1.0 / d)
    return rstd * (pull - m1 - normal * m2)


def turn_in(ref, b, eye, pad_in, out):
    _, slots, d = ref.shape
    pad_in[0:slots, 0:d] = ref[b]
    for lo in range(0, d, PITCH):
        hi = min(lo + PITCH, d)
        out[lo:hi, :] = mm_nt(eye[0 : hi - lo, 0 : hi - lo], pad_in[:, lo:hi]).astype(bf16)


def turned(eye, ref, out_ref, row=0):
    for lo in range(0, ref.shape[1], PITCH):
        hi = min(lo + PITCH, ref.shape[1])
        out_ref[row + lo : row + hi, :] = mm_nt(eye[0 : hi - lo, 0 : hi - lo], ref[:, lo:hi]).astype(bf16)


def attend_kernel(
    images,
    slots,
    heads,
    dp,
    fsdp,
    total_steps,
    locality_ref,
    tok_ref,
    vis_ref,
    all_ref,
    small_ref,
    upt_ref,
    dn_ref,
    xt_ref,
    qkvt_ref,
    pa_ref,
    pb_ref,
    mixture_ref,
    wqk_ref,
    wv_ref,
    feed_ref,
    eye,
    pick,
    spread_a,
    spread_b,
    cat_s,
    chunk_s,
    stage_s,
    whole_s,
    wide,
    block,
    wqkvt_s,
    vec_s,
    pad_in,
    placed,
    hid_s,
    kn_s,
    win_s,
    sc_s,
    mix_s,
    chunk_sem,
    own_sem,
    send,
    recv,
):
    d = tok_ref.shape[-1]
    u, w = d // dp, d // fsdp
    fu = upt_ref.shape[0]
    rows_all = all_ref.shape[2]
    hw = d // heads
    keys = placed.shape[1]
    n = images * PITCH
    scale = hw**-0.5
    step = pl.program_id(0)
    here = Place(dp, fsdp)
    zs, ys, xs, cores = here.zs, here.ys, here.xs, here.cores
    me = here.to()
    gatherer = Gatherer(here, block.shape[0], block, feed_ref, send, recv)
    own_copy = pltpu.make_async_copy(block, feed_ref.at[me[0], me[1]], own_sem.at[0])

    @pl.when(step == 0)
    def _():
        def fetch(k):
            return pltpu.make_async_copy(all_ref.at[k], chunk_s.at[k % 2], chunk_sem.at[k % 2])

        fetch(0).start()
        wide[...] = jnp.zeros_like(wide)
        wide[0:fu, 0:w] = upt_ref[...]
        wide[fu : 2 * fu, 0:w] = dn_ref[...]
        block[...] = wide[...].astype(bf16)
        peers = [here.to(dz=k) for k in range(1, zs)] + [here.to(dc=k) for k in range(1, cores)]
        peers += [here.to(dy=k) for k in range(1, ys)] + [here.to(dx=k) for k in range(1, xs)]
        greet(peers)
        gatherer.event(0)
        own_copy.start()

        eye[...] = identity()
        pad_in[...] = jnp.zeros_like(pad_in)
        dc, dr, far = offset_planes(keys)
        for h in range(heads):
            placed[h] = (locality_ref[0, h] * dc + locality_ref[1, h] * dr + locality_ref[2, h] * far) * LOG2E
        pick[...] = one_hot(pick.shape, w, lambda block, lane: block * w + lane)
        goal = lax.broadcasted_iota(jnp.int32, (d, 1), 0)
        goal = goal // w * (2 * w) + goal % w
        lane = lax.broadcasted_iota(jnp.int32, spread_a.shape, 1)
        spread_a[...] = jnp.where(lane == goal, 1.0, 0.0).astype(bf16)
        spread_b[...] = jnp.where(lane == goal + w, 1.0, 0.0).astype(bf16)

        def unpack(k, _):
            fetch(k).wait()

            @pl.when(k + 1 < dp)
            def _():
                fetch(k + 1).start()

            for f in range(fsdp):
                cat_s[:, 128 * f : 128 * (f + 1)] = chunk_s[k % 2, f].astype(f32)
            for p in range(3):
                stage_s[p, k, 0:u, :] = mm(cat_s[(p + 1) * u : (p + 2) * u, :].astype(bf16), pick[...])
            return 0

        lax.fori_loop(0, dp, unpack, 0)
        for p in range(3):
            for k in range(dp):
                whole_s[p, u * k : u * (k + 1), :] = stage_s[p, k, 0:u, :]
        wqkvt_s[2 * d : 3 * d, :] = whole_s[0].astype(bf16)
        turned(eye, wqkvt_s.at[2 * d : 3 * d], wv_ref)
        joint = mm(whole_s[1].astype(bf16), spread_a[...]) + mm(whole_s[2].astype(bf16), spread_b[...])
        wqk_ref[0] = joint[:, 0:d].astype(bf16)
        wqk_ref[1] = joint[:, d : 2 * d].astype(bf16)
        turned(eye, wqk_ref.at[0], wqkvt_s)
        turned(eye, wqk_ref.at[1], wqkvt_s, d)
        for f in range(fsdp):
            for r in range(2):
                vec_s[r, w * f : w * (f + 1), :] = column(small_ref[f, r : r + 1, :])[0:w]
        for ref in (win_s, mix_s):
            ref[...] = jnp.zeros_like(ref)

    for t in range(1, gatherer.events()):

        @pl.when(step == min(t, total_steps - 1))
        def _(t=t):
            gatherer.event(t)

    def enter(b, _):
        turn_in(tok_ref, b, eye, pad_in, xt_ref.at[b])
        return 0

    lax.fori_loop(0, images, enter, 0)

    for t in range(n // 128):
        at = 128 * t
        normal, _ = norm_stats(xt_ref[at // PITCH, :, at % PITCH : at % PITCH + 128].astype(f32))
        hid_s[:, at : at + 128] = (normal * vec_s[0] + vec_s[1]).astype(bf16)
    joint = mm(wqkvt_s[...], hid_s[...]).astype(bf16)
    for b in range(images):
        qkvt_ref[b] = joint[:, PITCH * b : PITCH * (b + 1)]

    sig, cosig = gates(locality_ref, heads)
    wins = windows(heads, hw, d)

    def forward(b, _):
        kn_s[...] = mm_nt(eye[0:keys, :], qkvt_ref[b, d : 2 * d, :]).astype(bf16)
        key_vis = mm_nt(eye[0:keys, :], jnp.broadcast_to(vis_ref[b, 0:1, :], (PITCH, PITCH)).astype(bf16))
        bias = jnp.where(key_vis > 0.5, 0.0, -1e30)

        def fa(h):
            lo, hi, at = wins[h]
            win_s[h, at : at + hw, :] = qkvt_ref[b, h * hw : (h + 1) * hw, :]
            sc_s[h % 2] = mm(kn_s[:, lo:hi], win_s[h, 0 : hi - lo, :])

        def fb(h):
            scores = sc_s[h % 2] * (scale * LOG2E) + bias
            p = jnp.exp2(scores - jnp.max(scores, axis=0, keepdims=True))
            pa = p * (cosig[h] / jnp.sum(p, axis=0, keepdims=True))
            z = placed[h] + bias
            e = jnp.exp2(z - jnp.max(z, axis=0, keepdims=True))
            pb = e * (sig[h] / jnp.sum(e, axis=0, keepdims=True))
            pa_ref[b, h] = pa.astype(bf16)
            pb_ref[b, h] = pb.astype(bf16)
            mix_s[h, 0:keys, :] = (pa + pb).astype(bf16)

        def fc(h):
            mixture_ref[b, h * hw : (h + 1) * hw, :] = mm(
                qkvt_ref[b, 2 * d + h * hw : 2 * d + (h + 1) * hw, :], mix_s[h]
            ).astype(bf16)

        for t in range(heads + 2):
            if t < heads:
                fa(t)
            if t >= 2:
                fc(t - 2)
            if 1 <= t <= heads:
                fb(t - 1)
        return 0

    lax.fori_loop(0, images, forward, 0)

    @pl.when(step == total_steps - 1)
    def _():
        own_copy.wait()
        gatherer.finish()


def run_attend(dp, fsdp, tokens, vis, everything, small, upt, dn, locality, images):
    b, slots, d = tokens.shape
    heads = locality.shape[1]
    keys = up16(slots)
    n = images * PITCH
    u = d // dp
    rows = everything.shape[2]
    feed_rows = up16(2 * upt.shape[0])

    def whole(shape):
        return pl.BlockSpec(shape, lambda g: (0,) * len(shape), pipeline_mode=pl.Buffered(1))

    def per(shape):
        return pl.BlockSpec((images,) + shape, lambda g: (g,) + (0,) * len(shape))

    kept_shapes = [(d, PITCH), (3 * d, PITCH), (heads, keys, PITCH), (heads, keys, PITCH), (d, PITCH)]
    scratch = [
        ((PITCH, PITCH), bf16),
        ((fsdp * 128, d), bf16),
        ((d, 2 * d), bf16),
        ((d, 2 * d), bf16),
        ((rows, fsdp * 128), f32),
        ((2, fsdp, rows, 128), bf16),
        ((3, dp, up16(u), d), f32),
        ((3, d, d), f32),
        ((feed_rows, 128), f32),
        ((feed_rows, 128), bf16),
        ((3 * d, d), bf16),
        ((2, d, 128), f32),
        ((PITCH, d), bf16),
        ((heads, keys, PITCH), f32),
        ((d, n), bf16),
        ((keys, d), bf16),
        ((heads, PITCH, PITCH), bf16),
        ((2, keys, PITCH), f32),
        ((heads, PITCH, PITCH), bf16),
    ]
    outs = pl.pallas_call(
        partial(attend_kernel, images, slots, heads, dp, fsdp, b // images),
        grid=(b // images,),
        out_shape=[jax.ShapeDtypeStruct((b,) + shape, bf16) for shape in kept_shapes]
        + [
            jax.ShapeDtypeStruct((2, d, d), bf16),
            jax.ShapeDtypeStruct((d, d), bf16),
            jax.ShapeDtypeStruct((dp, fsdp, feed_rows, 128), bf16),
        ],
        in_specs=[
            pl.BlockSpec(memory_space=pltpu.SMEM),
            per((slots, d)),
            per((1, PITCH)),
            pl.BlockSpec(memory_space=pl.ANY),
            whole(small.shape),
            whole(upt.shape),
            whole(dn.shape),
        ],
        out_specs=[per(shape) for shape in kept_shapes]
        + [whole((2, d, d)), whole((d, d)), pl.BlockSpec(memory_space=pl.ANY)],
        scratch_shapes=[pltpu.VMEM(*entry) for entry in scratch]
        + [
            pltpu.SemaphoreType.DMA((2,)),
            pltpu.SemaphoreType.DMA((1,)),
            pltpu.SemaphoreType.DMA((len(gatherer_keys(*shape_of(dp, fsdp))),)),
            pltpu.SemaphoreType.DMA((dp * fsdp, 2)),
        ],
        compiler_params=pltpu.CompilerParams(
            dimension_semantics=("arbitrary",),
            collective_id=2,
            has_side_effects=True,
            vmem_limit_bytes=62 * 1024 * 1024,
        ),
        cost_estimate=pl.CostEstimate(flops=20_000_000_000, bytes_accessed=70_000_000, transcendentals=0),
    )(locality, tokens, vis, everything, small, upt, dn)
    return outs


def feed_kernel(
    images,
    slots,
    cot_ref,
    vis_ref,
    xt_ref,
    mixture_ref,
    all_ref,
    feed_ref,
    small_ref,
    res_ref,
    dot_ref,
    mg_ref,
    part_ref,
    gsmall_ref,
    eye,
    pick,
    cat_s,
    chunk_s,
    chunk_sem,
    o_s,
    wot_s,
    wo_s,
    wupt_s,
    wup_s,
    wdnt_s,
    wdn_s,
    vec_s,
    upb_s,
    pad_in,
    acc_out,
    acc_up,
    acc_down,
    acc_vec,
    acc_upb,
    mixture_s,
    xh2_s,
    rstd_s,
    second_s,
    mid_s,
    cot_s,
    dlow_s,
    up_s,
    back_s,
    act_s,
    ug_s,
    blow_s,
):
    d = cot_ref.shape[-1]
    ff = upb_s.shape[0]
    dp, fsdp, o_at, _ = feed_ref.shape
    u, w = d // dp, d // fsdp
    fu = ff // dp
    split = row_plan(fu, u)[1]
    few = o_s.shape[2]
    n = images * PITCH
    step = pl.program_id(0)

    @pl.when(step == 0)
    def _():
        def fetch(k):
            return pltpu.make_async_copy(feed_ref.at[k], chunk_s.at[k % 2], chunk_sem.at[k % 2])

        fetch(0).start()
        rest = pltpu.make_async_copy(all_ref.at[:, :, pl.ds(0, few)], o_s, chunk_sem.at[2])
        rest.start()
        eye[...] = identity()
        pad_in[...] = jnp.zeros_like(pad_in)
        pick[...] = one_hot(pick.shape, w, lambda block, lane: block * w + lane)

        def unpack(k, _):
            fetch(k).wait()

            @pl.when(k + 1 < dp)
            def _():
                fetch(k + 1).start()

            for f in range(fsdp):
                cat_s[:, 128 * f : 128 * (f + 1)] = chunk_s[k % 2, f].astype(f32)
            big = pl.ds(pl.multiple_of(fu * k, 8), fu) if fu % 8 == 0 else pl.ds(fu * k, fu)
            acc_up[big, :] = mm(cat_s[0:fu, :].astype(bf16), pick[...])
            acc_down[big, :] = mm(cat_s[fu : 2 * fu, :].astype(bf16), pick[...])
            return 0

        if fu % 8 == 0:
            lax.fori_loop(0, dp, unpack, 0)
        else:
            for k in range(dp):
                unpack(k, 0)
        wupt_s[...] = acc_up[...].astype(bf16)
        turned(eye, wupt_s, wup_s)
        wdn_s[...] = acc_down[...].astype(bf16)
        turned(eye, wdn_s, wdnt_s)
        rest.wait()
        for k in range(dp):
            for f in range(fsdp):
                cat_s[0:few, 128 * f : 128 * (f + 1)] = o_s[k, f].astype(f32)
            acc_out[u * k : u * (k + 1), :] = mm(cat_s[0:u, :].astype(bf16), pick[...])
        wot_s[...] = acc_out[...].astype(bf16)
        turned(eye, wot_s, wo_s)
        for f in range(fsdp):
            for r in range(2, 6):
                vec_s[r, w * f : w * (f + 1), :] = column(small_ref[f, r : r + 1, :])[0:w]
            for r in range(ff // d):
                at = (f * (ff // d) + r) * w
                upb_s[at : at + w, :] = column(small_ref[f, 6 + r : 7 + r, :])[0:w]
        for ref in (acc_out, acc_up, acc_down, acc_vec, acc_upb):
            ref[...] = jnp.zeros_like(ref)

    tiles = [slice(128 * k, 128 * (k + 1)) for k in range(n // 128)]

    def seen(t):
        at = 128 * t
        return vis_ref[at // PITCH, 0:1, at % PITCH : at % PITCH + 128]

    def fold(v):
        total = v[:, 0:128]
        for k in range(1, n // 128):
            total = total + v[:, 128 * k : 128 * (k + 1)]
        return total

    def enter(b, _):
        cols = pl.ds(pl.multiple_of(b * PITCH, PITCH), PITCH)
        turn_in(cot_ref, b, eye, pad_in, cot_s.at[:, cols])
        mixture_s[:, cols] = mixture_ref[b]
        return 0

    lax.fori_loop(0, images, enter, 0)

    def x_tile(t):
        at = 128 * t
        return xt_ref[at // PITCH, :, at % PITCH : at % PITCH + 128].astype(f32)

    for t, tile in enumerate(tiles):
        down = cot_s[:, tile].astype(f32) * seen(t)
        dlow_s[:, tile] = down.astype(bf16)
        acc_vec[3] += down
    mid_s[...] = mm(wot_s[...], mixture_s[...])
    for t, tile in enumerate(tiles):
        middle = x_tile(t) + seen(t) * (mid_s[:, tile] + vec_s[4])
        mid_s[:, tile] = middle
        normal, rstd = norm_stats(middle)
        xh2_s[:, tile] = normal
        rstd_s[0:1, tile] = rstd
        second_s[:, tile] = (normal * vec_s[2] + vec_s[3]).astype(bf16)

    chunk = up_s.shape[1]
    steps = ff // chunk

    def feed_start(c):
        part = slice(c * chunk, (c + 1) * chunk)
        up_s[c % 2] = mm(wupt_s[part, :], second_s[...])
        back_s[c % 2] = mm(wdn_s[part, :], dlow_s[...])

    feed_start(0)
    for c in range(steps):
        if c + 1 < steps:
            feed_start(c + 1)
        part = slice(c * chunk, (c + 1) * chunk)
        act, slope = gelu_parts(up_s[c % 2] + jnp.concatenate([upb_s[part, :]] * (n // 128), axis=1))
        act_s[part, :] = act.astype(bf16)
        ug = (back_s[c % 2] * slope).astype(bf16)
        ug_s[part, :] = ug
        acc_upb[part, :] += fold(ug.astype(f32))

    second_grad = mm(wup_s[...], ug_s[...])
    acc_up[...] += mm_nt(ug_s[...], second_s[...])
    for t, tile in enumerate(tiles):
        grad = second_grad[:, tile]
        normal = xh2_s[:, tile]
        acc_vec[0] += grad * normal
        acc_vec[1] += grad
        middle_grad = cot_s[:, tile].astype(f32) + norm_back(grad, vec_s[2], normal, rstd_s[0:1, tile])
        at = 128 * t
        mg_ref[at // PITCH, :, at % PITCH : at % PITCH + 128] = middle_grad.astype(bf16)
        low = (seen(t) * middle_grad).astype(bf16)
        blow_s[:, tile] = low
        acc_vec[2] += low.astype(f32)
    acc_down[...] += mm_nt(act_s[...], dlow_s[...])
    mixture_grad = mm(wo_s[...], blow_s[...]).astype(bf16)
    for b in range(images):
        dot_ref[b] = mixture_grad[:, PITCH * b : PITCH * (b + 1)]
    acc_out[...] += mm_nt(blow_s[...], mixture_s[...])
    downward = mm(wdnt_s[...], act_s[...])
    for t, tile in enumerate(tiles):
        dlow_s[:, tile] = (mid_s[:, tile] + seen(t) * (downward[:, tile] + vec_s[5])).astype(bf16)
    for b in range(images):
        res_ref[b] = mm_nt(eye[0:slots, :], dlow_s[:, b * PITCH : (b + 1) * PITCH]).astype(bf16)

    @pl.when(step == pl.num_programs(0) - 1)
    def _():
        def put_rest(k):
            return pltpu.make_async_copy(
                chunk_s.at[k % 2, :, pl.ds(0, split - o_at)],
                part_ref.at[k, :, pl.ds(o_at, split - o_at)],
                chunk_sem.at[k % 2],
            )

        cat_s[...] = jnp.zeros_like(cat_s)
        for k in range(dp):
            cat_s[0:u, :] = mm_nt(acc_out[u * k : u * (k + 1), :].astype(bf16), pick[...])
            if k >= 2:
                put_rest(k - 2).wait()
            for f in range(fsdp):
                chunk_s[k % 2, f, 0 : split - o_at] = cat_s[0 : split - o_at, 128 * f : 128 * (f + 1)].astype(bf16)
            put_rest(k).start()
        for k in range(max(dp - 2, 0), dp):
            put_rest(k).wait()
        if o_at > 2 * fu:
            cat_s[2 * fu : o_at, :] = jnp.zeros((o_at - 2 * fu, fsdp * 128), f32)

        def put(k):
            return pltpu.make_async_copy(chunk_s.at[k % 2], part_ref.at[k, :, pl.ds(0, o_at)], chunk_sem.at[k % 2])

        def pack(k, _):
            big = pl.ds(pl.multiple_of(fu * k, 8), fu) if fu % 8 == 0 else pl.ds(fu * k, fu)
            cat_s[0:fu, :] = mm_nt(acc_up[big, :].astype(bf16), pick[...])
            cat_s[fu : 2 * fu, :] = mm_nt(acc_down[big, :].astype(bf16), pick[...])

            @pl.when(k >= 2)
            def _():
                put(k - 2).wait()

            for f in range(fsdp):
                chunk_s[k % 2, f] = cat_s[0:o_at, 128 * f : 128 * (f + 1)].astype(bf16)
            put(k).start()
            return 0

        if fu % 8 == 0:
            lax.fori_loop(0, dp, pack, 0)
        else:
            for k in range(dp):
                pack(k, 0)
        for k in range(max(dp - 2, 0), dp):
            put(k).wait()

        gsmall_ref[...] = jnp.zeros_like(gsmall_ref)
        for f in range(fsdp):
            for r in range(4):
                gsmall_ref[f, 2 + r : 3 + r, 0:w] = lane_sums(acc_vec[r, w * f : w * (f + 1), :])
            for r in range(ff // d):
                lo = (f * (ff // d) + r) * w
                gsmall_ref[f, 6 + r : 7 + r, 0:w] = lane_sums(acc_upb[lo : lo + w, :])


def run_feed(dp, fsdp, cotangent, vis, xt, mixture, everything, feed, small, ff, images):
    b, slots, d = cotangent.shape
    n = images * PITCH
    o_at, split, _ = row_plan(ff // dp, d // dp)
    few = up16(d // dp)

    def whole(shape):
        return pl.BlockSpec(shape, lambda g: (0,) * len(shape), pipeline_mode=pl.Buffered(1))

    def per(shape):
        return pl.BlockSpec((images,) + shape, lambda g: (g,) + (0,) * len(shape))

    scratch = [
        ((PITCH, PITCH), bf16),
        ((fsdp * 128, d), bf16),
        ((o_at, fsdp * 128), f32),
        ((2, fsdp, o_at, 128), bf16),
        None,
        ((dp, fsdp, few, 128), bf16),
        ((d, d), bf16),
        ((d, d), bf16),
        ((ff, d), bf16),
        ((d, ff), bf16),
        ((d, ff), bf16),
        ((ff, d), bf16),
        ((6, d, 128), f32),
        ((ff, 128), f32),
        ((PITCH, d), bf16),
        ((d, d), f32),
        ((ff, d), f32),
        ((ff, d), f32),
        ((4, d, 128), f32),
        ((ff, 128), f32),
        ((d, n), bf16),
        ((d, n), f32),
        ((8, n), f32),
        ((d, n), bf16),
        ((d, n), f32),
        ((d, n), bf16),
        ((d, n), bf16),
        ((2, ff // 6, n), f32),
        ((2, ff // 6, n), f32),
        ((ff, n), bf16),
        ((ff, n), bf16),
        ((d, n), bf16),
    ]
    scratch = [pltpu.SemaphoreType.DMA((3,)) if entry is None else pltpu.VMEM(*entry) for entry in scratch]
    return pl.pallas_call(
        partial(feed_kernel, images, slots),
        grid=(b // images,),
        out_shape=[
            jax.ShapeDtypeStruct((b, slots, d), bf16),
            jax.ShapeDtypeStruct((b, d, PITCH), bf16),
            jax.ShapeDtypeStruct((b, d, PITCH), bf16),
            jax.ShapeDtypeStruct((dp, fsdp, split, 128), bf16),
            jax.ShapeDtypeStruct((fsdp, 16, 128), f32),
        ],
        in_specs=[per((slots, d)), per((1, PITCH)), per((d, PITCH)), per((d, PITCH))]
        + [pl.BlockSpec(memory_space=pl.ANY)] * 2
        + [whole((fsdp, 16, 128))],
        out_specs=[per((slots, d)), per((d, PITCH)), per((d, PITCH)), pl.BlockSpec(memory_space=pl.ANY), whole((fsdp, 16, 128))],
        scratch_shapes=scratch,
        compiler_params=pltpu.CompilerParams(
            dimension_semantics=("arbitrary",), vmem_limit_bytes=63 * 1024 * 1024
        ),
        cost_estimate=pl.CostEstimate(flops=40_000_000_000, bytes_accessed=40_000_000, transcendentals=0),
    )(cotangent, vis, xt, mixture, everything, feed, small)


class Reducer:
    def __init__(self, here, rows, mine, theirs, other, bufs, send, recv):
        self.here, self.mine, self.theirs, self.other = here, mine, theirs, other
        self.got_x, self.got_y, self.got_x2, self.got_y2, self.got_z = bufs
        self.send, self.recv = send, recv
        half = rows // 32 * 16
        self.segs = (pl.ds(0, half), pl.ds(half, rows - half))
        self.order = z_order(here.zs)
        self.keys = reducer_keys(here.zs, here.ys, here.xs, here.cores)

    def f_at(self, dy, dx):
        return self.here.to(dy=dy, dx=dx)[1]

    def copy(self, key):
        here, segs, n = self.here, self.segs, key[1]
        if key[0] == "pair":
            src, dst, target = self.theirs(n), self.other.at[n], here.to(dc=1)
        elif key[0] == "a1":
            _, _, a, b = key
            src, dst, target = self.mine(n).at[self.f_at(a, b), segs[0]], self.got_x.at[n, a, b - 1], here.to(dx=b)
        elif key[0] == "b1":
            _, _, a, b = key
            src, dst, target = self.mine(n).at[self.f_at(a, b), segs[1]], self.got_y.at[n, b, a - 1], here.to(dy=a)
        elif key[0] == "a2":
            src, dst, target = self.mine(n).at[self.f_at(key[2], 0), segs[0]], self.got_y2.at[n, key[2] - 1], here.to(dy=key[2])
        elif key[0] == "b2":
            src, dst, target = self.mine(n).at[self.f_at(0, key[2]), segs[1]], self.got_x2.at[n, key[2] - 1], here.to(dx=key[2])
        else:
            seg = segs[key[2]]
            src, dst, target = self.mine(n).at[self.f_at(0, 0), seg], self.got_z.at[n, seg], here.to(dz=self.order[n])
        at = self.keys.index(key)
        return pltpu.make_async_remote_copy(
            src_ref=src, dst_ref=dst, send_sem=self.send.at[at], recv_sem=self.recv.at[at], device_id=target, device_id_type=MESH
        )

    def add(self, n, f, seg, got):
        ref = self.mine(n)
        ref[f, self.segs[seg]] = (ref[f, self.segs[seg]].astype(f32) + got.astype(f32)).astype(bf16)

    def begin(self):
        if self.here.cores > 1:
            for n in range(self.here.zs):
                self.copy(("pair", n)).start()

    def stage_one(self, n):
        here = self.here
        if here.cores > 1:
            self.copy(("pair", n)).wait_recv()
            ref = self.mine(n)

            def body(f, _):
                ref[f] = (ref[f].astype(f32) + self.other[n, f].astype(f32)).astype(bf16)
                return 0

            lax.fori_loop(0, here.fs, body, 0)
        for a in list(range(1, here.ys)) + [0]:
            for b in range(1, here.xs):
                self.copy(("a1", n, a, b)).start()
        for b in list(range(1, here.xs)) + [0]:
            for a in range(1, here.ys):
                self.copy(("b1", n, a, b)).start()

    def stage_two(self, n):
        here = self.here
        for a in list(range(1, here.ys)) + [0]:
            for b in range(1, here.xs):
                self.copy(("a1", n, a, b)).wait_recv()
                self.add(n, self.f_at(a, 0), 0, self.got_x[n, a, b - 1])
            if a:
                self.copy(("a2", n, a)).start()
        for b in list(range(1, here.xs)) + [0]:
            for a in range(1, here.ys):
                self.copy(("b1", n, a, b)).wait_recv()
                self.add(n, self.f_at(0, b), 1, self.got_y[n, b, a - 1])
            if b:
                self.copy(("b2", n, b)).start()

    def stage_three(self, n):
        here = self.here
        for a in range(1, here.ys):
            self.copy(("a2", n, a)).wait_recv()
            self.add(n, self.f_at(0, 0), 0, self.got_y2[n, a - 1])
        for b in range(1, here.xs):
            self.copy(("b2", n, b)).wait_recv()
            self.add(n, self.f_at(0, 0), 1, self.got_x2[n, b - 1])
        if self.order[n]:
            for seg in (0, 1):
                self.copy(("z", n, seg)).start()

    def turn(self, t):
        zs = self.here.zs
        if t < zs:
            self.stage_one(t)
        if 1 <= t <= zs:
            self.stage_two(t - 1)
        if 2 <= t < zs + 2:
            self.stage_three(t - 2)

    def total(self):
        zs = self.here.zs
        total = self.mine(zs - 1)[self.f_at(0, 0)].astype(f32)
        for n in range(zs - 1):
            for seg in (0, 1):
                self.copy(("z", n, seg)).wait_recv()
            total = total + self.got_z[n].astype(f32)
        return total

    def finish(self):
        for key in self.keys:
            self.copy(key).wait_send()


def z_order(zs):
    return sorted(range(1, zs), key=lambda k: min(k, zs - k)) + [0]


def reducer_keys(zs, ys, xs, cores):
    keys = []
    for n in range(zs):
        if cores > 1:
            keys.append(("pair", n))
        keys += [("a1", n, a, b) for a in range(ys) for b in range(1, xs)]
        keys += [("b1", n, a, b) for a in range(1, ys) for b in range(xs)]
        keys += [("a2", n, a) for a in range(1, ys)] + [("b2", n, b) for b in range(1, xs)]
        if n < zs - 1:
            keys += [("z", n, 0), ("z", n, 1)]
    return keys


def reducer_buffers(zs, ys, xs, rows):
    half = rows // 32 * 16
    rest = rows - half
    return [
        pltpu.VMEM((zs, ys, max(xs - 1, 1), half, 128), bf16),
        pltpu.VMEM((zs, xs, max(ys - 1, 1), rest, 128), bf16),
        pltpu.VMEM((zs, max(xs - 1, 1), rest, 128), bf16),
        pltpu.VMEM((zs, max(ys - 1, 1), half, 128), bf16),
        pltpu.VMEM((zs, rows, 128), bf16),
    ]


def exchange(here, ref, buf, send, recv, base, coordinate, size, targets):
    buf[base + coordinate] = ref[...]
    for k, target in enumerate(targets):
        pltpu.make_async_remote_copy(
            src_ref=ref,
            dst_ref=buf.at[base + coordinate],
            send_sem=send.at[base + k],
            recv_sem=recv.at[base + coordinate],
            device_id=target,
            device_id_type=MESH,
        ).start()

    def add():
        for k in range(1, size):
            pltpu.make_async_remote_copy(
                src_ref=ref,
                dst_ref=buf.at[base + coordinate],
                send_sem=send.at[base + k - 1],
                recv_sem=recv.at[base],
                device_id=here.to(),
                device_id_type=MESH,
            ).wait_send()
        for k in range(1, size):
            at = base + lax.rem(coordinate + k, size)
            pltpu.make_async_remote_copy(
                src_ref=ref,
                dst_ref=buf.at[at],
                send_sem=send.at[base],
                recv_sem=recv.at[at],
                device_id=here.to(),
                device_id_type=MESH,
            ).wait_recv()
        total = buf[base]
        for k in range(1, size):
            total = total + buf[base + k]
        ref[...] = total

    return add


def backward_kernel(
    images,
    slots,
    heads,
    dp,
    fsdp,
    ff,
    total_steps,
    locality_ref,
    xt_ref,
    qkvt_ref,
    pa_ref,
    pb_ref,
    dot_ref,
    mg_ref,
    small_ref,
    gsmall_ref,
    wqk_ref,
    wv_ref,
    part_ref,
    tgrad_ref,
    grad_ref,
    sum_ref,
    norm_ref,
    eye,
    pick,
    perm,
    cat_s,
    vec_s,
    acc_qk,
    acc_v,
    acc_vec,
    acc_place,
    acc_gate,
    hid_s,
    xh_s,
    rstd_s,
    vn_s,
    win_s,
    sc_s,
    mix_s,
    ds_s,
    dqkv_s,
    tg_s,
    last_s,
    a_mine,
    a_other,
    a_x,
    a_y,
    a_x2,
    a_y2,
    a_z,
    b_other,
    b_x,
    b_y,
    b_x2,
    b_y2,
    b_z,
    small_buf,
    norm_buf,
    load,
    a_send,
    a_recv,
    b_send,
    b_recv,
    sm_send,
    sm_recv,
    nm_send,
    nm_recv,
):
    d = xt_ref.shape[1]
    u, w = d // dp, d // fsdp
    _, split, rows_all = row_plan(ff // dp, u)
    hw = d // heads
    keys = acc_place.shape[1]
    n = images * PITCH
    scale = hw**-0.5
    step = pl.program_id(0)
    count = pl.num_programs(0)
    here = Place(dp, fsdp)
    zs, ys, xs, cores = here.zs, here.ys, here.xs, here.cores
    order = z_order(zs)

    def plane(k, dc=0):
        return here.to(dz=order[k], dc=dc)[0]

    first = Reducer(
        here,
        split,
        lambda k: a_mine.at[k],
        lambda k: part_ref.at[plane(k, 1)],
        a_other,
        (a_x, a_y, a_x2, a_y2, a_z),
        a_send,
        a_recv,
    )
    last = Reducer(
        here,
        rows_all - split,
        lambda k: last_s.at[plane(k)],
        lambda k: last_s.at[plane(k, 1)],
        b_other,
        (b_x, b_y, b_x2, b_y2, b_z),
        b_send,
        b_recv,
    )

    def loading(k):
        return pltpu.make_async_copy(part_ref.at[plane(k)], a_mine.at[k], load.at[k])

    @pl.when(step == 0)
    def _():
        for k in range(zs):
            loading(k).start()
        peers = [here.to(dz=k) for k in range(1, zs)] + [here.to(dc=k) for k in range(1, cores)]
        peers += [here.to(dy=a, dx=b) for a in range(ys) for b in range(xs) if a or b]
        peers = [
            here.to(dz=k, dc=c, dy=a, dx=b)
            for k in range(zs)
            for c in range(cores)
            for a in range(ys)
            for b in range(xs)
            if k or c or a or b
        ]
        greet(peers)
        first.begin()
        eye[...] = identity()
        pick[...] = one_hot(pick.shape, w, lambda block, lane: block * w + lane)
        e = lax.broadcasted_iota(jnp.int32, (2 * d, 1), 0)
        goal = (e % (2 * w)) // w * d + e // (2 * w) * w + e % w
        perm[...] = jnp.where(lax.broadcasted_iota(jnp.int32, perm.shape, 1) == goal, 1.0, 0.0).astype(bf16)
        for f in range(fsdp):
            for r in range(2):
                vec_s[r, w * f : w * (f + 1), :] = column(small_ref[f, r : r + 1, :])[0:w]
        for ref in (acc_qk, acc_v, acc_vec, acc_place, acc_gate, win_s, mix_s, ds_s):
            ref[...] = jnp.zeros_like(ref)
        for k in range(zs):
            loading(k).wait()

    spread = total_steps
    for t in range(zs + 2):

        @pl.when(step == min(t + 1, spread - 1))
        def _(t=t):
            first.turn(t)

    sig, cosig = gates(locality_ref, heads)
    wins = windows(heads, hw, d)
    tiles = [slice(128 * k, 128 * (k + 1)) for k in range(n // 128)]

    def place_of(t):
        at = 128 * t
        return at // PITCH, slice(at % PITCH, at % PITCH + 128)

    for t, tile in enumerate(tiles):
        b, lane = place_of(t)
        normal, rstd = norm_stats(xt_ref[b, :, lane].astype(f32))
        xh_s[:, tile] = normal
        rstd_s[0:1, tile] = rstd
        hid_s[:, tile] = (normal * vec_s[0] + vec_s[1]).astype(bf16)

    def backward(b, _):
        cols = pl.ds(pl.multiple_of(b * PITCH, PITCH), PITCH)
        vn_s[...] = mm_nt(eye[0:keys, :], qkvt_ref[b, 2 * d : 3 * d, :]).astype(bf16)

        def ba(h):
            lo, hi, at = wins[h]
            win_s[h, at : at + hw, :] = dot_ref[b, h * hw : (h + 1) * hw, :]
            sc_s[h % 2] = mm(vn_s[:, lo:hi], win_s[h, 0 : hi - lo, :])

        def bb(h):
            g = sc_s[h % 2]
            pa = pa_ref[b, h].astype(f32)
            pb = pb_ref[b, h].astype(f32)
            mix_s[h, 0:keys, :] = pa_ref[b, h] + pb_ref[b, h]
            pull_a = jnp.sum(g * pa, axis=0, keepdims=True) / cosig[h]
            pull_b = jnp.sum(g * pb, axis=0, keepdims=True) / sig[h]
            acc_gate[h : h + 1, :] += pull_b - pull_a
            acc_place[h] += pb * (g - pull_b)
            ds_s[h, 0:keys, :] = (pa * (g - pull_a)).astype(bf16)

        def bc(h):
            rows = slice(h * hw, (h + 1) * hw)
            dqkv_s[rows, cols] = (mm(qkvt_ref[b, d + h * hw : d + (h + 1) * hw, :], ds_s[h]) * scale).astype(bf16)
            dqkv_s[d + h * hw : d + (h + 1) * hw, cols] = (mm_nt(qkvt_ref[b, rows, :], ds_s[h]) * scale).astype(bf16)
            dqkv_s[2 * d + h * hw : 2 * d + (h + 1) * hw, cols] = mm_nt(dot_ref[b, rows, :], mix_s[h]).astype(bf16)

        for t in range(heads + 2):
            if t < heads:
                ba(t)
            if t >= 2:
                bc(t - 2)
            if 1 <= t <= heads:
                bb(t - 1)
        return 0

    lax.fori_loop(0, images, backward, 0)

    back = mm(wqk_ref[0], dqkv_s[0:d, :]) + mm(wqk_ref[1], dqkv_s[d : 2 * d, :]) + mm(wv_ref[...], dqkv_s[2 * d : 3 * d, :])
    acc_qk[...] += mm_nt(hid_s[...], dqkv_s[0 : 2 * d, :])
    for t, tile in enumerate(tiles):
        b, lane = place_of(t)
        grad = back[:, tile]
        normal = xh_s[:, tile]
        acc_vec[0] += grad * normal
        acc_vec[1] += grad
        pulled = norm_back(grad, vec_s[0], normal, rstd_s[0:1, tile])
        tg_s[:, tile] = (mg_ref[b, :, lane].astype(f32) + pulled).astype(bf16)
    acc_v[...] += mm_nt(dqkv_s[2 * d : 3 * d, :], hid_s[...])
    for b in range(images):
        tgrad_ref[b] = mm_nt(eye[0:slots, :], tg_s[:, b * PITCH : (b + 1) * PITCH]).astype(bf16)

    @pl.when(step == count - 1)
    def _():
        cat_s[...] = jnp.zeros_like(cat_s)
        acc_qk[...] = mm(acc_qk[...].astype(bf16), perm[...])
        for k in range(dp):
            cat_s[0:u, :] = mm_nt(acc_v[u * k : u * (k + 1), :].astype(bf16), pick[...])
            cat_s[u : 2 * u, :] = mm_nt(acc_qk[u * k : u * (k + 1), 0:d].astype(bf16), pick[...])
            cat_s[2 * u : 3 * u, :] = mm_nt(acc_qk[u * k : u * (k + 1), d : 2 * d].astype(bf16), pick[...])
            for f in range(fsdp):
                last_s[k, f] = cat_s[:, 128 * f : 128 * (f + 1)].astype(bf16)
        last.begin()

        sum_ref[...] = gsmall_ref[...]
        for f in range(fsdp):
            for r in range(2):
                sum_ref[f, r : r + 1, 0:w] = lane_sums(acc_vec[r, w * f : w * (f + 1), :])
        at = 6 + ff // d
        dc, dr, far = offset_planes(keys)
        rows = [[], [], []]
        for h in range(heads):
            pg = acc_place[h]
            for c, off in enumerate((dc, dr, far)):
                rows[c].append(jnp.sum(pg * off, axis=0, keepdims=True))
            acc_gate[h : h + 1, :] = acc_gate[h : h + 1, :] * (sig[h] * cosig[h])
        sum_ref[0, at + 3 : at + 4, 0 : acc_gate.shape[0]] = lane_sums(acc_gate[...])
        for c in range(3):
            for h in range(heads):
                acc_gate[h : h + 1, :] = rows[c][h]
            sum_ref[0, at + c : at + c + 1, 0 : acc_gate.shape[0]] = lane_sums(acc_gate[...])


        def small_round(base, coordinate, size, targets):
            return exchange(here, sum_ref, small_buf, sm_send, sm_recv, base, coordinate, size, targets)

        pending = small_round(0, here.c, cores, [here.to(dc=k) for k in range(1, cores)])
        total = first.total()
        grad_ref[0:split, :] = total
        squares = jnp.sum((total * total).reshape(split // 8, 8, 128), axis=0)
        for t in range(zs + 2):
            last.turn(t)
            if t == 0:
                pending()
                pending = small_round(cores, here.x, xs, [here.to(dx=b) for b in range(1, xs)])
            if t == 1:
                pending()
                pending = small_round(cores + xs, here.y, ys, [here.to(dy=a) for a in range(1, ys)])
            if t == 2:
                pending()
                pending = small_round(cores + xs + ys, here.z, zs, [here.to(dz=q) for q in range(1, zs)])
        pending()
        total = last.total()
        grad_ref[split:rows_all, :] = total
        norm_ref[...] = squares + jnp.sum((total * total).reshape((rows_all - split) // 8, 8, 128), axis=0)
        at = here.to()
        everyone = [
            here.to(dz=k, dc=c, dy=a, dx=b)
            for k in range(zs)
            for c in range(cores)
            for a in range(ys)
            for b in range(xs)
            if k or c or a or b
        ]
        exchange(here, norm_ref, norm_buf, nm_send, nm_recv, 0, at[0] * fsdp + at[1], dp * fsdp, everyone)()
        first.finish()
        last.finish()


def run_backward(dp, fsdp, slots, kept, small, small_part, wqk, wv, first_part, locality, ff, images):
    b, d, _ = kept[0].shape
    heads = locality.shape[1]
    keys = kept[2].shape[2]
    n = images * PITCH
    _, split, rows = row_plan(ff // dp, d // dp)
    more = rows - split
    cores = 2 if dp % 2 == 0 else 1
    zs = dp // cores
    ys = max(v for v in range(1, fsdp + 1) if fsdp % v == 0 and v * v <= fsdp)
    xs = fsdp // ys
    copies = len(reducer_keys(zs, ys, xs, cores))
    rounds = cores + xs + ys + zs

    def whole(shape):
        return pl.BlockSpec(shape, lambda g: (0,) * len(shape), pipeline_mode=pl.Buffered(1))

    def per(shape):
        mode = pl.Buffered(1) if fsdp > 4 and shape[-1] == PITCH else None
        return pl.BlockSpec((images,) + shape, lambda g: (g,) + (0,) * len(shape), pipeline_mode=mode)

    scratch = [
        pltpu.VMEM((PITCH, PITCH), bf16),
        pltpu.VMEM((fsdp * 128, d), bf16),
        pltpu.VMEM((2 * d, 2 * d), bf16),
        pltpu.VMEM((more, fsdp * 128), f32),
        pltpu.VMEM((2, d, 128), f32),
        pltpu.VMEM((d, 2 * d), f32),
        pltpu.VMEM((d, d), f32),
        pltpu.VMEM((2, d, 128), f32),
        pltpu.VMEM((heads, keys, PITCH), f32),
        pltpu.VMEM((-(-heads // 8) * 8, PITCH), f32),
        pltpu.VMEM((d, n), bf16),
        pltpu.VMEM((d, n), f32),
        pltpu.VMEM((8, n), f32),
        pltpu.VMEM((keys, d), bf16),
        pltpu.VMEM((heads, PITCH, PITCH), bf16),
        pltpu.VMEM((2, keys, PITCH), f32),
        pltpu.VMEM((heads, PITCH, PITCH), bf16),
        pltpu.VMEM((heads, PITCH, PITCH), bf16),
        pltpu.VMEM((3 * d, n), bf16),
        pltpu.VMEM((d, n), bf16),
        pltpu.VMEM((dp, fsdp, more, 128), bf16),
        pltpu.VMEM((zs, fsdp, split, 128), bf16),
        pltpu.VMEM((zs, fsdp, split, 128), bf16),
        *reducer_buffers(zs, ys, xs, split),
        pltpu.VMEM((zs, fsdp, more, 128), bf16),
        *reducer_buffers(zs, ys, xs, more),
        pltpu.VMEM((rounds,) + small.shape, f32),
        pltpu.VMEM((fsdp * dp, 8, 128), f32),
        pltpu.SemaphoreType.DMA((zs,)),
        pltpu.SemaphoreType.DMA((copies,)),
        pltpu.SemaphoreType.DMA((copies,)),
        pltpu.SemaphoreType.DMA((copies,)),
        pltpu.SemaphoreType.DMA((copies,)),
        pltpu.SemaphoreType.DMA((rounds,)),
        pltpu.SemaphoreType.DMA((rounds,)),
        pltpu.SemaphoreType.DMA((fsdp * dp,)),
        pltpu.SemaphoreType.DMA((fsdp * dp,)),
    ]
    return pl.pallas_call(
        partial(backward_kernel, images, slots, heads, dp, fsdp, ff, b // images),
        grid=(b // images,),
        out_shape=[
            jax.ShapeDtypeStruct((b, slots, d), bf16),
            jax.ShapeDtypeStruct((rows, 128), f32),
            jax.ShapeDtypeStruct(small.shape, f32),
            jax.ShapeDtypeStruct((8, 128), f32),
        ],
        in_specs=[pl.BlockSpec(memory_space=pltpu.SMEM)]
        + [per(v.shape[1:]) for v in kept]
        + [whole(small.shape), whole(small.shape), whole((2, d, d)), whole((d, d)), pl.BlockSpec(memory_space=pl.ANY)],
        out_specs=[per((slots, d)), whole((rows, 128)), whole(small.shape), whole((8, 128))],
        scratch_shapes=scratch,
        compiler_params=pltpu.CompilerParams(
            dimension_semantics=("arbitrary",),
            collective_id=1,
            has_side_effects=True,
            vmem_limit_bytes=63 * 1024 * 1024,
        ),
        cost_estimate=pl.CostEstimate(flops=25_000_000_000, bytes_accessed=70_000_000, transcendentals=0),
    )(locality, *kept, small, small_part, wqk, wv, first_part)


def adamw(parameter, moment_one, moment_two, gradient, rate, decay_rate):
    first_new = beta_one * moment_one + (1.0 - beta_one) * gradient
    second_new = beta_two * moment_two + (1.0 - beta_two) * gradient * gradient
    first_hat = first_new / (1.0 - beta_one**STEP)
    second_hat = second_new / (1.0 - beta_two**STEP)
    new_value = parameter - rate * (
        first_hat / (jnp.sqrt(second_hat) + adam_eps) + decay_rate * parameter
    )
    return (new_value, first_new, second_new)


def update_kernel(heads, *refs):
    grad_ref, small_ref, norm_ref = refs[0:3]
    states = [refs[3 + 3 * k : 6 + 3 * k] for k in range(8)]
    outs = refs[27:]
    small = small_ref[...]
    norm = jnp.sqrt(jnp.sum(norm_ref[...], keepdims=True) + jnp.sum(small * small, keepdims=True)[0])
    factor = clip_limit / jnp.maximum(norm, clip_limit)
    outs[0][...] = norm
    u, w = states[1][0].shape
    fu = states[3][0].shape[0]
    o_at, split, _ = row_plan(fu, u)
    starts = {1: split, 2: o_at, 3: 0, 4: fu}

    def matrix(k, state, gradient, place):
        new_value, first_new, second_new = adamw(
            state[0][place], state[1][place], state[2][place], gradient * factor, learn_rate, weight_decay
        )
        outs[1 + 4 * k][place] = new_value
        outs[2 + 4 * k][place] = new_value.astype(bf16)
        outs[3 + 4 * k][place] = first_new
        outs[4 + 4 * k][place] = second_new

    at = split + u
    gradient = jnp.concatenate([grad_ref[at : at + u, 0:w], grad_ref[at + u : at + 2 * u, 0:w]], axis=1)
    matrix(0, states[0], gradient, ...)
    for k in (1, 2, 3, 4):
        rows = states[k][0].shape[0]
        matrix(k, states[k], grad_ref[starts[k] : starts[k] + rows, 0:w], ...)
    mine = small_ref[lax.axis_index("fsdp")]
    share = states[6][0].shape[1] // w
    row = jnp.concatenate([mine[6 + r : 7 + r, 0:w] for r in range(share)], axis=1)
    gradients = (mine[0:6, 0:w], row, small_ref[0, 6 + share : 10 + share, 0:heads])
    for k in range(3):
        state = states[5 + k]
        new_value, first_new, second_new = adamw(
            state[0][...], state[1][...], state[2][...], gradients[k] * factor, small_rate, 0.0
        )
        outs[21 + 3 * k][...] = new_value
        outs[22 + 3 * k][...] = first_new
        outs[23 + 3 * k][...] = second_new


def update(heads, grad, small, norm, states):
    shapes = [jax.ShapeDtypeStruct((1, 1), f32)]
    for k in range(5):
        shape = states[3 * k].shape
        shapes += [jax.ShapeDtypeStruct(shape, kind) for kind in (f32, bf16, f32, f32)]
    for k in range(5, 8):
        shapes += [jax.ShapeDtypeStruct(states[3 * k].shape, f32)] * 3
    return pl.pallas_call(
        partial(update_kernel, heads),
        out_shape=shapes,
        in_specs=[pl.BlockSpec(memory_space=pltpu.VMEM)] * 27,
        out_specs=[pl.BlockSpec(memory_space=pltpu.VMEM)] * len(shapes),
        compiler_params=pltpu.CompilerParams(vmem_limit_bytes=62 * 1024 * 1024),
    )(grad, small, norm, *states)


def body(
    dp,
    fsdp,
    tokens,
    keep_mask,
    cotangent,
    qk_weight,
    qk_first,
    qk_second,
    value_weight,
    value_first,
    value_second,
    out_weight,
    out_first,
    out_second,
    up_weight,
    up_first,
    up_second,
    down_weight,
    down_first,
    down_second,
    vectors,
    vectors_first,
    vectors_second,
    up_bias,
    up_bias_first,
    up_bias_second,
    locality,
    locality_first,
    locality_second,
):
    d = tokens.shape[-1]
    heads = locality.shape[1]
    ff = up_bias.shape[0] * fsdp
    images = 2 if fsdp <= 4 else 1
    vis = jnp.pad(keep_mask.astype(f32), ((0, 0), (0, PITCH - tokens.shape[1])))[:, None, :]
    everything, small, tokens, cotangent = gather_all(
        dp,
        fsdp,
        up16(4 * d // dp),
        qk_weight,
        value_weight.T,
        out_weight.T,
        vectors,
        up_bias,
        tokens,
        cotangent,
    )
    xt, qkvt, pa, pb, mixture, wqk, wv, feed = run_attend(
        dp, fsdp, tokens, vis, everything, small, up_weight.T, down_weight, locality, images
    )
    result, mixture_grad, middle_grad, first_part, small_part = run_feed(
        dp, fsdp, cotangent, vis, xt, mixture, everything, feed, small, ff, images
    )
    kept = (xt, qkvt, pa, pb, mixture_grad, middle_grad)
    token_grad, grad, small_sum, norm = run_backward(
        dp, fsdp, tokens.shape[1], kept, small, small_part, wqk, wv, first_part, locality, ff, images
    )

    def flat(v):
        return v.reshape(1, -1)

    states = [qk_weight, qk_first, qk_second]
    states += [v.T for v in (value_weight, value_first, value_second, out_weight, out_first, out_second)]
    states += [v.T for v in (up_weight, up_first, up_second)]
    states += [down_weight, down_first, down_second, vectors, vectors_first, vectors_second]
    states += [flat(up_bias), flat(up_bias_first), flat(up_bias_second), locality, locality_first, locality_second]
    outs = list(update(heads, grad, small_sum, norm, states))
    for k in range(5, 17):
        outs[k] = outs[k].T
    for k in (24, 25, 26):
        outs[k] = outs[k].reshape(up_bias.shape)
    outs[0] = outs[0].reshape(())
    return (result, token_grad, *outs)


def solution(mesh):
    placed = (
        P(("dp", "fsdp"), None, None),
        P(("dp", "fsdp"), None),
        P(("dp", "fsdp"), None, None),
        P("dp", "fsdp"),
        P("dp", "fsdp"),
        P("dp", "fsdp"),
        P("fsdp", "dp"),
        P("fsdp", "dp"),
        P("fsdp", "dp"),
        P("fsdp", "dp"),
        P("fsdp", "dp"),
        P("fsdp", "dp"),
        P("fsdp", "dp"),
        P("fsdp", "dp"),
        P("fsdp", "dp"),
        P("dp", "fsdp"),
        P("dp", "fsdp"),
        P("dp", "fsdp"),
        P(None, "fsdp"),
        P(None, "fsdp"),
        P(None, "fsdp"),
        P("fsdp"),
        P("fsdp"),
        P("fsdp"),
        P(),
        P(),
        P(),
    )
    return jax.shard_map(
        partial(body, mesh.shape["dp"], mesh.shape["fsdp"]),
        mesh=mesh,
        in_specs=placed,
        out_specs=(
            P(("dp", "fsdp"), None, None),
            P(("dp", "fsdp"), None, None),
            P(),
            P("dp", "fsdp"),
            P("dp", "fsdp"),
            P("dp", "fsdp"),
            P("dp", "fsdp"),
            P("fsdp", "dp"),
            P("fsdp", "dp"),
            P("fsdp", "dp"),
            P("fsdp", "dp"),
            P("fsdp", "dp"),
            P("fsdp", "dp"),
            P("fsdp", "dp"),
            P("fsdp", "dp"),
            P("fsdp", "dp"),
            P("fsdp", "dp"),
            P("fsdp", "dp"),
            P("fsdp", "dp"),
            P("dp", "fsdp"),
            P("dp", "fsdp"),
            P("dp", "fsdp"),
            P("dp", "fsdp"),
            P(None, "fsdp"),
            P(None, "fsdp"),
            P(None, "fsdp"),
            P("fsdp"),
            P("fsdp"),
            P("fsdp"),
            P(),
            P(),
            P(),
        ),
        check_vma=False,
    )
```

```python
from functools import partial

import jax
import jax.numpy as jnp
from jax import lax
from jax.experimental import pallas as pl
from jax.experimental.pallas import tpu as pltpu
from jax.sharding import PartitionSpec as P

GRID = 14
STEP = 5
PITCH = 256

norm_eps = 1e-06
learn_rate = 0.03
small_rate = 0.3
beta_one = 0.5
beta_two = 0.5
adam_eps = 1e-08
weight_decay = 0.05
clip_limit = 1.0

LOG2E = 1.4426950408889634
PHI_ZERO = 0.3989422804014327

f32 = jnp.float32
bf16 = jnp.bfloat16


def mm(a, b):
    return lax.dot_general(a, b, (((1,), (0,)), ((), ())), preferred_element_type=f32)


def mm_nt(a, b):
    return lax.dot_general(a, b, (((1,), (1,)), ((), ())), preferred_element_type=f32)


def gelu_parts(u):
    v = u * 0.5**0.5
    cdf = 0.5 * lax.erf(v) + 0.5
    bell = jnp.exp2(v * v * -LOG2E)
    return u * cdf, cdf + (v * (PHI_ZERO * 2**0.5)) * bell


MESH = pl.DeviceIdType.MESH


def up16(v):
    return -(-v // 16) * 16


class Place:
    def __init__(self, dp, fsdp):
        self.cores = 2 if dp % 2 == 0 else 1
        self.zs = dp // self.cores
        self.ys = max(v for v in range(1, fsdp + 1) if fsdp % v == 0 and v * v <= fsdp)
        self.xs = fsdp // self.ys
        self.fs = fsdp
        at_dp, at_f = lax.axis_index("dp"), lax.axis_index("fsdp")
        self.z, self.c = at_dp // self.cores, at_dp % self.cores
        self.y, self.x = at_f // self.xs, at_f % self.xs

    def to(self, dz=0, dc=0, dy=0, dx=0):
        z = lax.rem(self.z + dz, self.zs)
        c = lax.rem(self.c + dc, self.cores)
        y = lax.rem(self.y + dy, self.ys)
        x = lax.rem(self.x + dx, self.xs)
        return (z * self.cores + c, y * self.xs + x)


def greet(peers):
    barrier = pltpu.get_barrier_semaphore()
    for peer in peers:
        pl.semaphore_signal(barrier, inc=1, device_id=peer, device_id_type=MESH)
    pl.semaphore_wait(barrier, len(peers))


def row_plan(fu, u):
    o_at = 2 * up16(fu)
    split = up16(o_at + u)
    return o_at, split, split + up16(3 * u)


class Gatherer:
    def __init__(self, here, rows, block, slots, send, recv):
        self.here, self.block, self.slots, self.send, self.recv = here, block, slots, send, recv
        half = rows // 32 * 16
        self.segs = (pl.ds(0, half), pl.ds(half, rows - half))
        self.keys = gatherer_keys(here.zs, here.ys, here.xs, here.cores)
        self.order = [0] + z_order(here.zs)[:-1]

    def slot(self, owner, seg):
        return self.slots.at[owner[0], owner[1], self.segs[seg]]

    def copy(self, key):
        here, kind, k, a, b, seg, to = self.here, *key
        owner = here.to(dz=k, dy=a, dx=b)
        own = (k, a, b) == (0, 0, 0)
        target = {"z": here.to(dz=to), "y": here.to(dy=to), "x": here.to(dx=to), "c": here.to(dc=to)}[kind]
        return pltpu.make_async_remote_copy(
            src_ref=self.block.at[self.segs[seg]] if own else self.slot(owner, seg),
            dst_ref=self.slot(owner, seg),
            send_sem=self.send.at[self.keys.index(key)],
            recv_sem=self.recv.at[owner[0] * here.fs + owner[1], seg],
            device_id=target,
            device_id_type=MESH,
        )

    def push(self, kind, k, a, b, seg):
        for key in self.keys:
            if key[:5] == (kind, k, a, b, seg):
                self.copy(key).start()

    def arrive(self, k, a, b, seg, dc=0):
        owner = self.here.to(dz=k, dy=a, dx=b, dc=dc)
        slot = self.slot(owner, seg)
        pltpu.make_async_remote_copy(
            src_ref=slot,
            dst_ref=slot,
            send_sem=self.send.at[0],
            recv_sem=self.recv.at[owner[0] * self.here.fs + owner[1], seg],
            device_id=self.here.to(),
            device_id_type=MESH,
        ).wait_recv()

    def spread(self, k):
        for kind in "yxc":
            for seg in (0, 1):
                self.push(kind, k, 0, 0, seg)

    def relay(self, k):
        here = self.here
        for a in range(1, here.ys):
            self.arrive(k, a, 0, 0)
            self.push("x", k, a, 0, 0)
        for b in range(1, here.xs):
            self.arrive(k, 0, b, 1)
            self.push("y", k, 0, b, 1)
        for a in range(1, here.ys):
            self.arrive(k, a, 0, 1)
            for seg in (0, 1):
                self.push("c", k, a, 0, seg)
        for b in range(1, here.xs):
            self.arrive(k, 0, b, 0)
            for seg in (0, 1):
                self.push("c", k, 0, b, seg)

    def corner(self, k):
        for a in range(1, self.here.ys):
            for b in range(1, self.here.xs):
                for seg in (0, 1):
                    self.arrive(k, a, b, seg)
                    self.push("c", k, a, b, seg)

    def twin(self, k):
        here = self.here
        for c in range(1, here.cores):
            for a in range(here.ys):
                for b in range(here.xs):
                    for seg in (0, 1):
                        self.arrive(k, a, b, seg, c)

    def events(self):
        return self.here.zs + 3

    def event(self, t):
        zs = self.here.zs
        if t == 0:
            for seg in (0, 1):
                self.push("z", 0, 0, 0, seg)
            self.spread(0)
        elif t < zs:
            for seg in (0, 1):
                self.arrive(self.order[t], 0, 0, seg)
            self.spread(self.order[t])
            self.relay(self.order[t - 1])
        elif t == zs:
            self.relay(self.order[zs - 1])
            for k in self.order[: zs // 2]:
                self.corner(k)
        elif t == zs + 1:
            for k in self.order[zs // 2 :]:
                self.corner(k)
        else:
            for k in self.order:
                self.twin(k)

    def finish(self):
        for key in self.keys:
            self.copy(key).wait_send()


def gatherer_keys(zs, ys, xs, cores):
    keys = [("z", 0, 0, 0, seg, k) for seg in (0, 1) for k in range(1, zs)]
    for k in range(zs):
        for seg in (0, 1):
            keys += [("y", k, 0, 0, seg, a) for a in range(1, ys)]
            keys += [("x", k, 0, 0, seg, b) for b in range(1, xs)]
        keys += [("x", k, a, 0, 0, b) for a in range(1, ys) for b in range(1, xs)]
        keys += [("y", k, 0, b, 1, a) for a in range(1, ys) for b in range(1, xs)]
        keys += [("c", k, a, b, seg, c) for a in range(ys) for b in range(xs) for seg in (0, 1) for c in range(1, cores)]
    return keys


def gather_kernel(dp, fsdp, rows, qk_ref, vt_ref, ot_ref, vec_ref, upb_ref, tok_ref, cot_ref, all_ref, small_ref, tok_out, cot_out, wide, block, part, slab, rows_s, turned_s, in_qk, in_vt, in_ot, in_vec, in_upb, in_sem, send, recv, small_send, small_recv, local, turn_sem):
    here = Place(dp, fsdp)
    zs, ys, xs, cores = here.zs, here.ys, here.xs, here.cores
    u, w = vt_ref.shape
    me = here.to()
    peers = [here.to(dz=k) for k in range(1, zs)] + [here.to(dc=k) for k in range(1, cores)]
    peers += [here.to(dy=a, dx=b) for a in range(ys) for b in range(xs) if a or b]

    loads = []
    for ref, into in ((qk_ref, in_qk), (vt_ref, in_vt), (ot_ref, in_ot), (vec_ref, in_vec), (upb_ref, in_upb)):
        loads.append(pltpu.make_async_copy(ref, into, in_sem.at[len(loads)]))
        loads[-1].start()
    slots, images, d = tok_ref.shape
    spans = [(lo, min(lo + 128, d)) for lo in range(0, d, 128)]
    arrivals = [pltpu.make_async_copy(ref, slab.at[n], turn_sem.at[n]) for n, ref in enumerate((tok_ref, cot_ref))]
    for copy in arrivals:
        copy.start()

    def widen_all(n):
        arrivals[n].wait()

        def widen(k, _):
            for c, (lo, hi) in enumerate(spans):
                rows_s[c, pl.ds(pl.multiple_of(k * images, 8), images), 0 : hi - lo] = slab[n, k, :, lo:hi].astype(f32)
            return 0

        lax.fori_loop(0, slots, widen, 0, unroll=4)

    def pick_all(n, out, first, count):
        def pick(k, _):
            for c, (lo, hi) in enumerate(spans):
                turned_s[n, k, :, lo:hi] = rows_s[c, pl.ds(k, slots, stride=images), :][:, 0 : hi - lo].astype(bf16)
            return 0

        lax.fori_loop(first, first + count, pick, 0)
        copy = pltpu.make_async_copy(turned_s.at[n, pl.ds(first, count)], out.at[pl.ds(first, count)], turn_sem.at[n])
        copy.start()
        return copy

    wide[...] = jnp.zeros_like(wide)
    part[...] = jnp.zeros_like(part)
    for copy in loads:
        copy.wait()
    wide[0:u, 0:w] = in_ot[...]
    wide[u : 2 * u, 0:w] = in_vt[...]
    for k in range(in_qk.shape[1] // w):
        wide[(k + 2) * u : (k + 3) * u, 0:w] = in_qk[:, k * w : (k + 1) * w]
    block[...] = wide[...].astype(bf16)
    part[0:6, 0:w] = in_vec[...]
    for r in range(in_upb.shape[1] // w):
        part[6 + r : 7 + r, 0:w] = in_upb[:, r * w : (r + 1) * w]

    greet(peers)
    gatherer = Gatherer(here, rows, block, all_ref, send, recv)
    gatherer.event(0)
    own_copy = pltpu.make_async_copy(block, all_ref.at[me[0], me[1]], local.at[0])
    own_copy.start()
    small_copy = pltpu.make_async_copy(part, small_ref.at[me[1]], local.at[1])
    small_copy.start()
    smalls = []
    for a in range(ys):
        for b in range(xs):
            if a or b:
                n = len(smalls)
                copy = pltpu.make_async_remote_copy(
                    src_ref=part,
                    dst_ref=small_ref.at[me[1]],
                    send_sem=small_send.at[n],
                    recv_sem=small_recv.at[me[1]],
                    device_id=here.to(dy=a, dx=b),
                    device_id_type=MESH,
                )
                copy.start()
                smalls.append(copy)
    turns = []
    jobs = [
        lambda: widen_all(0),
        lambda: turns.append(pick_all(0, tok_out, 0, images)),
        lambda: widen_all(1),
        lambda: turns.append(pick_all(1, cot_out, 0, images)),
    ]
    for t in range(1, gatherer.events()):
        if jobs:
            jobs.pop(0)()
        gatherer.event(t)
    for job in jobs:
        job()
    for a in range(ys):
        for b in range(xs):
            if a or b:
                peer = here.to(dy=a, dx=b)
                pltpu.make_async_remote_copy(
                    src_ref=part,
                    dst_ref=small_ref.at[peer[1]],
                    send_sem=small_send.at[0],
                    recv_sem=small_recv.at[peer[1]],
                    device_id=me,
                    device_id_type=MESH,
                ).wait_recv()
    gatherer.finish()
    for copy in smalls:
        copy.wait_send()
    own_copy.wait()
    small_copy.wait()
    for copy in turns:
        copy.wait()


def shape_of(dp, fsdp):
    cores = 2 if dp % 2 == 0 else 1
    ys = max(v for v in range(1, fsdp + 1) if fsdp % v == 0 and v * v <= fsdp)
    return dp // cores, ys, fsdp // ys, cores


def gather_all(dp, fsdp, rows, qk, vt, ot, vectors, up_bias, tokens, cotangent):
    images, slots, d = tokens.shape
    flat_bias = up_bias.reshape(1, -1)
    shards = (qk, vt, ot, vectors, flat_bias)
    return pl.pallas_call(
        partial(gather_kernel, dp, fsdp, rows),
        out_shape=[
            jax.ShapeDtypeStruct((dp, fsdp, rows, 128), bf16),
            jax.ShapeDtypeStruct((fsdp, 16, 128), f32),
            jax.ShapeDtypeStruct((images, slots, d), bf16),
            jax.ShapeDtypeStruct((images, slots, d), bf16),
        ],
        in_specs=[pl.BlockSpec(memory_space=pl.ANY)] * 7,
        out_specs=[pl.BlockSpec(memory_space=pl.ANY)] * 4,
        scratch_shapes=[
            pltpu.VMEM((rows, 128), f32),
            pltpu.VMEM((rows, 128), bf16),
            pltpu.VMEM((16, 128), f32),
            pltpu.VMEM((2, slots, images, d), bf16),
            pltpu.VMEM((-(-d // 128), slots * images, 128), f32),
            pltpu.VMEM((2, images, slots, d), bf16),
            *[pltpu.VMEM(v.shape, f32) for v in shards],
            pltpu.SemaphoreType.DMA((len(shards),)),
            pltpu.SemaphoreType.DMA((len(gatherer_keys(*shape_of(dp, fsdp))),)),
            pltpu.SemaphoreType.DMA((dp * fsdp, 2)),
            pltpu.SemaphoreType.DMA((fsdp,)),
            pltpu.SemaphoreType.DMA((fsdp,)),
            pltpu.SemaphoreType.DMA((2,)),
            pltpu.SemaphoreType.DMA((2,)),
        ],
        compiler_params=pltpu.CompilerParams(collective_id=0, has_side_effects=True, vmem_limit_bytes=62 * 1024 * 1024),
    )(*shards, tokens.transpose(1, 0, 2), cotangent.transpose(1, 0, 2))


def identity():
    rows = lax.broadcasted_iota(jnp.int32, (PITCH, PITCH), 0)
    cols = lax.broadcasted_iota(jnp.int32, (PITCH, PITCH), 1)
    return jnp.where(rows == cols, 1.0, 0.0).astype(bf16)


def one_hot(shape, w, goal):
    r = lax.broadcasted_iota(jnp.int32, shape, 0)
    c = lax.broadcasted_iota(jnp.int32, shape, 1)
    block, lane = r // 128, r % 128
    return jnp.where((c == goal(block, lane)) & (lane < w), 1.0, 0.0).astype(bf16)


def offset_planes(keys):
    j = lax.broadcasted_iota(jnp.int32, (keys, PITCH), 0)
    i = lax.broadcasted_iota(jnp.int32, (keys, PITCH), 1)
    rj, ri = j // GRID, i // GRID
    dc = ((j - rj * GRID) - (i - ri * GRID)).astype(f32)
    dr = (rj - ri).astype(f32)
    return dc, dr, dc * dc + dr * dr


def gates(locality_ref, heads):
    sig, cosig = [], []
    for h in range(heads):
        s = 1.0 / (1.0 + jnp.exp(-jnp.full((1, PITCH), locality_ref[3, h], f32)))
        sig.append(s)
        cosig.append(1.0 - s)
    return sig, cosig


def windows(heads, hw, d):
    wins = []
    for h in range(heads):
        lo = (h * hw) // 128 * 128
        wins.append((lo, min(lo + PITCH, d), h * hw - lo))
    return wins


def lane_sums(v):
    ones = jnp.ones((16, v.shape[1]), bf16)
    high = v.astype(bf16)
    low = (v - high.astype(f32)).astype(bf16)
    return (mm_nt(ones, high) + mm_nt(ones, low))[0:1]


def column(row):
    return jnp.broadcast_to(row, (128, 128)).T


def norm_stats(x):
    d = x.shape[0]
    mean = jnp.sum(x, axis=0, keepdims=True) * (1.0 / d)
    center = x - mean
    rstd = lax.rsqrt(jnp.sum(center * center, axis=0, keepdims=True) * (1.0 / d) + norm_eps)
    return center * rstd, rstd


def norm_back(grad, gain, normal, rstd):
    d = grad.shape[0]
    pull = grad * gain
    m1 = jnp.sum(pull, axis=0, keepdims=True) * (1.0 / d)
    m2 = jnp.sum(pull * normal, axis=0, keepdims=True) * (1.0 / d)
    return rstd * (pull - m1 - normal * m2)


def turn_in(ref, b, eye, pad_in, out):
    _, slots, d = ref.shape
    pad_in[0:slots, 0:d] = ref[b]
    for lo in range(0, d, PITCH):
        hi = min(lo + PITCH, d)
        out[lo:hi, :] = mm_nt(eye[0 : hi - lo, 0 : hi - lo], pad_in[:, lo:hi]).astype(bf16)


def turned(eye, ref, out_ref, row=0):
    for lo in range(0, ref.shape[1], PITCH):
        hi = min(lo + PITCH, ref.shape[1])
        out_ref[row + lo : row + hi, :] = mm_nt(eye[0 : hi - lo, 0 : hi - lo], ref[:, lo:hi]).astype(bf16)


def attend_kernel(
    images,
    slots,
    heads,
    dp,
    fsdp,
    total_steps,
    locality_ref,
    tok_ref,
    vis_ref,
    all_ref,
    small_ref,
    upt_ref,
    dn_ref,
    xt_ref,
    qkvt_ref,
    pa_ref,
    pb_ref,
    mixture_ref,
    wqk_ref,
    wv_ref,
    feed_ref,
    eye,
    pick,
    spread_a,
    spread_b,
    cat_s,
    chunk_s,
    whole_s,
    wide,
    block,
    wqkvt_s,
    vec_s,
    pad_in,
    placed,
    hid_s,
    kn_s,
    win_s,
    sc_s,
    mix_s,
    chunk_sem,
    own_sem,
    send,
    recv,
):
    d = tok_ref.shape[-1]
    u, w = d // dp, d // fsdp
    fu = upt_ref.shape[0]
    ring = chunk_s.shape[0]
    hw = d // heads
    keys = placed.shape[1]
    n = images * PITCH
    scale = hw**-0.5
    step = pl.program_id(0)
    here = Place(dp, fsdp)
    zs, ys, xs, cores = here.zs, here.ys, here.xs, here.cores
    me = here.to()
    gatherer = Gatherer(here, block.shape[0], block, feed_ref, send, recv)
    own_copy = pltpu.make_async_copy(block, feed_ref.at[me[0], me[1]], own_sem.at[0])

    @pl.when(step == 0)
    def _():
        def fetch(k):
            return pltpu.make_async_copy(all_ref.at[k], chunk_s.at[k % ring], chunk_sem.at[k % ring])

        for k in range(ring):
            fetch(k).start()
        wide[...] = jnp.zeros_like(wide)
        wide[0:fu, 0:w] = upt_ref[...]
        wide[up16(fu) : up16(fu) + fu, 0:w] = dn_ref[...]
        block[...] = wide[...].astype(bf16)
        peers = [here.to(dz=k) for k in range(1, zs)] + [here.to(dc=k) for k in range(1, cores)]
        peers += [here.to(dy=k) for k in range(1, ys)] + [here.to(dx=k) for k in range(1, xs)]
        greet(peers)
        gatherer.event(0)
        own_copy.start()

        eye[...] = identity()
        pad_in[...] = jnp.zeros_like(pad_in)
        dc, dr, far = offset_planes(keys)
        for h in range(heads):
            placed[h] = (locality_ref[0, h] * dc + locality_ref[1, h] * dr + locality_ref[2, h] * far) * LOG2E
        pick[...] = one_hot(pick.shape, w, lambda block, lane: block * w + lane)
        goal = lax.broadcasted_iota(jnp.int32, (d, 1), 0)
        goal = goal // w * (2 * w) + goal % w
        lane = lax.broadcasted_iota(jnp.int32, spread_a.shape, 1)
        spread_a[...] = jnp.where(lane == goal, 1.0, 0.0).astype(bf16)
        spread_b[...] = jnp.where(lane == goal + w, 1.0, 0.0).astype(bf16)

        for k in range(dp):
            fetch(k).wait()
            for f in range(fsdp):
                cat_s[:, 128 * f : 128 * (f + 1)] = chunk_s[k % ring, f].astype(f32)
            if k + ring < dp:
                fetch(k + ring).start()
            for p in range(3):
                whole_s[p, u * k : u * (k + 1), :] = cat_s[(p + 1) * u : (p + 2) * u, :]

        def dense(p):
            return mm(whole_s[p].astype(bf16), pick[...]).astype(bf16)

        wqkvt_s[2 * d : 3 * d, :] = dense(0)
        turned(eye, wqkvt_s.at[2 * d : 3 * d], wv_ref)
        joint = mm(dense(1), spread_a[...]) + mm(dense(2), spread_b[...])
        wqk_ref[0] = joint[:, 0:d].astype(bf16)
        wqk_ref[1] = joint[:, d : 2 * d].astype(bf16)
        turned(eye, wqk_ref.at[0], wqkvt_s)
        turned(eye, wqk_ref.at[1], wqkvt_s, d)
        for f in range(fsdp):
            for r in range(2):
                vec_s[r, w * f : w * (f + 1), :] = column(small_ref[f, r : r + 1, :])[0:w]
        for ref in (win_s, mix_s):
            ref[...] = jnp.zeros_like(ref)

    for t in range(1, gatherer.events()):

        @pl.when(step == min(t, total_steps - 1))
        def _(t=t):
            gatherer.event(t)

    def enter(b, _):
        turn_in(tok_ref, b, eye, pad_in, xt_ref.at[b])
        return 0

    lax.fori_loop(0, images, enter, 0)

    for t in range(n // 128):
        at = 128 * t
        normal, _ = norm_stats(xt_ref[at // PITCH, :, at % PITCH : at % PITCH + 128].astype(f32))
        hid_s[:, at : at + 128] = (normal * vec_s[0] + vec_s[1]).astype(bf16)
    joint = mm(wqkvt_s[...], hid_s[...]).astype(bf16)
    for b in range(images):
        qkvt_ref[b] = joint[:, PITCH * b : PITCH * (b + 1)]

    sig, cosig = gates(locality_ref, heads)
    wins = windows(heads, hw, d)

    def forward(b, _):
        kn_s[...] = mm_nt(eye[0:keys, :], qkvt_ref[b, d : 2 * d, :]).astype(bf16)
        key_vis = mm_nt(eye[0:keys, :], jnp.broadcast_to(vis_ref[b, 0:1, :], (PITCH, PITCH)).astype(bf16))
        bias = jnp.where(key_vis > 0.5, 0.0, -1e30)

        def fa(h):
            lo, hi, at = wins[h]
            win_s[h, at : at + hw, :] = qkvt_ref[b, h * hw : (h + 1) * hw, :]
            sc_s[h % 2] = mm(kn_s[:, lo:hi], win_s[h, 0 : hi - lo, :])

        def fb(h):
            scores = sc_s[h % 2] * (scale * LOG2E) + bias
            p = jnp.exp2(scores - jnp.max(scores, axis=0, keepdims=True))
            pa = p * (cosig[h] / jnp.sum(p, axis=0, keepdims=True))
            z = placed[h] + bias
            e = jnp.exp2(z - jnp.max(z, axis=0, keepdims=True))
            pb = e * (sig[h] / jnp.sum(e, axis=0, keepdims=True))
            pa_ref[b, h] = pa.astype(bf16)
            pb_ref[b, h] = pb.astype(bf16)
            mix_s[h, 0:keys, :] = (pa + pb).astype(bf16)

        def fc(h):
            mixture_ref[b, h * hw : (h + 1) * hw, :] = mm(
                qkvt_ref[b, 2 * d + h * hw : 2 * d + (h + 1) * hw, :], mix_s[h]
            ).astype(bf16)

        for t in range(heads + 2):
            if t < heads:
                fa(t)
            if t >= 2:
                fc(t - 2)
            if 1 <= t <= heads:
                fb(t - 1)
        return 0

    lax.fori_loop(0, images, forward, 0)

    @pl.when(step == total_steps - 1)
    def _():
        own_copy.wait()
        gatherer.finish()


def run_attend(dp, fsdp, tokens, vis, everything, small, upt, dn, locality, images):
    b, slots, d = tokens.shape
    heads = locality.shape[1]
    keys = up16(slots)
    n = images * PITCH
    u = d // dp
    rows = everything.shape[2]
    ring = dp if fsdp <= 4 else 2
    feed_rows = 2 * up16(upt.shape[0])

    def whole(shape):
        return pl.BlockSpec(shape, lambda g: (0,) * len(shape), pipeline_mode=pl.Buffered(1))

    def per(shape):
        return pl.BlockSpec((images,) + shape, lambda g: (g,) + (0,) * len(shape))

    kept_shapes = [(d, PITCH), (3 * d, PITCH), (heads, keys, PITCH), (heads, keys, PITCH), (d, PITCH)]
    scratch = [
        ((PITCH, PITCH), bf16),
        ((fsdp * 128, d), bf16),
        ((d, 2 * d), bf16),
        ((d, 2 * d), bf16),
        ((rows, fsdp * 128), f32),
        ((ring, fsdp, rows, 128), bf16),
        ((3, d, fsdp * 128), f32),
        ((feed_rows, 128), f32),
        ((feed_rows, 128), bf16),
        ((3 * d, d), bf16),
        ((2, d, 128), f32),
        ((PITCH, d), bf16),
        ((heads, keys, PITCH), f32),
        ((d, n), bf16),
        ((keys, d), bf16),
        ((heads, PITCH, PITCH), bf16),
        ((2, keys, PITCH), f32),
        ((heads, PITCH, PITCH), bf16),
    ]
    outs = pl.pallas_call(
        partial(attend_kernel, images, slots, heads, dp, fsdp, b // images),
        grid=(b // images,),
        out_shape=[jax.ShapeDtypeStruct((b,) + shape, bf16) for shape in kept_shapes]
        + [
            jax.ShapeDtypeStruct((2, d, d), bf16),
            jax.ShapeDtypeStruct((d, d), bf16),
            jax.ShapeDtypeStruct((dp, fsdp, feed_rows, 128), bf16),
        ],
        in_specs=[
            pl.BlockSpec(memory_space=pltpu.SMEM),
            per((slots, d)),
            per((1, PITCH)),
            pl.BlockSpec(memory_space=pl.ANY),
            whole(small.shape),
            whole(upt.shape),
            whole(dn.shape),
        ],
        out_specs=[per(shape) for shape in kept_shapes]
        + [whole((2, d, d)), whole((d, d)), pl.BlockSpec(memory_space=pl.ANY)],
        scratch_shapes=[pltpu.VMEM(*entry) for entry in scratch]
        + [
            pltpu.SemaphoreType.DMA((ring,)),
            pltpu.SemaphoreType.DMA((1,)),
            pltpu.SemaphoreType.DMA((len(gatherer_keys(*shape_of(dp, fsdp))),)),
            pltpu.SemaphoreType.DMA((dp * fsdp, 2)),
        ],
        compiler_params=pltpu.CompilerParams(
            dimension_semantics=("arbitrary",),
            collective_id=2,
            has_side_effects=True,
            vmem_limit_bytes=62 * 1024 * 1024,
        ),
        cost_estimate=pl.CostEstimate(flops=20_000_000_000, bytes_accessed=70_000_000, transcendentals=0),
    )(locality, tokens, vis, everything, small, upt, dn)
    return outs


def feed_kernel(
    images,
    slots,
    cot_ref,
    vis_ref,
    xt_ref,
    mixture_ref,
    all_ref,
    feed_ref,
    small_ref,
    res_ref,
    dot_ref,
    mg_ref,
    part_ref,
    gsmall_ref,
    eye,
    pick,
    chunk_s,
    chunk_sem,
    o_s,
    wot_s,
    wo_s,
    wupt_s,
    wup_s,
    wdnt_s,
    wdn_s,
    vec_s,
    upb_s,
    pad_in,
    acc_out,
    acc_up,
    acc_down,
    acc_vec,
    acc_upb,
    mixture_s,
    xh2_s,
    rstd_s,
    second_s,
    mid_s,
    cot_s,
    dlow_s,
    up_s,
    back_s,
    act_s,
    ug_s,
    blow_s,
):
    d = cot_ref.shape[-1]
    ff = upb_s.shape[0]
    dp, fsdp, o_at, _ = feed_ref.shape
    u, w = d // dp, d // fsdp
    fu = ff // dp
    dn_at = up16(fu)
    ring = chunk_s.shape[0]
    fits = ring == dp
    split = row_plan(fu, u)[1]
    few = o_s.shape[2]
    n = images * PITCH
    step = pl.program_id(0)

    @pl.when(step == 0)
    def _():
        def fetch(k):
            return pltpu.make_async_copy(
                feed_ref.at[k], chunk_s.at[k % ring, :, pl.ds(0, o_at)], chunk_sem.at[k % ring]
            )

        for k in range(ring):
            fetch(k).start()
        rest = pltpu.make_async_copy(all_ref.at[:, :, pl.ds(0, few)], o_s, chunk_sem.at[ring])
        rest.start()
        eye[...] = identity()
        pad_in[...] = jnp.zeros_like(pad_in)
        pick[...] = one_hot(pick.shape, w, lambda block, lane: block * w + lane)

        def unpack(k, _):
            fetch(k).wait()


            def joined(at):
                return jnp.concatenate([chunk_s[k % ring, f, at : at + fu] for f in range(fsdp)], axis=1)

            big = slice(fu * k, fu * (k + 1))
            acc_up[big, :] = mm(joined(0), pick[...])
            acc_down[big, :] = mm(joined(dn_at), pick[...])
            if k + ring < dp:
                fetch(k + ring).start()
            return 0

        if fits:
            for k in range(dp):
                fetch(k).wait()
                for f in range(fsdp):
                    act_s[fu * k : fu * (k + 1), 128 * f : 128 * (f + 1)] = chunk_s[k, f, 0:fu]
                    ug_s[fu * k : fu * (k + 1), 128 * f : 128 * (f + 1)] = chunk_s[k, f, dn_at : dn_at + fu]
            wupt_s[...] = mm(act_s[...], pick[...]).astype(bf16)
            wdn_s[...] = mm(ug_s[...], pick[...]).astype(bf16)
        else:
            for k in range(dp):
                unpack(k, 0)
            wupt_s[...] = acc_up[...].astype(bf16)
            wdn_s[...] = acc_down[...].astype(bf16)
        turned(eye, wupt_s, wup_s)
        turned(eye, wdn_s, wdnt_s)
        rest.wait()
        for k in range(dp):
            joined = jnp.concatenate([o_s[k, f, 0:u] for f in range(fsdp)], axis=1)
            if fits:
                mid_s[u * k : u * (k + 1), :] = joined.astype(f32)
            else:
                acc_out[u * k : u * (k + 1), :] = mm(joined, pick[...])
        wot_s[...] = (mm(mid_s[...].astype(bf16), pick[...]) if fits else acc_out[...]).astype(bf16)
        turned(eye, wot_s, wo_s)
        for f in range(fsdp):
            for r in range(2, 6):
                vec_s[r, w * f : w * (f + 1), :] = column(small_ref[f, r : r + 1, :])[0:w]
            for r in range(ff // d):
                at = (f * (ff // d) + r) * w
                upb_s[at : at + w, :] = column(small_ref[f, 6 + r : 7 + r, :])[0:w]
        for ref in (acc_out, acc_up, acc_down, acc_vec, acc_upb):
            ref[...] = jnp.zeros_like(ref)

    tiles = [slice(128 * k, 128 * (k + 1)) for k in range(n // 128)]

    def seen(t):
        at = 128 * t
        return vis_ref[at // PITCH, 0:1, at % PITCH : at % PITCH + 128]

    def fold(v):
        total = v[:, 0:128]
        for k in range(1, n // 128):
            total = total + v[:, 128 * k : 128 * (k + 1)]
        return total

    def enter(b, _):
        cols = pl.ds(pl.multiple_of(b * PITCH, PITCH), PITCH)
        turn_in(cot_ref, b, eye, pad_in, cot_s.at[:, cols])
        mixture_s[:, cols] = mixture_ref[b]
        return 0

    lax.fori_loop(0, images, enter, 0)

    def x_tile(t):
        at = 128 * t
        return xt_ref[at // PITCH, :, at % PITCH : at % PITCH + 128].astype(f32)

    for t, tile in enumerate(tiles):
        down = cot_s[:, tile].astype(f32) * seen(t)
        dlow_s[:, tile] = down.astype(bf16)
        acc_vec[3] += down
    mid_s[...] = mm(wot_s[...], mixture_s[...])
    for t, tile in enumerate(tiles):
        middle = x_tile(t) + seen(t) * (mid_s[:, tile] + vec_s[4])
        mid_s[:, tile] = middle
        normal, rstd = norm_stats(middle)
        xh2_s[:, tile] = normal
        rstd_s[0:1, tile] = rstd
        second_s[:, tile] = (normal * vec_s[2] + vec_s[3]).astype(bf16)

    chunk = up_s.shape[1]
    steps = ff // chunk

    def feed_start(c):
        part = slice(c * chunk, (c + 1) * chunk)
        up_s[c % 2] = mm(wupt_s[part, :], second_s[...])
        back_s[c % 2] = mm(wdn_s[part, :], dlow_s[...])

    feed_start(0)
    for c in range(steps):
        if c + 1 < steps:
            feed_start(c + 1)
        part = slice(c * chunk, (c + 1) * chunk)
        act, slope = gelu_parts(up_s[c % 2] + jnp.concatenate([upb_s[part, :]] * (n // 128), axis=1))
        act_s[part, :] = act.astype(bf16)
        ug = (back_s[c % 2] * slope).astype(bf16)
        ug_s[part, :] = ug
        acc_upb[part, :] += fold(ug.astype(f32))

    second_grad = mm(wup_s[...], ug_s[...])
    acc_up[...] += mm_nt(ug_s[...], second_s[...])
    for t, tile in enumerate(tiles):
        grad = second_grad[:, tile]
        normal = xh2_s[:, tile]
        acc_vec[0] += grad * normal
        acc_vec[1] += grad
        middle_grad = cot_s[:, tile].astype(f32) + norm_back(grad, vec_s[2], normal, rstd_s[0:1, tile])
        at = 128 * t
        mg_ref[at // PITCH, :, at % PITCH : at % PITCH + 128] = middle_grad.astype(bf16)
        low = (seen(t) * middle_grad).astype(bf16)
        blow_s[:, tile] = low
        acc_vec[2] += low.astype(f32)
    acc_down[...] += mm_nt(act_s[...], dlow_s[...])
    mixture_grad = mm(wo_s[...], blow_s[...]).astype(bf16)
    for b in range(images):
        dot_ref[b] = mixture_grad[:, PITCH * b : PITCH * (b + 1)]
    acc_out[...] += mm_nt(blow_s[...], mixture_s[...])
    downward = mm(wdnt_s[...], act_s[...])
    for t, tile in enumerate(tiles):
        dlow_s[:, tile] = (mid_s[:, tile] + seen(t) * (downward[:, tile] + vec_s[5])).astype(bf16)
    for b in range(images):
        res_ref[b] = mm_nt(eye[0:slots, :], dlow_s[:, b * PITCH : (b + 1) * PITCH]).astype(bf16)

    @pl.when(step == pl.num_programs(0) - 1)
    def _():
        def put_rest(k):
            return pltpu.make_async_copy(
                chunk_s.at[k % 2, :, pl.ds(0, split - o_at)],
                part_ref.at[k, :, pl.ds(o_at, split - o_at)],
                chunk_sem.at[k % 2],
            )

        chunk_s[...] = jnp.zeros_like(chunk_s)
        for k in [] if fits else range(dp):
            piece = mm_nt(acc_out[u * k : u * (k + 1), :].astype(bf16), pick[...]).astype(bf16)
            if k >= 2:
                put_rest(k - 2).wait()
            for f in range(fsdp):
                chunk_s[k % 2, f, 0:u] = piece[:, 128 * f : 128 * (f + 1)]
            put_rest(k).start()
        for k in [] if fits else range(max(dp - 2, 0), dp):
            put_rest(k).wait()
        def put(k):
            if fits:
                return pltpu.make_async_copy(chunk_s.at[k], part_ref.at[k], chunk_sem.at[k])
            return pltpu.make_async_copy(
                chunk_s.at[k % 2, :, pl.ds(0, o_at)], part_ref.at[k, :, pl.ds(0, o_at)], chunk_sem.at[k % 2]
            )

        def pack(k, _):
            big = slice(fu * k, fu * (k + 1))

            if k >= 2:
                put(k - 2).wait()

            for at, ref in ((0, acc_up), (dn_at, acc_down)):
                piece = mm_nt(ref[big, :].astype(bf16), pick[...]).astype(bf16)
                for f in range(fsdp):
                    chunk_s[k % 2, f, at : at + fu] = piece[:, 128 * f : 128 * (f + 1)]
            put(k).start()
            return 0

        if fits:
            act_s[...] = mm_nt(acc_up[...].astype(bf16), pick[...]).astype(bf16)
            ug_s[...] = mm_nt(acc_down[...].astype(bf16), pick[...]).astype(bf16)
            mid_s[...] = mm_nt(acc_out[...].astype(bf16), pick[...])
            for k in range(dp):
                for f in range(fsdp):
                    lane = slice(128 * f, 128 * (f + 1))
                    chunk_s[k, f, 0:fu] = act_s[fu * k : fu * (k + 1), lane]
                    chunk_s[k, f, dn_at : dn_at + fu] = ug_s[fu * k : fu * (k + 1), lane]
                    chunk_s[k, f, o_at : o_at + u] = mid_s[u * k : u * (k + 1), lane].astype(bf16)
                put(k).start()
        else:
            for k in range(dp):
                pack(k, 0)
        for k in range(0 if fits else max(dp - 2, 0), dp):
            put(k).wait()

        gsmall_ref[...] = jnp.zeros_like(gsmall_ref)
        for f in range(fsdp):
            for r in range(4):
                gsmall_ref[f, 2 + r : 3 + r, 0:w] = lane_sums(acc_vec[r, w * f : w * (f + 1), :])
            for r in range(ff // d):
                lo = (f * (ff // d) + r) * w
                gsmall_ref[f, 6 + r : 7 + r, 0:w] = lane_sums(acc_upb[lo : lo + w, :])


def run_feed(dp, fsdp, cotangent, vis, xt, mixture, everything, feed, small, ff, images):
    b, slots, d = cotangent.shape
    n = images * PITCH
    o_at, split, _ = row_plan(ff // dp, d // dp)
    few = up16(d // dp)
    ring = dp if n == fsdp * 128 else 2

    def whole(shape):
        return pl.BlockSpec(shape, lambda g: (0,) * len(shape), pipeline_mode=pl.Buffered(1))

    def per(shape):
        return pl.BlockSpec((images,) + shape, lambda g: (g,) + (0,) * len(shape))

    scratch = [
        ((PITCH, PITCH), bf16),
        ((fsdp * 128, d), bf16),
        ((ring, fsdp, split if ring == dp else o_at, 128), bf16),
        None,
        ((dp, fsdp, few, 128), bf16),
        ((d, d), bf16),
        ((d, d), bf16),
        ((ff, d), bf16),
        ((d, ff), bf16),
        ((d, ff), bf16),
        ((ff, d), bf16),
        ((6, d, 128), f32),
        ((ff, 128), f32),
        ((PITCH, d), bf16),
        ((d, d), f32),
        ((ff, d), f32),
        ((ff, d), f32),
        ((4, d, 128), f32),
        ((ff, 128), f32),
        ((d, n), bf16),
        ((d, n), f32),
        ((8, n), f32),
        ((d, n), bf16),
        ((d, n), f32),
        ((d, n), bf16),
        ((d, n), bf16),
        ((2, ff // 6, n), f32),
        ((2, ff // 6, n), f32),
        ((ff, n), bf16),
        ((ff, n), bf16),
        ((d, n), bf16),
    ]
    scratch = [pltpu.SemaphoreType.DMA((ring + 1,)) if entry is None else pltpu.VMEM(*entry) for entry in scratch]
    return pl.pallas_call(
        partial(feed_kernel, images, slots),
        grid=(b // images,),
        out_shape=[
            jax.ShapeDtypeStruct((b, slots, d), bf16),
            jax.ShapeDtypeStruct((b, d, PITCH), bf16),
            jax.ShapeDtypeStruct((b, d, PITCH), bf16),
            jax.ShapeDtypeStruct((dp, fsdp, split, 128), bf16),
            jax.ShapeDtypeStruct((fsdp, 16, 128), f32),
        ],
        in_specs=[per((slots, d)), per((1, PITCH)), per((d, PITCH)), per((d, PITCH))]
        + [pl.BlockSpec(memory_space=pl.ANY)] * 2
        + [whole((fsdp, 16, 128))],
        out_specs=[per((slots, d)), per((d, PITCH)), per((d, PITCH)), pl.BlockSpec(memory_space=pl.ANY), whole((fsdp, 16, 128))],
        scratch_shapes=scratch,
        compiler_params=pltpu.CompilerParams(
            dimension_semantics=("arbitrary",), vmem_limit_bytes=63 * 1024 * 1024
        ),
        cost_estimate=pl.CostEstimate(flops=40_000_000_000, bytes_accessed=40_000_000, transcendentals=0),
    )(cotangent, vis, xt, mixture, everything, feed, small)


class Reducer:
    def __init__(self, here, rows, mine, theirs, other, bufs, send, recv):
        self.here, self.mine, self.theirs, self.other = here, mine, theirs, other
        self.got_x, self.got_y, self.got_x2, self.got_y2, self.got_z = bufs
        self.send, self.recv = send, recv
        half = rows // 32 * 16
        self.segs = (pl.ds(0, half), pl.ds(half, rows - half))
        self.order = z_order(here.zs)
        self.keys = reducer_keys(here.zs, here.ys, here.xs, here.cores)

    def f_at(self, dy, dx):
        return self.here.to(dy=dy, dx=dx)[1]

    def copy(self, key):
        here, segs, n = self.here, self.segs, key[1]
        if key[0] == "pair":
            src, dst, target = self.theirs(n), self.other.at[n], here.to(dc=1)
        elif key[0] == "a1":
            _, _, a, b = key
            src, dst, target = self.mine(n).at[self.f_at(a, b), segs[0]], self.got_x.at[n, a, b - 1], here.to(dx=b)
        elif key[0] == "b1":
            _, _, a, b = key
            src, dst, target = self.mine(n).at[self.f_at(a, b), segs[1]], self.got_y.at[n, b, a - 1], here.to(dy=a)
        elif key[0] == "a2":
            src, dst, target = self.mine(n).at[self.f_at(key[2], 0), segs[0]], self.got_y2.at[n, key[2] - 1], here.to(dy=key[2])
        elif key[0] == "b2":
            src, dst, target = self.mine(n).at[self.f_at(0, key[2]), segs[1]], self.got_x2.at[n, key[2] - 1], here.to(dx=key[2])
        else:
            seg = segs[key[2]]
            src, dst, target = self.mine(n).at[self.f_at(0, 0), seg], self.got_z.at[n, seg], here.to(dz=self.order[n])
        at = self.keys.index(key)
        return pltpu.make_async_remote_copy(
            src_ref=src, dst_ref=dst, send_sem=self.send.at[at], recv_sem=self.recv.at[at], device_id=target, device_id_type=MESH
        )

    def add(self, n, f, seg, got):
        ref = self.mine(n)
        ref[f, self.segs[seg]] = (ref[f, self.segs[seg]].astype(f32) + got.astype(f32)).astype(bf16)

    def begin(self):
        if self.here.cores > 1:
            for n in range(self.here.zs):
                self.copy(("pair", n)).start()

    def stage_one(self, n):
        here = self.here
        if here.cores > 1:
            self.copy(("pair", n)).wait_recv()
            ref = self.mine(n)

            def body(f, _):
                ref[f] = (ref[f].astype(f32) + self.other[n, f].astype(f32)).astype(bf16)
                return 0

            lax.fori_loop(0, here.fs, body, 0)
        for a in list(range(1, here.ys)) + [0]:
            for b in range(1, here.xs):
                self.copy(("a1", n, a, b)).start()
        for b in list(range(1, here.xs)) + [0]:
            for a in range(1, here.ys):
                self.copy(("b1", n, a, b)).start()

    def stage_two(self, n):
        here = self.here
        for a in list(range(1, here.ys)) + [0]:
            for b in range(1, here.xs):
                self.copy(("a1", n, a, b)).wait_recv()
                self.add(n, self.f_at(a, 0), 0, self.got_x[n, a, b - 1])
            if a:
                self.copy(("a2", n, a)).start()
        for b in list(range(1, here.xs)) + [0]:
            for a in range(1, here.ys):
                self.copy(("b1", n, a, b)).wait_recv()
                self.add(n, self.f_at(0, b), 1, self.got_y[n, b, a - 1])
            if b:
                self.copy(("b2", n, b)).start()

    def stage_three(self, n):
        here = self.here
        for a in range(1, here.ys):
            self.copy(("a2", n, a)).wait_recv()
            self.add(n, self.f_at(0, 0), 0, self.got_y2[n, a - 1])
        for b in range(1, here.xs):
            self.copy(("b2", n, b)).wait_recv()
            self.add(n, self.f_at(0, 0), 1, self.got_x2[n, b - 1])
        if self.order[n]:
            for seg in (0, 1):
                self.copy(("z", n, seg)).start()

    def turn(self, t):
        zs = self.here.zs
        if t < zs:
            self.stage_one(t)
        if 1 <= t <= zs:
            self.stage_two(t - 1)
        if 2 <= t < zs + 2:
            self.stage_three(t - 2)

    def total(self):
        zs = self.here.zs
        total = self.mine(zs - 1)[self.f_at(0, 0)].astype(f32)
        for n in range(zs - 1):
            for seg in (0, 1):
                self.copy(("z", n, seg)).wait_recv()
            total = total + self.got_z[n].astype(f32)
        return total

    def finish(self):
        for key in self.keys:
            self.copy(key).wait_send()


def z_order(zs):
    return sorted(range(1, zs), key=lambda k: min(k, zs - k)) + [0]


def reducer_keys(zs, ys, xs, cores):
    keys = []
    for n in range(zs):
        if cores > 1:
            keys.append(("pair", n))
        keys += [("a1", n, a, b) for a in range(ys) for b in range(1, xs)]
        keys += [("b1", n, a, b) for a in range(1, ys) for b in range(xs)]
        keys += [("a2", n, a) for a in range(1, ys)] + [("b2", n, b) for b in range(1, xs)]
        if n < zs - 1:
            keys += [("z", n, 0), ("z", n, 1)]
    return keys


def reducer_buffers(zs, ys, xs, rows):
    half = rows // 32 * 16
    rest = rows - half
    return [
        pltpu.VMEM((zs, ys, max(xs - 1, 1), half, 128), bf16),
        pltpu.VMEM((zs, xs, max(ys - 1, 1), rest, 128), bf16),
        pltpu.VMEM((zs, max(xs - 1, 1), rest, 128), bf16),
        pltpu.VMEM((zs, max(ys - 1, 1), half, 128), bf16),
        pltpu.VMEM((zs, rows, 128), bf16),
    ]


def exchange(here, ref, buf, send, recv, base, coordinate, size, targets):
    buf[base + coordinate] = ref[...]
    for k, target in enumerate(targets):
        pltpu.make_async_remote_copy(
            src_ref=ref,
            dst_ref=buf.at[base + coordinate],
            send_sem=send.at[base + k],
            recv_sem=recv.at[base + coordinate],
            device_id=target,
            device_id_type=MESH,
        ).start()

    def add():
        for k in range(1, size):
            pltpu.make_async_remote_copy(
                src_ref=ref,
                dst_ref=buf.at[base + coordinate],
                send_sem=send.at[base + k - 1],
                recv_sem=recv.at[base],
                device_id=here.to(),
                device_id_type=MESH,
            ).wait_send()
        for k in range(1, size):
            at = base + lax.rem(coordinate + k, size)
            pltpu.make_async_remote_copy(
                src_ref=ref,
                dst_ref=buf.at[at],
                send_sem=send.at[base],
                recv_sem=recv.at[at],
                device_id=here.to(),
                device_id_type=MESH,
            ).wait_recv()
        total = buf[base]
        for k in range(1, size):
            total = total + buf[base + k]
        ref[...] = total

    return add


def backward_kernel(
    images,
    slots,
    heads,
    dp,
    fsdp,
    ff,
    total_steps,
    locality_ref,
    xt_ref,
    qkvt_ref,
    pa_ref,
    pb_ref,
    dot_ref,
    mg_ref,
    small_ref,
    gsmall_ref,
    wqk_ref,
    wv_ref,
    part_ref,
    tgrad_ref,
    grad_ref,
    sum_ref,
    norm_ref,
    eye,
    pick,
    perm,
    cat_s,
    whole_s,
    vec_s,
    acc_qk,
    acc_v,
    acc_vec,
    acc_place,
    acc_gate,
    hid_s,
    xh_s,
    rstd_s,
    vn_s,
    win_s,
    sc_s,
    mix_s,
    ds_s,
    dqkv_s,
    tg_s,
    last_s,
    a_mine,
    a_other,
    a_x,
    a_y,
    a_x2,
    a_y2,
    a_z,
    b_other,
    b_x,
    b_y,
    b_x2,
    b_y2,
    b_z,
    small_buf,
    norm_buf,
    load,
    a_send,
    a_recv,
    b_send,
    b_recv,
    sm_send,
    sm_recv,
    nm_send,
    nm_recv,
):
    d = xt_ref.shape[1]
    u, w = d // dp, d // fsdp
    _, split, rows_all = row_plan(ff // dp, u)
    hw = d // heads
    keys = acc_place.shape[1]
    n = images * PITCH
    scale = hw**-0.5
    fits = fsdp <= 4
    step = pl.program_id(0)
    count = pl.num_programs(0)
    here = Place(dp, fsdp)
    zs, ys, xs, cores = here.zs, here.ys, here.xs, here.cores
    order = z_order(zs)

    def plane(k, dc=0):
        return here.to(dz=order[k], dc=dc)[0]

    first = Reducer(
        here,
        split,
        lambda k: a_mine.at[k],
        lambda k: part_ref.at[plane(k, 1)],
        a_other,
        (a_x, a_y, a_x2, a_y2, a_z),
        a_send,
        a_recv,
    )
    last = Reducer(
        here,
        rows_all - split,
        lambda k: last_s.at[plane(k)],
        lambda k: last_s.at[plane(k, 1)],
        b_other,
        (b_x, b_y, b_x2, b_y2, b_z),
        b_send,
        b_recv,
    )

    def loading(k):
        return pltpu.make_async_copy(part_ref.at[plane(k)], a_mine.at[k], load.at[k])

    @pl.when(step == 0)
    def _():
        for k in range(zs):
            loading(k).start()
        peers = [here.to(dz=k) for k in range(1, zs)] + [here.to(dc=k) for k in range(1, cores)]
        peers += [here.to(dy=a, dx=b) for a in range(ys) for b in range(xs) if a or b]
        peers = [
            here.to(dz=k, dc=c, dy=a, dx=b)
            for k in range(zs)
            for c in range(cores)
            for a in range(ys)
            for b in range(xs)
            if k or c or a or b
        ]
        greet(peers)
        first.begin()
        eye[...] = identity()
        pick[...] = one_hot(pick.shape, w, lambda block, lane: block * w + lane)
        e = lax.broadcasted_iota(jnp.int32, (2 * d, 1), 0)
        goal = (e % (2 * w)) // w * d + e // (2 * w) * w + e % w
        perm[...] = jnp.where(lax.broadcasted_iota(jnp.int32, perm.shape, 1) == goal, 1.0, 0.0).astype(bf16)
        for f in range(fsdp):
            for r in range(2):
                vec_s[r, w * f : w * (f + 1), :] = column(small_ref[f, r : r + 1, :])[0:w]
        for ref in (acc_qk, acc_v, acc_vec, acc_place, acc_gate, win_s, mix_s, ds_s):
            ref[...] = jnp.zeros_like(ref)
        for k in range(zs):
            loading(k).wait()

    spread = total_steps
    for t in range(zs + 2):

        @pl.when(step == min(t + 1, spread - 1))
        def _(t=t):
            first.turn(t)

    sig, cosig = gates(locality_ref, heads)
    wins = windows(heads, hw, d)
    tiles = [slice(128 * k, 128 * (k + 1)) for k in range(n // 128)]

    def place_of(t):
        at = 128 * t
        return at // PITCH, slice(at % PITCH, at % PITCH + 128)

    for t, tile in enumerate(tiles):
        b, lane = place_of(t)
        normal, rstd = norm_stats(xt_ref[b, :, lane].astype(f32))
        xh_s[:, tile] = normal
        rstd_s[0:1, tile] = rstd
        hid_s[:, tile] = (normal * vec_s[0] + vec_s[1]).astype(bf16)

    def backward(b, _):
        cols = pl.ds(pl.multiple_of(b * PITCH, PITCH), PITCH)
        vn_s[...] = mm_nt(eye[0:keys, :], qkvt_ref[b, 2 * d : 3 * d, :]).astype(bf16)

        def ba(h):
            lo, hi, at = wins[h]
            win_s[h, at : at + hw, :] = dot_ref[b, h * hw : (h + 1) * hw, :]
            sc_s[h % 2] = mm(vn_s[:, lo:hi], win_s[h, 0 : hi - lo, :])

        def bb(h):
            g = sc_s[h % 2]
            pa = pa_ref[b, h].astype(f32)
            pb = pb_ref[b, h].astype(f32)
            mix_s[h, 0:keys, :] = pa_ref[b, h] + pb_ref[b, h]
            pull_a = jnp.sum(g * pa, axis=0, keepdims=True) / cosig[h]
            pull_b = jnp.sum(g * pb, axis=0, keepdims=True) / sig[h]
            acc_gate[h : h + 1, :] += pull_b - pull_a
            acc_place[h] += pb * (g - pull_b)
            ds_s[h, 0:keys, :] = (pa * (g - pull_a)).astype(bf16)

        def bc(h):
            rows = slice(h * hw, (h + 1) * hw)
            dqkv_s[rows, cols] = (mm(qkvt_ref[b, d + h * hw : d + (h + 1) * hw, :], ds_s[h]) * scale).astype(bf16)
            dqkv_s[d + h * hw : d + (h + 1) * hw, cols] = (mm_nt(qkvt_ref[b, rows, :], ds_s[h]) * scale).astype(bf16)
            dqkv_s[2 * d + h * hw : 2 * d + (h + 1) * hw, cols] = mm_nt(dot_ref[b, rows, :], mix_s[h]).astype(bf16)

        for t in range(heads + 2):
            if t < heads:
                ba(t)
            if t >= 2:
                bc(t - 2)
            if 1 <= t <= heads:
                bb(t - 1)
        return 0

    lax.fori_loop(0, images, backward, 0)

    back = mm(wqk_ref[0], dqkv_s[0:d, :]) + mm(wqk_ref[1], dqkv_s[d : 2 * d, :]) + mm(wv_ref[...], dqkv_s[2 * d : 3 * d, :])
    acc_qk[...] += mm_nt(hid_s[...], dqkv_s[0 : 2 * d, :])
    for t, tile in enumerate(tiles):
        b, lane = place_of(t)
        grad = back[:, tile]
        normal = xh_s[:, tile]
        acc_vec[0] += grad * normal
        acc_vec[1] += grad
        pulled = norm_back(grad, vec_s[0], normal, rstd_s[0:1, tile])
        tg_s[:, tile] = (mg_ref[b, :, lane].astype(f32) + pulled).astype(bf16)
    acc_v[...] += mm_nt(dqkv_s[2 * d : 3 * d, :], hid_s[...])
    for b in range(images):
        tgrad_ref[b] = mm_nt(eye[0:slots, :], tg_s[:, b * PITCH : (b + 1) * PITCH]).astype(bf16)

    @pl.when(step == count - 1)
    def _():
        cat_s[...] = jnp.zeros_like(cat_s)
        acc_qk[...] = mm(acc_qk[...].astype(bf16), perm[...])
        if fits:
            whole_s[0] = mm_nt(acc_v[...].astype(bf16), pick[...])
            whole_s[1] = mm_nt(acc_qk[:, 0:d].astype(bf16), pick[...])
            whole_s[2] = mm_nt(acc_qk[:, d : 2 * d].astype(bf16), pick[...])
        for k in range(dp):
            own = slice(u * k, u * (k + 1))
            if fits:
                for p in range(3):
                    cat_s[p * u : (p + 1) * u, :] = whole_s[p, own, :]
            else:
                cat_s[0:u, :] = mm_nt(acc_v[own, :].astype(bf16), pick[...])
                cat_s[u : 2 * u, :] = mm_nt(acc_qk[own, 0:d].astype(bf16), pick[...])
                cat_s[2 * u : 3 * u, :] = mm_nt(acc_qk[own, d : 2 * d].astype(bf16), pick[...])
            for f in range(fsdp):
                last_s[k, f] = cat_s[:, 128 * f : 128 * (f + 1)].astype(bf16)
        last.begin()

        sum_ref[...] = gsmall_ref[...]
        for f in range(fsdp):
            for r in range(2):
                sum_ref[f, r : r + 1, 0:w] = lane_sums(acc_vec[r, w * f : w * (f + 1), :])
        at = 6 + ff // d
        dc, dr, far = offset_planes(keys)
        rows = [[], [], []]
        for h in range(heads):
            pg = acc_place[h]
            for c, off in enumerate((dc, dr, far)):
                rows[c].append(jnp.sum(pg * off, axis=0, keepdims=True))
            acc_gate[h : h + 1, :] = acc_gate[h : h + 1, :] * (sig[h] * cosig[h])
        sum_ref[0, at + 3 : at + 4, 0 : acc_gate.shape[0]] = lane_sums(acc_gate[...])
        for c in range(3):
            for h in range(heads):
                acc_gate[h : h + 1, :] = rows[c][h]
            sum_ref[0, at + c : at + c + 1, 0 : acc_gate.shape[0]] = lane_sums(acc_gate[...])


        def small_round(base, coordinate, size, targets):
            return exchange(here, sum_ref, small_buf, sm_send, sm_recv, base, coordinate, size, targets)

        pending = small_round(0, here.c, cores, [here.to(dc=k) for k in range(1, cores)])
        total = first.total()
        grad_ref[0:split, :] = total
        squares = jnp.sum((total * total).reshape(split // 8, 8, 128), axis=0)
        for t in range(zs + 2):
            last.turn(t)
            if t == 0:
                pending()
                pending = small_round(cores, here.x, xs, [here.to(dx=b) for b in range(1, xs)])
            if t == 1:
                pending()
                pending = small_round(cores + xs, here.y, ys, [here.to(dy=a) for a in range(1, ys)])
            if t == 2:
                pending()
                pending = small_round(cores + xs + ys, here.z, zs, [here.to(dz=q) for q in range(1, zs)])
        pending()
        total = last.total()
        grad_ref[split:rows_all, :] = total
        norm_ref[...] = squares + jnp.sum((total * total).reshape((rows_all - split) // 8, 8, 128), axis=0)
        at = here.to()
        everyone = [
            here.to(dz=k, dc=c, dy=a, dx=b)
            for k in range(zs)
            for c in range(cores)
            for a in range(ys)
            for b in range(xs)
            if k or c or a or b
        ]
        exchange(here, norm_ref, norm_buf, nm_send, nm_recv, 0, at[0] * fsdp + at[1], dp * fsdp, everyone)()
        first.finish()
        last.finish()


def run_backward(dp, fsdp, slots, kept, small, small_part, wqk, wv, first_part, locality, ff, images):
    b, d, _ = kept[0].shape
    heads = locality.shape[1]
    keys = kept[2].shape[2]
    n = images * PITCH
    _, split, rows = row_plan(ff // dp, d // dp)
    more = rows - split
    cores = 2 if dp % 2 == 0 else 1
    zs = dp // cores
    ys = max(v for v in range(1, fsdp + 1) if fsdp % v == 0 and v * v <= fsdp)
    xs = fsdp // ys
    copies = len(reducer_keys(zs, ys, xs, cores))
    rounds = cores + xs + ys + zs

    def whole(shape):
        return pl.BlockSpec(shape, lambda g: (0,) * len(shape), pipeline_mode=pl.Buffered(1))

    def per(shape):
        mode = pl.Buffered(1) if fsdp > 4 and shape[-1] == PITCH else None
        return pl.BlockSpec((images,) + shape, lambda g: (g,) + (0,) * len(shape), pipeline_mode=mode)

    scratch = [
        pltpu.VMEM((PITCH, PITCH), bf16),
        pltpu.VMEM((fsdp * 128, d), bf16),
        pltpu.VMEM((2 * d, 2 * d), bf16),
        pltpu.VMEM((more, fsdp * 128), f32),
        pltpu.VMEM((3, d, fsdp * 128) if fsdp <= 4 else (1, 8, 128), f32),
        pltpu.VMEM((2, d, 128), f32),
        pltpu.VMEM((d, 2 * d), f32),
        pltpu.VMEM((d, d), f32),
        pltpu.VMEM((2, d, 128), f32),
        pltpu.VMEM((heads, keys, PITCH), f32),
        pltpu.VMEM((-(-heads // 8) * 8, PITCH), f32),
        pltpu.VMEM((d, n), bf16),
        pltpu.VMEM((d, n), f32),
        pltpu.VMEM((8, n), f32),
        pltpu.VMEM((keys, d), bf16),
        pltpu.VMEM((heads, PITCH, PITCH), bf16),
        pltpu.VMEM((2, keys, PITCH), f32),
        pltpu.VMEM((heads, PITCH, PITCH), bf16),
        pltpu.VMEM((heads, PITCH, PITCH), bf16),
        pltpu.VMEM((3 * d, n), bf16),
        pltpu.VMEM((d, n), bf16),
        pltpu.VMEM((dp, fsdp, more, 128), bf16),
        pltpu.VMEM((zs, fsdp, split, 128), bf16),
        pltpu.VMEM((zs, fsdp, split, 128), bf16),
        *reducer_buffers(zs, ys, xs, split),
        pltpu.VMEM((zs, fsdp, more, 128), bf16),
        *reducer_buffers(zs, ys, xs, more),
        pltpu.VMEM((rounds,) + small.shape, f32),
        pltpu.VMEM((fsdp * dp, 8, 128), f32),
        pltpu.SemaphoreType.DMA((zs,)),
        pltpu.SemaphoreType.DMA((copies,)),
        pltpu.SemaphoreType.DMA((copies,)),
        pltpu.SemaphoreType.DMA((copies,)),
        pltpu.SemaphoreType.DMA((copies,)),
        pltpu.SemaphoreType.DMA((rounds,)),
        pltpu.SemaphoreType.DMA((rounds,)),
        pltpu.SemaphoreType.DMA((fsdp * dp,)),
        pltpu.SemaphoreType.DMA((fsdp * dp,)),
    ]
    return pl.pallas_call(
        partial(backward_kernel, images, slots, heads, dp, fsdp, ff, b // images),
        grid=(b // images,),
        out_shape=[
            jax.ShapeDtypeStruct((b, slots, d), bf16),
            jax.ShapeDtypeStruct((rows, 128), f32),
            jax.ShapeDtypeStruct(small.shape, f32),
            jax.ShapeDtypeStruct((8, 128), f32),
        ],
        in_specs=[pl.BlockSpec(memory_space=pltpu.SMEM)]
        + [per(v.shape[1:]) for v in kept]
        + [whole(small.shape), whole(small.shape), whole((2, d, d)), whole((d, d)), pl.BlockSpec(memory_space=pl.ANY)],
        out_specs=[per((slots, d)), whole((rows, 128)), whole(small.shape), whole((8, 128))],
        scratch_shapes=scratch,
        compiler_params=pltpu.CompilerParams(
            dimension_semantics=("arbitrary",),
            collective_id=1,
            has_side_effects=True,
            vmem_limit_bytes=63 * 1024 * 1024,
        ),
        cost_estimate=pl.CostEstimate(flops=25_000_000_000, bytes_accessed=70_000_000, transcendentals=0),
    )(locality, *kept, small, small_part, wqk, wv, first_part)


def adamw(parameter, moment_one, moment_two, gradient, rate, decay_rate):
    first_new = beta_one * moment_one + (1.0 - beta_one) * gradient
    second_new = beta_two * moment_two + (1.0 - beta_two) * gradient * gradient
    first_hat = first_new / (1.0 - beta_one**STEP)
    second_hat = second_new / (1.0 - beta_two**STEP)
    new_value = parameter - rate * (
        first_hat / (jnp.sqrt(second_hat) + adam_eps) + decay_rate * parameter
    )
    return (new_value, first_new, second_new)


def update_kernel(heads, *refs):
    grad_ref, small_ref, norm_ref = refs[0:3]
    states = [refs[3 + 3 * k : 6 + 3 * k] for k in range(8)]
    outs = refs[27:]
    small = small_ref[...]
    norm = jnp.sqrt(jnp.sum(norm_ref[...], keepdims=True) + jnp.sum(small * small, keepdims=True)[0])
    factor = clip_limit / jnp.maximum(norm, clip_limit)
    outs[0][...] = norm
    u, w = states[1][0].shape
    fu = states[3][0].shape[0]
    o_at, split, _ = row_plan(fu, u)
    starts = {1: split, 2: o_at, 3: 0, 4: up16(fu)}

    def matrix(k, state, gradient, place):
        new_value, first_new, second_new = adamw(
            state[0][place], state[1][place], state[2][place], gradient * factor, learn_rate, weight_decay
        )
        outs[1 + 4 * k][place] = new_value
        outs[2 + 4 * k][place] = new_value.astype(bf16)
        outs[3 + 4 * k][place] = first_new
        outs[4 + 4 * k][place] = second_new

    at = split + u
    gradient = jnp.concatenate([grad_ref[at : at + u, 0:w], grad_ref[at + u : at + 2 * u, 0:w]], axis=1)
    matrix(0, states[0], gradient, ...)
    for k in (1, 2, 3, 4):
        rows = states[k][0].shape[0]
        matrix(k, states[k], grad_ref[starts[k] : starts[k] + rows, 0:w], ...)
    mine = small_ref[lax.axis_index("fsdp")]
    share = states[6][0].shape[1] // w
    row = jnp.concatenate([mine[6 + r : 7 + r, 0:w] for r in range(share)], axis=1)
    gradients = (mine[0:6, 0:w], row, small_ref[0, 6 + share : 10 + share, 0:heads])
    for k in range(3):
        state = states[5 + k]
        new_value, first_new, second_new = adamw(
            state[0][...], state[1][...], state[2][...], gradients[k] * factor, small_rate, 0.0
        )
        outs[21 + 3 * k][...] = new_value
        outs[22 + 3 * k][...] = first_new
        outs[23 + 3 * k][...] = second_new


def update(heads, grad, small, norm, states):
    shapes = [jax.ShapeDtypeStruct((1, 1), f32)]
    for k in range(5):
        shape = states[3 * k].shape
        shapes += [jax.ShapeDtypeStruct(shape, kind) for kind in (f32, bf16, f32, f32)]
    for k in range(5, 8):
        shapes += [jax.ShapeDtypeStruct(states[3 * k].shape, f32)] * 3
    return pl.pallas_call(
        partial(update_kernel, heads),
        out_shape=shapes,
        in_specs=[pl.BlockSpec(memory_space=pltpu.VMEM)] * 27,
        out_specs=[pl.BlockSpec(memory_space=pltpu.VMEM)] * len(shapes),
        compiler_params=pltpu.CompilerParams(vmem_limit_bytes=62 * 1024 * 1024),
    )(grad, small, norm, *states)


def body(
    dp,
    fsdp,
    tokens,
    keep_mask,
    cotangent,
    qk_weight,
    qk_first,
    qk_second,
    value_weight,
    value_first,
    value_second,
    out_weight,
    out_first,
    out_second,
    up_weight,
    up_first,
    up_second,
    down_weight,
    down_first,
    down_second,
    vectors,
    vectors_first,
    vectors_second,
    up_bias,
    up_bias_first,
    up_bias_second,
    locality,
    locality_first,
    locality_second,
):
    d = tokens.shape[-1]
    heads = locality.shape[1]
    ff = up_bias.shape[0] * fsdp
    images = 2 if fsdp <= 4 else 1
    vis = jnp.pad(keep_mask.astype(f32), ((0, 0), (0, PITCH - tokens.shape[1])))[:, None, :]
    everything, small, tokens, cotangent = gather_all(
        dp,
        fsdp,
        up16(4 * d // dp),
        qk_weight,
        value_weight.T,
        out_weight.T,
        vectors,
        up_bias,
        tokens,
        cotangent,
    )
    xt, qkvt, pa, pb, mixture, wqk, wv, feed = run_attend(
        dp, fsdp, tokens, vis, everything, small, up_weight.T, down_weight, locality, images
    )
    result, mixture_grad, middle_grad, first_part, small_part = run_feed(
        dp, fsdp, cotangent, vis, xt, mixture, everything, feed, small, ff, images
    )
    kept = (xt, qkvt, pa, pb, mixture_grad, middle_grad)
    token_grad, grad, small_sum, norm = run_backward(
        dp, fsdp, tokens.shape[1], kept, small, small_part, wqk, wv, first_part, locality, ff, images
    )

    def flat(v):
        return v.reshape(1, -1)

    states = [qk_weight, qk_first, qk_second]
    states += [v.T for v in (value_weight, value_first, value_second, out_weight, out_first, out_second)]
    states += [v.T for v in (up_weight, up_first, up_second)]
    states += [down_weight, down_first, down_second, vectors, vectors_first, vectors_second]
    states += [flat(up_bias), flat(up_bias_first), flat(up_bias_second), locality, locality_first, locality_second]
    outs = list(update(heads, grad, small_sum, norm, states))
    for k in range(5, 17):
        outs[k] = outs[k].T
    for k in (24, 25, 26):
        outs[k] = outs[k].reshape(up_bias.shape)
    outs[0] = outs[0].reshape(())
    return (result, token_grad, *outs)


def solution(mesh):
    placed = (
        P(("dp", "fsdp"), None, None),
        P(("dp", "fsdp"), None),
        P(("dp", "fsdp"), None, None),
        P("dp", "fsdp"),
        P("dp", "fsdp"),
        P("dp", "fsdp"),
        P("fsdp", "dp"),
        P("fsdp", "dp"),
        P("fsdp", "dp"),
        P("fsdp", "dp"),
        P("fsdp", "dp"),
        P("fsdp", "dp"),
        P("fsdp", "dp"),
        P("fsdp", "dp"),
        P("fsdp", "dp"),
        P("dp", "fsdp"),
        P("dp", "fsdp"),
        P("dp", "fsdp"),
        P(None, "fsdp"),
        P(None, "fsdp"),
        P(None, "fsdp"),
        P("fsdp"),
        P("fsdp"),
        P("fsdp"),
        P(),
        P(),
        P(),
    )
    return jax.shard_map(
        partial(body, mesh.shape["dp"], mesh.shape["fsdp"]),
        mesh=mesh,
        in_specs=placed,
        out_specs=(
            P(("dp", "fsdp"), None, None),
            P(("dp", "fsdp"), None, None),
            P(),
            P("dp", "fsdp"),
            P("dp", "fsdp"),
            P("dp", "fsdp"),
            P("dp", "fsdp"),
            P("fsdp", "dp"),
            P("fsdp", "dp"),
            P("fsdp", "dp"),
            P("fsdp", "dp"),
            P("fsdp", "dp"),
            P("fsdp", "dp"),
            P("fsdp", "dp"),
            P("fsdp", "dp"),
            P("fsdp", "dp"),
            P("fsdp", "dp"),
            P("fsdp", "dp"),
            P("fsdp", "dp"),
            P("dp", "fsdp"),
            P("dp", "fsdp"),
            P("dp", "fsdp"),
            P("dp", "fsdp"),
            P(None, "fsdp"),
            P(None, "fsdp"),
            P(None, "fsdp"),
            P("fsdp"),
            P("fsdp"),
            P("fsdp"),
            P(),
            P(),
            P(),
        ),
        check_vma=False,
    )
```

```python
from functools import partial

import jax
import jax.numpy as jnp
from jax import lax
from jax.experimental import pallas as pl
from jax.experimental.pallas import tpu as pltpu
from jax.sharding import PartitionSpec as P

GRID = 14
STEP = 5
PITCH = 256

norm_eps = 1e-06
learn_rate = 0.03
small_rate = 0.3
beta_one = 0.5
beta_two = 0.5
adam_eps = 1e-08
weight_decay = 0.05
clip_limit = 1.0

LOG2E = 1.4426950408889634
PHI_ZERO = 0.3989422804014327

f32 = jnp.float32
bf16 = jnp.bfloat16


def mm(a, b):
    return lax.dot_general(a, b, (((1,), (0,)), ((), ())), preferred_element_type=f32)


def mm_nt(a, b):
    return lax.dot_general(a, b, (((1,), (1,)), ((), ())), preferred_element_type=f32)


def gelu_parts(u):
    v = u * 0.5**0.5
    cdf = 0.5 * lax.erf(v) + 0.5
    bell = jnp.exp2(v * v * -LOG2E)
    return u * cdf, cdf + (v * (PHI_ZERO * 2**0.5)) * bell


MESH = pl.DeviceIdType.MESH


def up16(v):
    return -(-v // 16) * 16


class Place:
    def __init__(self, dp, fsdp):
        self.cores = 2 if dp % 2 == 0 else 1
        self.zs = dp // self.cores
        self.ys = max(v for v in range(1, fsdp + 1) if fsdp % v == 0 and v * v <= fsdp)
        self.xs = fsdp // self.ys
        self.fs = fsdp
        at_dp, at_f = lax.axis_index("dp"), lax.axis_index("fsdp")
        self.z, self.c = at_dp // self.cores, at_dp % self.cores
        self.y, self.x = at_f // self.xs, at_f % self.xs

    def to(self, dz=0, dc=0, dy=0, dx=0):
        z = lax.rem(self.z + dz, self.zs)
        c = lax.rem(self.c + dc, self.cores)
        y = lax.rem(self.y + dy, self.ys)
        x = lax.rem(self.x + dx, self.xs)
        return (z * self.cores + c, y * self.xs + x)


def greet(peers):
    barrier = pltpu.get_barrier_semaphore()
    for peer in peers:
        pl.semaphore_signal(barrier, inc=1, device_id=peer, device_id_type=MESH)
    pl.semaphore_wait(barrier, len(peers))


def row_plan(fu, u):
    o_at = 2 * up16(fu)
    split = up16(o_at + u)
    return o_at, split, split + up16(3 * u)


class Gatherer:
    def __init__(self, here, rows, block, slots, send, recv):
        self.here, self.block, self.slots, self.send, self.recv = here, block, slots, send, recv
        half = rows // 32 * 16
        self.segs = (pl.ds(0, half), pl.ds(half, rows - half))
        self.keys = gatherer_keys(here.zs, here.ys, here.xs, here.cores)
        self.order = [0] + z_order(here.zs)[:-1]

    def slot(self, owner, seg):
        return self.slots.at[owner[0], owner[1], self.segs[seg]]

    def copy(self, key):
        here, kind, k, a, b, seg, to = self.here, *key
        owner = here.to(dz=k, dy=a, dx=b)
        own = (k, a, b) == (0, 0, 0)
        target = {"z": here.to(dz=to), "y": here.to(dy=to), "x": here.to(dx=to), "c": here.to(dc=to)}[kind]
        return pltpu.make_async_remote_copy(
            src_ref=self.block.at[self.segs[seg]] if own else self.slot(owner, seg),
            dst_ref=self.slot(owner, seg),
            send_sem=self.send.at[self.keys.index(key)],
            recv_sem=self.recv.at[owner[0] * here.fs + owner[1], seg],
            device_id=target,
            device_id_type=MESH,
        )

    def push(self, kind, k, a, b, seg):
        for key in self.keys:
            if key[:5] == (kind, k, a, b, seg):
                self.copy(key).start()

    def arrive(self, k, a, b, seg, dc=0):
        owner = self.here.to(dz=k, dy=a, dx=b, dc=dc)
        slot = self.slot(owner, seg)
        pltpu.make_async_remote_copy(
            src_ref=slot,
            dst_ref=slot,
            send_sem=self.send.at[0],
            recv_sem=self.recv.at[owner[0] * self.here.fs + owner[1], seg],
            device_id=self.here.to(),
            device_id_type=MESH,
        ).wait_recv()

    def spread(self, k):
        for kind in "yxc":
            for seg in (0, 1):
                self.push(kind, k, 0, 0, seg)

    def relay(self, k):
        here = self.here
        for a in range(1, here.ys):
            self.arrive(k, a, 0, 0)
            self.push("x", k, a, 0, 0)
        for b in range(1, here.xs):
            self.arrive(k, 0, b, 1)
            self.push("y", k, 0, b, 1)
        for a in range(1, here.ys):
            self.arrive(k, a, 0, 1)
            for seg in (0, 1):
                self.push("c", k, a, 0, seg)
        for b in range(1, here.xs):
            self.arrive(k, 0, b, 0)
            for seg in (0, 1):
                self.push("c", k, 0, b, seg)

    def corner(self, k):
        for a in range(1, self.here.ys):
            for b in range(1, self.here.xs):
                for seg in (0, 1):
                    self.arrive(k, a, b, seg)
                    self.push("c", k, a, b, seg)

    def twin(self, k):
        here = self.here
        for c in range(1, here.cores):
            for a in range(here.ys):
                for b in range(here.xs):
                    for seg in (0, 1):
                        self.arrive(k, a, b, seg, c)

    def events(self):
        return self.here.zs + 3

    def event(self, t):
        zs = self.here.zs
        if t == 0:
            for seg in (0, 1):
                self.push("z", 0, 0, 0, seg)
            self.spread(0)
        elif t < zs:
            for seg in (0, 1):
                self.arrive(self.order[t], 0, 0, seg)
            self.spread(self.order[t])
            self.relay(self.order[t - 1])
        elif t == zs:
            self.relay(self.order[zs - 1])
            for k in self.order[: zs // 2]:
                self.corner(k)
        elif t == zs + 1:
            for k in self.order[zs // 2 :]:
                self.corner(k)
        else:
            for k in self.order:
                self.twin(k)

    def finish(self):
        for key in self.keys:
            self.copy(key).wait_send()


def gatherer_keys(zs, ys, xs, cores):
    keys = [("z", 0, 0, 0, seg, k) for seg in (0, 1) for k in range(1, zs)]
    for k in range(zs):
        for seg in (0, 1):
            keys += [("y", k, 0, 0, seg, a) for a in range(1, ys)]
            keys += [("x", k, 0, 0, seg, b) for b in range(1, xs)]
        keys += [("x", k, a, 0, 0, b) for a in range(1, ys) for b in range(1, xs)]
        keys += [("y", k, 0, b, 1, a) for a in range(1, ys) for b in range(1, xs)]
        keys += [("c", k, a, b, seg, c) for a in range(ys) for b in range(xs) for seg in (0, 1) for c in range(1, cores)]
    return keys


def gather_kernel(dp, fsdp, rows, qk_ref, vt_ref, ot_ref, vec_ref, upb_ref, tok_ref, cot_ref, all_ref, small_ref, tok_out, cot_out, wide, block, part, slab, rows_s, turned_s, in_qk, in_vt, in_ot, in_vec, in_upb, in_sem, send, recv, small_send, small_recv, local, turn_sem):
    here = Place(dp, fsdp)
    zs, ys, xs, cores = here.zs, here.ys, here.xs, here.cores
    u, w = vt_ref.shape
    me = here.to()
    peers = [here.to(dz=k) for k in range(1, zs)] + [here.to(dc=k) for k in range(1, cores)]
    peers += [here.to(dy=a, dx=b) for a in range(ys) for b in range(xs) if a or b]

    loads = []
    for ref, into in ((qk_ref, in_qk), (vt_ref, in_vt), (ot_ref, in_ot), (vec_ref, in_vec), (upb_ref, in_upb)):
        loads.append(pltpu.make_async_copy(ref, into, in_sem.at[len(loads)]))
        loads[-1].start()
    slots, images, d = tok_ref.shape
    spans = [(lo, min(lo + 128, d)) for lo in range(0, d, 128)]
    arrivals = [pltpu.make_async_copy(ref, slab.at[n], turn_sem.at[n]) for n, ref in enumerate((tok_ref, cot_ref))]
    for copy in arrivals:
        copy.start()

    def widen_all(n):
        arrivals[n].wait()

        def widen(k, _):
            for c, (lo, hi) in enumerate(spans):
                rows_s[c, pl.ds(pl.multiple_of(k * images, 8), images), 0 : hi - lo] = slab[n, k, :, lo:hi].astype(f32)
            return 0

        lax.fori_loop(0, slots, widen, 0, unroll=4)

    def pick_all(n, out, first, count):
        def pick(k, _):
            for c, (lo, hi) in enumerate(spans):
                turned_s[n, k, :, lo:hi] = rows_s[c, pl.ds(k, slots, stride=images), :][:, 0 : hi - lo].astype(bf16)
            return 0

        lax.fori_loop(first, first + count, pick, 0)
        copy = pltpu.make_async_copy(turned_s.at[n, pl.ds(first, count)], out.at[pl.ds(first, count)], turn_sem.at[n])
        copy.start()
        return copy

    wide[...] = jnp.zeros_like(wide)
    part[...] = jnp.zeros_like(part)
    for copy in loads:
        copy.wait()
    wide[0:u, 0:w] = in_ot[...]
    wide[u : 2 * u, 0:w] = in_vt[...]
    for k in range(in_qk.shape[1] // w):
        wide[(k + 2) * u : (k + 3) * u, 0:w] = in_qk[:, k * w : (k + 1) * w]
    block[...] = wide[...].astype(bf16)
    part[0:6, 0:w] = in_vec[...]
    for r in range(in_upb.shape[1] // w):
        part[6 + r : 7 + r, 0:w] = in_upb[:, r * w : (r + 1) * w]

    greet(peers)
    gatherer = Gatherer(here, rows, block, all_ref, send, recv)
    gatherer.event(0)
    own_copy = pltpu.make_async_copy(block, all_ref.at[me[0], me[1]], local.at[0])
    own_copy.start()
    small_copy = pltpu.make_async_copy(part, small_ref.at[me[1]], local.at[1])
    small_copy.start()
    smalls = []
    for a in range(ys):
        for b in range(xs):
            if a or b:
                n = len(smalls)
                copy = pltpu.make_async_remote_copy(
                    src_ref=part,
                    dst_ref=small_ref.at[me[1]],
                    send_sem=small_send.at[n],
                    recv_sem=small_recv.at[me[1]],
                    device_id=here.to(dy=a, dx=b),
                    device_id_type=MESH,
                )
                copy.start()
                smalls.append(copy)
    turns = []
    jobs = [
        lambda: widen_all(0),
        lambda: turns.append(pick_all(0, tok_out, 0, images)),
        lambda: widen_all(1),
        lambda: turns.append(pick_all(1, cot_out, 0, images)),
    ]
    for t in range(1, gatherer.events()):
        if jobs:
            jobs.pop(0)()
        gatherer.event(t)
    for job in jobs:
        job()
    for a in range(ys):
        for b in range(xs):
            if a or b:
                peer = here.to(dy=a, dx=b)
                pltpu.make_async_remote_copy(
                    src_ref=part,
                    dst_ref=small_ref.at[peer[1]],
                    send_sem=small_send.at[0],
                    recv_sem=small_recv.at[peer[1]],
                    device_id=me,
                    device_id_type=MESH,
                ).wait_recv()
    gatherer.finish()
    for copy in smalls:
        copy.wait_send()
    own_copy.wait()
    small_copy.wait()
    for copy in turns:
        copy.wait()


def shape_of(dp, fsdp):
    cores = 2 if dp % 2 == 0 else 1
    ys = max(v for v in range(1, fsdp + 1) if fsdp % v == 0 and v * v <= fsdp)
    return dp // cores, ys, fsdp // ys, cores


def gather_all(dp, fsdp, rows, qk, vt, ot, vectors, up_bias, tokens, cotangent):
    images, slots, d = tokens.shape
    flat_bias = up_bias.reshape(1, -1)
    shards = (qk, vt, ot, vectors, flat_bias)
    return pl.pallas_call(
        partial(gather_kernel, dp, fsdp, rows),
        out_shape=[
            jax.ShapeDtypeStruct((dp, fsdp, rows, 128), bf16),
            jax.ShapeDtypeStruct((fsdp, 16, 128), f32),
            jax.ShapeDtypeStruct((images, slots, d), bf16),
            jax.ShapeDtypeStruct((images, slots, d), bf16),
        ],
        in_specs=[pl.BlockSpec(memory_space=pl.ANY)] * 7,
        out_specs=[pl.BlockSpec(memory_space=pl.ANY)] * 4,
        scratch_shapes=[
            pltpu.VMEM((rows, 128), f32),
            pltpu.VMEM((rows, 128), bf16),
            pltpu.VMEM((16, 128), f32),
            pltpu.VMEM((2, slots, images, d), bf16),
            pltpu.VMEM((-(-d // 128), slots * images, 128), f32),
            pltpu.VMEM((2, images, slots, d), bf16),
            *[pltpu.VMEM(v.shape, f32) for v in shards],
            pltpu.SemaphoreType.DMA((len(shards),)),
            pltpu.SemaphoreType.DMA((len(gatherer_keys(*shape_of(dp, fsdp))),)),
            pltpu.SemaphoreType.DMA((dp * fsdp, 2)),
            pltpu.SemaphoreType.DMA((fsdp,)),
            pltpu.SemaphoreType.DMA((fsdp,)),
            pltpu.SemaphoreType.DMA((2,)),
            pltpu.SemaphoreType.DMA((2,)),
        ],
        compiler_params=pltpu.CompilerParams(collective_id=0, has_side_effects=True, vmem_limit_bytes=62 * 1024 * 1024),
    )(*shards, tokens.transpose(1, 0, 2), cotangent.transpose(1, 0, 2))


def identity():
    rows = lax.broadcasted_iota(jnp.int32, (PITCH, PITCH), 0)
    cols = lax.broadcasted_iota(jnp.int32, (PITCH, PITCH), 1)
    return jnp.where(rows == cols, 1.0, 0.0).astype(bf16)


def one_hot(shape, w, goal):
    r = lax.broadcasted_iota(jnp.int32, shape, 0)
    c = lax.broadcasted_iota(jnp.int32, shape, 1)
    block, lane = r // 128, r % 128
    return jnp.where((c == goal(block, lane)) & (lane < w), 1.0, 0.0).astype(bf16)


def offset_planes(keys):
    j = lax.broadcasted_iota(jnp.int32, (keys, PITCH), 0)
    i = lax.broadcasted_iota(jnp.int32, (keys, PITCH), 1)
    rj, ri = j // GRID, i // GRID
    dc = ((j - rj * GRID) - (i - ri * GRID)).astype(f32)
    dr = (rj - ri).astype(f32)
    return dc, dr, dc * dc + dr * dr


def gates(locality_ref, heads):
    sig, cosig = [], []
    for h in range(heads):
        s = 1.0 / (1.0 + jnp.exp(-jnp.full((1, PITCH), locality_ref[3, h], f32)))
        sig.append(s)
        cosig.append(1.0 - s)
    return sig, cosig


def windows(heads, hw, d):
    wins = []
    for h in range(heads):
        lo = (h * hw) // 128 * 128
        wins.append((lo, min(lo + PITCH, d), h * hw - lo))
    return wins


def lane_sums(v):
    ones = jnp.ones((16, v.shape[1]), bf16)
    high = v.astype(bf16)
    low = (v - high.astype(f32)).astype(bf16)
    return (mm_nt(ones, high) + mm_nt(ones, low))[0:1]


def column(row):
    return jnp.broadcast_to(row, (128, 128)).T


def norm_stats(x):
    d = x.shape[0]
    mean = jnp.sum(x, axis=0, keepdims=True) * (1.0 / d)
    center = x - mean
    rstd = lax.rsqrt(jnp.sum(center * center, axis=0, keepdims=True) * (1.0 / d) + norm_eps)
    return center * rstd, rstd


def norm_back(grad, gain, normal, rstd):
    d = grad.shape[0]
    pull = grad * gain
    m1 = jnp.sum(pull, axis=0, keepdims=True) * (1.0 / d)
    m2 = jnp.sum(pull * normal, axis=0, keepdims=True) * (1.0 / d)
    return rstd * (pull - m1 - normal * m2)


def turn_in(ref, b, eye, pad_in, out):
    _, slots, d = ref.shape
    pad_in[0:slots, 0:d] = ref[b]
    for lo in range(0, d, PITCH):
        hi = min(lo + PITCH, d)
        out[lo:hi, :] = mm_nt(eye[0 : hi - lo, 0 : hi - lo], pad_in[:, lo:hi]).astype(bf16)


def turned(eye, ref, out_ref, row=0):
    for lo in range(0, ref.shape[1], PITCH):
        hi = min(lo + PITCH, ref.shape[1])
        out_ref[row + lo : row + hi, :] = mm_nt(eye[0 : hi - lo, 0 : hi - lo], ref[:, lo:hi]).astype(bf16)


def attend_kernel(
    images,
    slots,
    heads,
    dp,
    fsdp,
    total_steps,
    locality_ref,
    tok_ref,
    vis_ref,
    all_ref,
    small_ref,
    upt_ref,
    dn_ref,
    xt_ref,
    qkvt_ref,
    pa_0,
    pa_1,
    pa_2,
    pb_0,
    pb_1,
    pb_2,
    mixture_ref,
    wqk_ref,
    wv_ref,
    feed_ref,
    eye,
    pick,
    spread_a,
    spread_b,
    cat_s,
    chunk_s,
    whole_s,
    wide,
    block,
    wqkvt_s,
    vec_s,
    pad_in,
    placed,
    hid_s,
    kn_s,
    win_s,
    sc_s,
    mix_s,
    chunk_sem,
    own_sem,
    send,
    recv,
):
    d = tok_ref.shape[-1]
    u, w = d // dp, d // fsdp
    fu = upt_ref.shape[0]
    ring = chunk_s.shape[0]
    hw = d // heads
    keys = placed.shape[1]
    n = images * PITCH
    scale = hw**-0.5
    step = pl.program_id(0)
    here = Place(dp, fsdp)
    zs, ys, xs, cores = here.zs, here.ys, here.xs, here.cores
    me = here.to()
    gatherer = Gatherer(here, block.shape[0], block, feed_ref, send, recv)
    own_copy = pltpu.make_async_copy(block, feed_ref.at[me[0], me[1]], own_sem.at[0])

    @pl.when(step == 0)
    def _():
        def fetch(k):
            return pltpu.make_async_copy(all_ref.at[k], chunk_s.at[k % ring], chunk_sem.at[k % ring])

        for k in range(ring):
            fetch(k).start()
        wide[...] = jnp.zeros_like(wide)
        wide[0:fu, 0:w] = upt_ref[...]
        wide[up16(fu) : up16(fu) + fu, 0:w] = dn_ref[...]
        block[...] = wide[...].astype(bf16)
        peers = [here.to(dz=k) for k in range(1, zs)] + [here.to(dc=k) for k in range(1, cores)]
        peers += [here.to(dy=k) for k in range(1, ys)] + [here.to(dx=k) for k in range(1, xs)]
        greet(peers)
        gatherer.event(0)
        own_copy.start()

        eye[...] = identity()
        pad_in[...] = jnp.zeros_like(pad_in)
        dc, dr, far = offset_planes(keys)
        for h in range(heads):
            placed[h] = (locality_ref[0, h] * dc + locality_ref[1, h] * dr + locality_ref[2, h] * far) * LOG2E
        pick[...] = one_hot(pick.shape, w, lambda block, lane: block * w + lane)
        goal = lax.broadcasted_iota(jnp.int32, (d, 1), 0)
        goal = goal // w * (2 * w) + goal % w
        lane = lax.broadcasted_iota(jnp.int32, spread_a.shape, 1)
        spread_a[...] = jnp.where(lane == goal, 1.0, 0.0).astype(bf16)
        spread_b[...] = jnp.where(lane == goal + w, 1.0, 0.0).astype(bf16)

        for k in range(dp):
            fetch(k).wait()
            for f in range(fsdp):
                cat_s[:, 128 * f : 128 * (f + 1)] = chunk_s[k % ring, f].astype(f32)
            if k + ring < dp:
                fetch(k + ring).start()
            for p in range(3):
                whole_s[p, u * k : u * (k + 1), :] = cat_s[(p + 1) * u : (p + 2) * u, :]

        def dense(p):
            return mm(whole_s[p].astype(bf16), pick[...]).astype(bf16)

        wqkvt_s[2 * d : 3 * d, :] = dense(0)
        turned(eye, wqkvt_s.at[2 * d : 3 * d], wv_ref)
        joint = mm(dense(1), spread_a[...]) + mm(dense(2), spread_b[...])
        wqk_ref[0] = joint[:, 0:d].astype(bf16)
        wqk_ref[1] = joint[:, d : 2 * d].astype(bf16)
        turned(eye, wqk_ref.at[0], wqkvt_s)
        turned(eye, wqk_ref.at[1], wqkvt_s, d)
        for f in range(fsdp):
            for r in range(2):
                vec_s[r, w * f : w * (f + 1), :] = column(small_ref[f, r : r + 1, :])[0:w]
        for ref in (win_s, mix_s):
            ref[...] = jnp.zeros_like(ref)

    for t in range(1, gatherer.events()):

        @pl.when(step == min(t, total_steps - 1))
        def _(t=t):
            gatherer.event(t)

    def enter(b, _):
        turn_in(tok_ref, b, eye, pad_in, xt_ref.at[b])
        return 0

    lax.fori_loop(0, images, enter, 0)

    for t in range(n // 128):
        at = 128 * t
        normal, _ = norm_stats(xt_ref[at // PITCH, :, at % PITCH : at % PITCH + 128].astype(f32))
        hid_s[:, at : at + 128] = (normal * vec_s[0] + vec_s[1]).astype(bf16)
    joint = mm(wqkvt_s[...], hid_s[...]).astype(bf16)
    for b in range(images):
        qkvt_ref[b] = joint[:, PITCH * b : PITCH * (b + 1)]

    sig, cosig = gates(locality_ref, heads)
    wins = windows(heads, hw, d)

    def forward(b, _):
        kn_s[...] = mm_nt(eye[0:keys, :], qkvt_ref[b, d : 2 * d, :]).astype(bf16)
        key_vis = mm_nt(eye[0:keys, :], jnp.broadcast_to(vis_ref[b, 0:1, :], (PITCH, PITCH)).astype(bf16))
        bias = jnp.where(key_vis > 0.5, 0.0, -1e30)

        def fa(h):
            lo, hi, at = wins[h]
            win_s[h, at : at + hw, :] = qkvt_ref[b, h * hw : (h + 1) * hw, :]
            sc_s[h % 2] = mm(kn_s[:, lo:hi], win_s[h, 0 : hi - lo, :])

        def fb(h):
            scores = sc_s[h % 2] * (scale * LOG2E) + bias
            p = jnp.exp2(scores - jnp.max(scores, axis=0, keepdims=True))
            pa = p * (cosig[h] / jnp.sum(p, axis=0, keepdims=True))
            z = placed[h] + bias
            e = jnp.exp2(z - jnp.max(z, axis=0, keepdims=True))
            pb = e * (sig[h] / jnp.sum(e, axis=0, keepdims=True))
            (pa_0, pa_1, pa_2)[h // 3][b, h % 3] = pa.astype(bf16)
            (pb_0, pb_1, pb_2)[h // 3][b, h % 3] = pb.astype(bf16)
            mix_s[h, 0:keys, :] = (pa + pb).astype(bf16)

        def fc(h):
            mixture_ref[b, h * hw : (h + 1) * hw, :] = mm(
                qkvt_ref[b, 2 * d + h * hw : 2 * d + (h + 1) * hw, :], mix_s[h]
            ).astype(bf16)

        for t in range(heads + 2):
            if t < heads:
                fa(t)
            if t >= 2:
                fc(t - 2)
            if 1 <= t <= heads:
                fb(t - 1)
        return 0

    lax.fori_loop(0, images, forward, 0)

    @pl.when(step == total_steps - 1)
    def _():
        own_copy.wait()
        gatherer.finish()


def run_attend(dp, fsdp, tokens, vis, everything, small, upt, dn, locality, images):
    b, slots, d = tokens.shape
    heads = locality.shape[1]
    keys = up16(slots)
    n = images * PITCH
    u = d // dp
    rows = everything.shape[2]
    ring = dp if fsdp <= 4 else 2
    feed_rows = 2 * up16(upt.shape[0])

    def whole(shape):
        return pl.BlockSpec(shape, lambda g: (0,) * len(shape), pipeline_mode=pl.Buffered(1))

    def per(shape):
        return pl.BlockSpec((images,) + shape, lambda g: (g,) + (0,) * len(shape))

    kept_shapes = [(d, PITCH), (3 * d, PITCH), *[(heads // 3, keys, PITCH)] * 6, (d, PITCH)]
    scratch = [
        ((PITCH, PITCH), bf16),
        ((fsdp * 128, d), bf16),
        ((d, 2 * d), bf16),
        ((d, 2 * d), bf16),
        ((rows, fsdp * 128), f32),
        ((ring, fsdp, rows, 128), bf16),
        ((3, d, fsdp * 128), f32),
        ((feed_rows, 128), f32),
        ((feed_rows, 128), bf16),
        ((3 * d, d), bf16),
        ((2, d, 128), f32),
        ((PITCH, d), bf16),
        ((heads, keys, PITCH), f32),
        ((d, n), bf16),
        ((keys, d), bf16),
        ((heads, PITCH, PITCH), bf16),
        ((2, keys, PITCH), f32),
        ((heads, PITCH, PITCH), bf16),
    ]
    outs = pl.pallas_call(
        partial(attend_kernel, images, slots, heads, dp, fsdp, b // images),
        grid=(b // images,),
        out_shape=[jax.ShapeDtypeStruct((b,) + shape, bf16) for shape in kept_shapes]
        + [
            jax.ShapeDtypeStruct((2, d, d), bf16),
            jax.ShapeDtypeStruct((d, d), bf16),
            jax.ShapeDtypeStruct((dp, fsdp, feed_rows, 128), bf16),
        ],
        in_specs=[
            pl.BlockSpec(memory_space=pltpu.SMEM),
            per((slots, d)),
            per((1, PITCH)),
            pl.BlockSpec(memory_space=pl.ANY),
            whole(small.shape),
            whole(upt.shape),
            whole(dn.shape),
        ],
        out_specs=[per(shape) for shape in kept_shapes]
        + [whole((2, d, d)), whole((d, d)), pl.BlockSpec(memory_space=pl.ANY)],
        scratch_shapes=[pltpu.VMEM(*entry) for entry in scratch]
        + [
            pltpu.SemaphoreType.DMA((ring,)),
            pltpu.SemaphoreType.DMA((1,)),
            pltpu.SemaphoreType.DMA((len(gatherer_keys(*shape_of(dp, fsdp))),)),
            pltpu.SemaphoreType.DMA((dp * fsdp, 2)),
        ],
        compiler_params=pltpu.CompilerParams(
            dimension_semantics=("arbitrary",),
            collective_id=2,
            has_side_effects=True,
            vmem_limit_bytes=62 * 1024 * 1024,
        ),
        cost_estimate=pl.CostEstimate(flops=20_000_000_000, bytes_accessed=70_000_000, transcendentals=0),
    )(locality, tokens, vis, everything, small, upt, dn)
    return outs


def feed_kernel(
    images,
    slots,
    cot_ref,
    vis_ref,
    xt_ref,
    mixture_ref,
    all_ref,
    feed_ref,
    small_ref,
    res_ref,
    dot_ref,
    mg_ref,
    part_ref,
    gsmall_ref,
    eye,
    pick,
    chunk_s,
    chunk_sem,
    o_s,
    wot_s,
    wo_s,
    wupt_s,
    wup_s,
    wdnt_s,
    wdn_s,
    vec_s,
    upb_s,
    pad_in,
    acc_out,
    acc_up,
    acc_down,
    acc_vec,
    acc_upb,
    mixture_s,
    xh2_s,
    rstd_s,
    second_s,
    mid_s,
    cot_s,
    dlow_s,
    up_s,
    back_s,
    act_s,
    ug_s,
    blow_s,
):
    d = cot_ref.shape[-1]
    ff = upb_s.shape[0]
    dp, fsdp, o_at, _ = feed_ref.shape
    u, w = d // dp, d // fsdp
    fu = ff // dp
    dn_at = up16(fu)
    ring = chunk_s.shape[0]
    fits = ring == dp
    split = row_plan(fu, u)[1]
    few = o_s.shape[2]
    n = images * PITCH
    step = pl.program_id(0)

    @pl.when(step == 0)
    def _():
        def fetch(k):
            return pltpu.make_async_copy(
                feed_ref.at[k], chunk_s.at[k % ring, :, pl.ds(0, o_at)], chunk_sem.at[k % ring]
            )

        for k in range(ring):
            fetch(k).start()
        rest = pltpu.make_async_copy(all_ref.at[:, :, pl.ds(0, few)], o_s, chunk_sem.at[ring])
        rest.start()
        eye[...] = identity()
        pad_in[...] = jnp.zeros_like(pad_in)
        pick[...] = one_hot(pick.shape, w, lambda block, lane: block * w + lane)

        def unpack(k, _):
            fetch(k).wait()


            def joined(at):
                return jnp.concatenate([chunk_s[k % ring, f, at : at + fu] for f in range(fsdp)], axis=1)

            big = slice(fu * k, fu * (k + 1))
            acc_up[big, :] = mm(joined(0), pick[...])
            acc_down[big, :] = mm(joined(dn_at), pick[...])
            if k + ring < dp:
                fetch(k + ring).start()
            return 0

        if fits:
            for k in range(dp):
                fetch(k).wait()
                for f in range(fsdp):
                    act_s[fu * k : fu * (k + 1), 128 * f : 128 * (f + 1)] = chunk_s[k, f, 0:fu]
                    ug_s[fu * k : fu * (k + 1), 128 * f : 128 * (f + 1)] = chunk_s[k, f, dn_at : dn_at + fu]
            wupt_s[...] = mm(act_s[...], pick[...]).astype(bf16)
            wdn_s[...] = mm(ug_s[...], pick[...]).astype(bf16)
        else:
            for k in range(dp):
                unpack(k, 0)
            wupt_s[...] = acc_up[...].astype(bf16)
            wdn_s[...] = acc_down[...].astype(bf16)
        turned(eye, wupt_s, wup_s)
        turned(eye, wdn_s, wdnt_s)
        rest.wait()
        for k in range(dp):
            joined = jnp.concatenate([o_s[k, f, 0:u] for f in range(fsdp)], axis=1)
            if fits:
                mid_s[u * k : u * (k + 1), :] = joined.astype(f32)
            else:
                acc_out[u * k : u * (k + 1), :] = mm(joined, pick[...])
        wot_s[...] = (mm(mid_s[...].astype(bf16), pick[...]) if fits else acc_out[...]).astype(bf16)
        turned(eye, wot_s, wo_s)
        for f in range(fsdp):
            for r in range(2, 6):
                vec_s[r, w * f : w * (f + 1), :] = column(small_ref[f, r : r + 1, :])[0:w]
            for r in range(ff // d):
                at = (f * (ff // d) + r) * w
                upb_s[at : at + w, :] = column(small_ref[f, 6 + r : 7 + r, :])[0:w]
        for ref in (acc_out, acc_up, acc_down, acc_vec, acc_upb):
            ref[...] = jnp.zeros_like(ref)

    tiles = [slice(128 * k, 128 * (k + 1)) for k in range(n // 128)]

    def seen(t):
        at = 128 * t
        return vis_ref[at // PITCH, 0:1, at % PITCH : at % PITCH + 128]

    def fold(v):
        total = v[:, 0:128]
        for k in range(1, n // 128):
            total = total + v[:, 128 * k : 128 * (k + 1)]
        return total

    def enter(b, _):
        cols = pl.ds(pl.multiple_of(b * PITCH, PITCH), PITCH)
        turn_in(cot_ref, b, eye, pad_in, cot_s.at[:, cols])
        mixture_s[:, cols] = mixture_ref[b]
        return 0

    lax.fori_loop(0, images, enter, 0)

    def x_tile(t):
        at = 128 * t
        return xt_ref[at // PITCH, :, at % PITCH : at % PITCH + 128].astype(f32)

    for t, tile in enumerate(tiles):
        down = cot_s[:, tile].astype(f32) * seen(t)
        dlow_s[:, tile] = down.astype(bf16)
        acc_vec[3] += down
    mid_s[...] = mm(wot_s[...], mixture_s[...])
    for t, tile in enumerate(tiles):
        middle = x_tile(t) + seen(t) * (mid_s[:, tile] + vec_s[4])
        mid_s[:, tile] = middle
        normal, rstd = norm_stats(middle)
        xh2_s[:, tile] = normal
        rstd_s[0:1, tile] = rstd
        second_s[:, tile] = (normal * vec_s[2] + vec_s[3]).astype(bf16)

    chunk = up_s.shape[1]
    steps = ff // chunk

    def feed_start(c):
        part = slice(c * chunk, (c + 1) * chunk)
        up_s[c % 2] = mm(wupt_s[part, :], second_s[...])
        back_s[c % 2] = mm(wdn_s[part, :], dlow_s[...])

    feed_start(0)
    for c in range(steps):
        if c + 1 < steps:
            feed_start(c + 1)
        part = slice(c * chunk, (c + 1) * chunk)
        act, slope = gelu_parts(up_s[c % 2] + jnp.concatenate([upb_s[part, :]] * (n // 128), axis=1))
        act_s[part, :] = act.astype(bf16)
        ug = (back_s[c % 2] * slope).astype(bf16)
        ug_s[part, :] = ug
        acc_upb[part, :] += fold(ug.astype(f32))

    second_grad = mm(wup_s[...], ug_s[...])
    acc_up[...] += mm_nt(ug_s[...], second_s[...])
    for t, tile in enumerate(tiles):
        grad = second_grad[:, tile]
        normal = xh2_s[:, tile]
        acc_vec[0] += grad * normal
        acc_vec[1] += grad
        middle_grad = cot_s[:, tile].astype(f32) + norm_back(grad, vec_s[2], normal, rstd_s[0:1, tile])
        at = 128 * t
        mg_ref[at // PITCH, :, at % PITCH : at % PITCH + 128] = middle_grad.astype(bf16)
        low = (seen(t) * middle_grad).astype(bf16)
        blow_s[:, tile] = low
        acc_vec[2] += low.astype(f32)
    acc_down[...] += mm_nt(act_s[...], dlow_s[...])
    mixture_grad = mm(wo_s[...], blow_s[...]).astype(bf16)
    for b in range(images):
        dot_ref[b] = mixture_grad[:, PITCH * b : PITCH * (b + 1)]
    acc_out[...] += mm_nt(blow_s[...], mixture_s[...])
    downward = mm(wdnt_s[...], act_s[...])
    for t, tile in enumerate(tiles):
        dlow_s[:, tile] = (mid_s[:, tile] + seen(t) * (downward[:, tile] + vec_s[5])).astype(bf16)
    for b in range(images):
        res_ref[b] = mm_nt(eye[0:slots, :], dlow_s[:, b * PITCH : (b + 1) * PITCH]).astype(bf16)

    @pl.when(step == pl.num_programs(0) - 1)
    def _():
        def put_rest(k):
            return pltpu.make_async_copy(
                chunk_s.at[k % 2, :, pl.ds(0, split - o_at)],
                part_ref.at[k, :, pl.ds(o_at, split - o_at)],
                chunk_sem.at[k % 2],
            )

        chunk_s[...] = jnp.zeros_like(chunk_s)
        for k in [] if fits else range(dp):
            piece = mm_nt(acc_out[u * k : u * (k + 1), :].astype(bf16), pick[...]).astype(bf16)
            if k >= 2:
                put_rest(k - 2).wait()
            for f in range(fsdp):
                chunk_s[k % 2, f, 0:u] = piece[:, 128 * f : 128 * (f + 1)]
            put_rest(k).start()
        for k in [] if fits else range(max(dp - 2, 0), dp):
            put_rest(k).wait()
        def put(k):
            if fits:
                return pltpu.make_async_copy(chunk_s.at[k], part_ref.at[k], chunk_sem.at[k])
            return pltpu.make_async_copy(
                chunk_s.at[k % 2, :, pl.ds(0, o_at)], part_ref.at[k, :, pl.ds(0, o_at)], chunk_sem.at[k % 2]
            )

        def pack(k, _):
            big = slice(fu * k, fu * (k + 1))

            if k >= 2:
                put(k - 2).wait()

            for at, ref in ((0, acc_up), (dn_at, acc_down)):
                piece = mm_nt(ref[big, :].astype(bf16), pick[...]).astype(bf16)
                for f in range(fsdp):
                    chunk_s[k % 2, f, at : at + fu] = piece[:, 128 * f : 128 * (f + 1)]
            put(k).start()
            return 0

        if fits:
            act_s[...] = mm_nt(acc_up[...].astype(bf16), pick[...]).astype(bf16)
            ug_s[...] = mm_nt(acc_down[...].astype(bf16), pick[...]).astype(bf16)
            mid_s[...] = mm_nt(acc_out[...].astype(bf16), pick[...])
            for k in range(dp):
                for f in range(fsdp):
                    lane = slice(128 * f, 128 * (f + 1))
                    chunk_s[k, f, 0:fu] = act_s[fu * k : fu * (k + 1), lane]
                    chunk_s[k, f, dn_at : dn_at + fu] = ug_s[fu * k : fu * (k + 1), lane]
                    chunk_s[k, f, o_at : o_at + u] = mid_s[u * k : u * (k + 1), lane].astype(bf16)
                put(k).start()
        else:
            for k in range(dp):
                pack(k, 0)
        for k in range(0 if fits else max(dp - 2, 0), dp):
            put(k).wait()

        gsmall_ref[...] = jnp.zeros_like(gsmall_ref)
        for f in range(fsdp):
            for r in range(4):
                gsmall_ref[f, 2 + r : 3 + r, 0:w] = lane_sums(acc_vec[r, w * f : w * (f + 1), :])
            for r in range(ff // d):
                lo = (f * (ff // d) + r) * w
                gsmall_ref[f, 6 + r : 7 + r, 0:w] = lane_sums(acc_upb[lo : lo + w, :])


def run_feed(dp, fsdp, cotangent, vis, xt, mixture, everything, feed, small, ff, images):
    b, slots, d = cotangent.shape
    n = images * PITCH
    o_at, split, _ = row_plan(ff // dp, d // dp)
    few = up16(d // dp)
    ring = dp if n == fsdp * 128 else 2

    def whole(shape):
        return pl.BlockSpec(shape, lambda g: (0,) * len(shape), pipeline_mode=pl.Buffered(1))

    def per(shape):
        return pl.BlockSpec((images,) + shape, lambda g: (g,) + (0,) * len(shape))

    scratch = [
        ((PITCH, PITCH), bf16),
        ((fsdp * 128, d), bf16),
        ((ring, fsdp, split if ring == dp else o_at, 128), bf16),
        None,
        ((dp, fsdp, few, 128), bf16),
        ((d, d), bf16),
        ((d, d), bf16),
        ((ff, d), bf16),
        ((d, ff), bf16),
        ((d, ff), bf16),
        ((ff, d), bf16),
        ((6, d, 128), f32),
        ((ff, 128), f32),
        ((PITCH, d), bf16),
        ((d, d), f32),
        ((ff, d), f32),
        ((ff, d), f32),
        ((4, d, 128), f32),
        ((ff, 128), f32),
        ((d, n), bf16),
        ((d, n), f32),
        ((8, n), f32),
        ((d, n), bf16),
        ((d, n), f32),
        ((d, n), bf16),
        ((d, n), bf16),
        ((2, ff // 6, n), f32),
        ((2, ff // 6, n), f32),
        ((ff, n), bf16),
        ((ff, n), bf16),
        ((d, n), bf16),
    ]
    scratch = [pltpu.SemaphoreType.DMA((ring + 1,)) if entry is None else pltpu.VMEM(*entry) for entry in scratch]
    return pl.pallas_call(
        partial(feed_kernel, images, slots),
        grid=(b // images,),
        out_shape=[
            jax.ShapeDtypeStruct((b, slots, d), bf16),
            jax.ShapeDtypeStruct((b, d, PITCH), bf16),
            jax.ShapeDtypeStruct((b, d, PITCH), bf16),
            jax.ShapeDtypeStruct((dp, fsdp, split, 128), bf16),
            jax.ShapeDtypeStruct((fsdp, 16, 128), f32),
        ],
        in_specs=[per((slots, d)), per((1, PITCH)), per((d, PITCH)), per((d, PITCH))]
        + [pl.BlockSpec(memory_space=pl.ANY)] * 2
        + [whole((fsdp, 16, 128))],
        out_specs=[per((slots, d)), per((d, PITCH)), per((d, PITCH)), pl.BlockSpec(memory_space=pl.ANY), whole((fsdp, 16, 128))],
        scratch_shapes=scratch,
        compiler_params=pltpu.CompilerParams(
            dimension_semantics=("arbitrary",), vmem_limit_bytes=63 * 1024 * 1024
        ),
        cost_estimate=pl.CostEstimate(flops=40_000_000_000, bytes_accessed=40_000_000, transcendentals=0),
    )(cotangent, vis, xt, mixture, everything, feed, small)


class Reducer:
    def __init__(self, here, rows, mine, theirs, other, bufs, send, recv):
        self.here, self.mine, self.theirs, self.other = here, mine, theirs, other
        self.got_x, self.got_y, self.got_x2, self.got_y2, self.got_z = bufs
        self.send, self.recv = send, recv
        half = rows // 32 * 16
        self.segs = (pl.ds(0, half), pl.ds(half, rows - half))
        self.order = z_order(here.zs)
        self.keys = reducer_keys(here.zs, here.ys, here.xs, here.cores)

    def f_at(self, dy, dx):
        return self.here.to(dy=dy, dx=dx)[1]

    def copy(self, key):
        here, segs, n = self.here, self.segs, key[1]
        if key[0] == "pair":
            src, dst, target = self.theirs(n), self.other.at[n], here.to(dc=1)
        elif key[0] == "a1":
            _, _, a, b = key
            src, dst, target = self.mine(n).at[self.f_at(a, b), segs[0]], self.got_x.at[n, a, b - 1], here.to(dx=b)
        elif key[0] == "b1":
            _, _, a, b = key
            src, dst, target = self.mine(n).at[self.f_at(a, b), segs[1]], self.got_y.at[n, b, a - 1], here.to(dy=a)
        elif key[0] == "a2":
            src, dst, target = self.mine(n).at[self.f_at(key[2], 0), segs[0]], self.got_y2.at[n, key[2] - 1], here.to(dy=key[2])
        elif key[0] == "b2":
            src, dst, target = self.mine(n).at[self.f_at(0, key[2]), segs[1]], self.got_x2.at[n, key[2] - 1], here.to(dx=key[2])
        else:
            seg = segs[key[2]]
            src, dst, target = self.mine(n).at[self.f_at(0, 0), seg], self.got_z.at[n, seg], here.to(dz=self.order[n])
        at = self.keys.index(key)
        return pltpu.make_async_remote_copy(
            src_ref=src, dst_ref=dst, send_sem=self.send.at[at], recv_sem=self.recv.at[at], device_id=target, device_id_type=MESH
        )

    def add(self, n, f, seg, got):
        ref = self.mine(n)
        ref[f, self.segs[seg]] = (ref[f, self.segs[seg]].astype(f32) + got.astype(f32)).astype(bf16)

    def begin(self):
        if self.here.cores > 1:
            for n in range(self.here.zs):
                self.copy(("pair", n)).start()

    def stage_one(self, n):
        here = self.here
        if here.cores > 1:
            self.copy(("pair", n)).wait_recv()
            ref = self.mine(n)

            def body(f, _):
                ref[f] = (ref[f].astype(f32) + self.other[n, f].astype(f32)).astype(bf16)
                return 0

            lax.fori_loop(0, here.fs, body, 0)
        for a in list(range(1, here.ys)) + [0]:
            for b in range(1, here.xs):
                self.copy(("a1", n, a, b)).start()
        for b in list(range(1, here.xs)) + [0]:
            for a in range(1, here.ys):
                self.copy(("b1", n, a, b)).start()

    def stage_two(self, n):
        here = self.here
        for a in list(range(1, here.ys)) + [0]:
            for b in range(1, here.xs):
                self.copy(("a1", n, a, b)).wait_recv()
                self.add(n, self.f_at(a, 0), 0, self.got_x[n, a, b - 1])
            if a:
                self.copy(("a2", n, a)).start()
        for b in list(range(1, here.xs)) + [0]:
            for a in range(1, here.ys):
                self.copy(("b1", n, a, b)).wait_recv()
                self.add(n, self.f_at(0, b), 1, self.got_y[n, b, a - 1])
            if b:
                self.copy(("b2", n, b)).start()

    def stage_three(self, n):
        here = self.here
        for a in range(1, here.ys):
            self.copy(("a2", n, a)).wait_recv()
            self.add(n, self.f_at(0, 0), 0, self.got_y2[n, a - 1])
        for b in range(1, here.xs):
            self.copy(("b2", n, b)).wait_recv()
            self.add(n, self.f_at(0, 0), 1, self.got_x2[n, b - 1])
        if self.order[n]:
            for seg in (0, 1):
                self.copy(("z", n, seg)).start()

    def turn(self, t):
        zs = self.here.zs
        if t < zs:
            self.stage_one(t)
        if 1 <= t <= zs:
            self.stage_two(t - 1)
        if 2 <= t < zs + 2:
            self.stage_three(t - 2)

    def total(self):
        zs = self.here.zs
        total = self.mine(zs - 1)[self.f_at(0, 0)].astype(f32)
        for n in range(zs - 1):
            for seg in (0, 1):
                self.copy(("z", n, seg)).wait_recv()
            total = total + self.got_z[n].astype(f32)
        return total

    def finish(self):
        for key in self.keys:
            self.copy(key).wait_send()


def z_order(zs):
    return sorted(range(1, zs), key=lambda k: min(k, zs - k)) + [0]


def reducer_keys(zs, ys, xs, cores):
    keys = []
    for n in range(zs):
        if cores > 1:
            keys.append(("pair", n))
        keys += [("a1", n, a, b) for a in range(ys) for b in range(1, xs)]
        keys += [("b1", n, a, b) for a in range(1, ys) for b in range(xs)]
        keys += [("a2", n, a) for a in range(1, ys)] + [("b2", n, b) for b in range(1, xs)]
        if n < zs - 1:
            keys += [("z", n, 0), ("z", n, 1)]
    return keys


def reducer_buffers(zs, ys, xs, rows):
    half = rows // 32 * 16
    rest = rows - half
    return [
        pltpu.VMEM((zs, ys, max(xs - 1, 1), half, 128), bf16),
        pltpu.VMEM((zs, xs, max(ys - 1, 1), rest, 128), bf16),
        pltpu.VMEM((zs, max(xs - 1, 1), rest, 128), bf16),
        pltpu.VMEM((zs, max(ys - 1, 1), half, 128), bf16),
        pltpu.VMEM((zs, rows, 128), bf16),
    ]


def exchange(here, ref, buf, send, recv, base, coordinate, size, targets):
    buf[base + coordinate] = ref[...]
    for k, target in enumerate(targets):
        pltpu.make_async_remote_copy(
            src_ref=ref,
            dst_ref=buf.at[base + coordinate],
            send_sem=send.at[base + k],
            recv_sem=recv.at[base + coordinate],
            device_id=target,
            device_id_type=MESH,
        ).start()

    def add():
        for k in range(1, size):
            pltpu.make_async_remote_copy(
                src_ref=ref,
                dst_ref=buf.at[base + coordinate],
                send_sem=send.at[base + k - 1],
                recv_sem=recv.at[base],
                device_id=here.to(),
                device_id_type=MESH,
            ).wait_send()
        for k in range(1, size):
            at = base + lax.rem(coordinate + k, size)
            pltpu.make_async_remote_copy(
                src_ref=ref,
                dst_ref=buf.at[at],
                send_sem=send.at[base],
                recv_sem=recv.at[at],
                device_id=here.to(),
                device_id_type=MESH,
            ).wait_recv()
        total = buf[base]
        for k in range(1, size):
            total = total + buf[base + k]
        ref[...] = total

    return add


def backward_kernel(
    images,
    slots,
    heads,
    dp,
    fsdp,
    ff,
    total_steps,
    locality_ref,
    xt_ref,
    qkvt_ref,
    pa_0,
    pa_1,
    pa_2,
    pb_0,
    pb_1,
    pb_2,
    dot_ref,
    mg_ref,
    small_ref,
    gsmall_ref,
    wqk_ref,
    wv_ref,
    part_ref,
    tgrad_ref,
    grad_ref,
    sum_ref,
    norm_ref,
    eye,
    pick,
    perm,
    cat_s,
    whole_s,
    vec_s,
    acc_qk,
    acc_v,
    acc_vec,
    acc_place,
    acc_gate,
    hid_s,
    xh_s,
    rstd_s,
    vn_s,
    win_s,
    sc_s,
    mix_s,
    ds_s,
    dqkv_s,
    tg_s,
    last_s,
    a_mine,
    a_other,
    a_x,
    a_y,
    a_x2,
    a_y2,
    a_z,
    b_other,
    b_x,
    b_y,
    b_x2,
    b_y2,
    b_z,
    small_buf,
    norm_buf,
    load,
    a_send,
    a_recv,
    b_send,
    b_recv,
    sm_send,
    sm_recv,
    nm_send,
    nm_recv,
):
    d = xt_ref.shape[1]
    u, w = d // dp, d // fsdp
    _, split, rows_all = row_plan(ff // dp, u)
    hw = d // heads
    keys = acc_place.shape[1]
    n = images * PITCH
    scale = hw**-0.5
    fits = fsdp <= 4
    step = pl.program_id(0)
    count = pl.num_programs(0)
    here = Place(dp, fsdp)
    zs, ys, xs, cores = here.zs, here.ys, here.xs, here.cores
    order = z_order(zs)

    def plane(k, dc=0):
        return here.to(dz=order[k], dc=dc)[0]

    first = Reducer(
        here,
        split,
        lambda k: a_mine.at[k],
        lambda k: part_ref.at[plane(k, 1)],
        a_other,
        (a_x, a_y, a_x2, a_y2, a_z),
        a_send,
        a_recv,
    )
    last = Reducer(
        here,
        rows_all - split,
        lambda k: last_s.at[plane(k)],
        lambda k: last_s.at[plane(k, 1)],
        b_other,
        (b_x, b_y, b_x2, b_y2, b_z),
        b_send,
        b_recv,
    )

    def loading(k):
        return pltpu.make_async_copy(part_ref.at[plane(k)], a_mine.at[k], load.at[k])

    @pl.when(step == 0)
    def _():
        for k in range(zs):
            loading(k).start()
        peers = [here.to(dz=k) for k in range(1, zs)] + [here.to(dc=k) for k in range(1, cores)]
        peers += [here.to(dy=a, dx=b) for a in range(ys) for b in range(xs) if a or b]
        peers = [
            here.to(dz=k, dc=c, dy=a, dx=b)
            for k in range(zs)
            for c in range(cores)
            for a in range(ys)
            for b in range(xs)
            if k or c or a or b
        ]
        greet(peers)
        first.begin()
        eye[...] = identity()
        pick[...] = one_hot(pick.shape, w, lambda block, lane: block * w + lane)
        e = lax.broadcasted_iota(jnp.int32, (2 * d, 1), 0)
        goal = (e % (2 * w)) // w * d + e // (2 * w) * w + e % w
        perm[...] = jnp.where(lax.broadcasted_iota(jnp.int32, perm.shape, 1) == goal, 1.0, 0.0).astype(bf16)
        for f in range(fsdp):
            for r in range(2):
                vec_s[r, w * f : w * (f + 1), :] = column(small_ref[f, r : r + 1, :])[0:w]
        for ref in (acc_qk, acc_v, acc_vec, acc_place, acc_gate, win_s, mix_s, ds_s):
            ref[...] = jnp.zeros_like(ref)
        for k in range(zs):
            loading(k).wait()

    spread = total_steps
    for t in range(zs + 2):

        @pl.when(step == min(t + 1, spread - 1))
        def _(t=t):
            first.turn(t)

    sig, cosig = gates(locality_ref, heads)
    wins = windows(heads, hw, d)
    tiles = [slice(128 * k, 128 * (k + 1)) for k in range(n // 128)]

    def place_of(t):
        at = 128 * t
        return at // PITCH, slice(at % PITCH, at % PITCH + 128)

    for t, tile in enumerate(tiles):
        b, lane = place_of(t)
        normal, rstd = norm_stats(xt_ref[b, :, lane].astype(f32))
        xh_s[:, tile] = normal
        rstd_s[0:1, tile] = rstd
        hid_s[:, tile] = (normal * vec_s[0] + vec_s[1]).astype(bf16)

    def backward(b, _):
        cols = pl.ds(pl.multiple_of(b * PITCH, PITCH), PITCH)
        vn_s[...] = mm_nt(eye[0:keys, :], qkvt_ref[b, 2 * d : 3 * d, :]).astype(bf16)

        def ba(h):
            lo, hi, at = wins[h]
            win_s[h, at : at + hw, :] = dot_ref[b, h * hw : (h + 1) * hw, :]
            sc_s[h % 2] = mm(vn_s[:, lo:hi], win_s[h, 0 : hi - lo, :])

        def bb(h):
            g = sc_s[h % 2]
            pa = (pa_0, pa_1, pa_2)[h // 3][b, h % 3].astype(f32)
            pb = (pb_0, pb_1, pb_2)[h // 3][b, h % 3].astype(f32)
            mix_s[h, 0:keys, :] = (pa_0, pa_1, pa_2)[h // 3][b, h % 3] + (pb_0, pb_1, pb_2)[h // 3][b, h % 3]
            pull_a = jnp.sum(g * pa, axis=0, keepdims=True) / cosig[h]
            pull_b = jnp.sum(g * pb, axis=0, keepdims=True) / sig[h]
            acc_gate[h : h + 1, :] += pull_b - pull_a
            acc_place[h] += pb * (g - pull_b)
            ds_s[h, 0:keys, :] = (pa * (g - pull_a)).astype(bf16)

        def bc(h):
            rows = slice(h * hw, (h + 1) * hw)
            dqkv_s[rows, cols] = (mm(qkvt_ref[b, d + h * hw : d + (h + 1) * hw, :], ds_s[h]) * scale).astype(bf16)
            dqkv_s[d + h * hw : d + (h + 1) * hw, cols] = (mm_nt(qkvt_ref[b, rows, :], ds_s[h]) * scale).astype(bf16)
            dqkv_s[2 * d + h * hw : 2 * d + (h + 1) * hw, cols] = mm_nt(dot_ref[b, rows, :], mix_s[h]).astype(bf16)

        for t in range(heads + 2):
            if t < heads:
                ba(t)
            if t >= 2:
                bc(t - 2)
            if 1 <= t <= heads:
                bb(t - 1)
        return 0

    lax.fori_loop(0, images, backward, 0)

    back = mm(wqk_ref[0], dqkv_s[0:d, :]) + mm(wqk_ref[1], dqkv_s[d : 2 * d, :]) + mm(wv_ref[...], dqkv_s[2 * d : 3 * d, :])
    acc_qk[...] += mm_nt(hid_s[...], dqkv_s[0 : 2 * d, :])
    for t, tile in enumerate(tiles):
        b, lane = place_of(t)
        grad = back[:, tile]
        normal = xh_s[:, tile]
        acc_vec[0] += grad * normal
        acc_vec[1] += grad
        pulled = norm_back(grad, vec_s[0], normal, rstd_s[0:1, tile])
        tg_s[:, tile] = (mg_ref[b, :, lane].astype(f32) + pulled).astype(bf16)
    acc_v[...] += mm_nt(dqkv_s[2 * d : 3 * d, :], hid_s[...])
    for b in range(images):
        tgrad_ref[b] = mm_nt(eye[0:slots, :], tg_s[:, b * PITCH : (b + 1) * PITCH]).astype(bf16)

    @pl.when(step == count - 1)
    def _():
        cat_s[...] = jnp.zeros_like(cat_s)
        acc_qk[...] = mm(acc_qk[...].astype(bf16), perm[...])
        if fits:
            whole_s[0] = mm_nt(acc_v[...].astype(bf16), pick[...])
            whole_s[1] = mm_nt(acc_qk[:, 0:d].astype(bf16), pick[...])
            whole_s[2] = mm_nt(acc_qk[:, d : 2 * d].astype(bf16), pick[...])
        for k in range(dp):
            own = slice(u * k, u * (k + 1))
            if fits:
                for p in range(3):
                    cat_s[p * u : (p + 1) * u, :] = whole_s[p, own, :]
            else:
                cat_s[0:u, :] = mm_nt(acc_v[own, :].astype(bf16), pick[...])
                cat_s[u : 2 * u, :] = mm_nt(acc_qk[own, 0:d].astype(bf16), pick[...])
                cat_s[2 * u : 3 * u, :] = mm_nt(acc_qk[own, d : 2 * d].astype(bf16), pick[...])
            for f in range(fsdp):
                last_s[k, f] = cat_s[:, 128 * f : 128 * (f + 1)].astype(bf16)
        last.begin()

        sum_ref[...] = gsmall_ref[...]
        for f in range(fsdp):
            for r in range(2):
                sum_ref[f, r : r + 1, 0:w] = lane_sums(acc_vec[r, w * f : w * (f + 1), :])
        at = 6 + ff // d
        dc, dr, far = offset_planes(keys)
        rows = [[], [], []]
        for h in range(heads):
            pg = acc_place[h]
            for c, off in enumerate((dc, dr, far)):
                rows[c].append(jnp.sum(pg * off, axis=0, keepdims=True))
            acc_gate[h : h + 1, :] = acc_gate[h : h + 1, :] * (sig[h] * cosig[h])
        sum_ref[0, at + 3 : at + 4, 0 : acc_gate.shape[0]] = lane_sums(acc_gate[...])
        for c in range(3):
            for h in range(heads):
                acc_gate[h : h + 1, :] = rows[c][h]
            sum_ref[0, at + c : at + c + 1, 0 : acc_gate.shape[0]] = lane_sums(acc_gate[...])


        def small_round(base, coordinate, size, targets):
            return exchange(here, sum_ref, small_buf, sm_send, sm_recv, base, coordinate, size, targets)

        pending = small_round(0, here.c, cores, [here.to(dc=k) for k in range(1, cores)])
        total = first.total()
        grad_ref[0:split, :] = total
        squares = jnp.sum((total * total).reshape(split // 8, 8, 128), axis=0)
        for t in range(zs + 2):
            last.turn(t)
            if t == 0:
                pending()
                pending = small_round(cores, here.x, xs, [here.to(dx=b) for b in range(1, xs)])
            if t == 1:
                pending()
                pending = small_round(cores + xs, here.y, ys, [here.to(dy=a) for a in range(1, ys)])
            if t == 2:
                pending()
                pending = small_round(cores + xs + ys, here.z, zs, [here.to(dz=q) for q in range(1, zs)])
        pending()
        total = last.total()
        grad_ref[split:rows_all, :] = total
        norm_ref[...] = squares + jnp.sum((total * total).reshape((rows_all - split) // 8, 8, 128), axis=0)
        at = here.to()
        everyone = [
            here.to(dz=k, dc=c, dy=a, dx=b)
            for k in range(zs)
            for c in range(cores)
            for a in range(ys)
            for b in range(xs)
            if k or c or a or b
        ]
        exchange(here, norm_ref, norm_buf, nm_send, nm_recv, 0, at[0] * fsdp + at[1], dp * fsdp, everyone)()
        first.finish()
        last.finish()


def run_backward(dp, fsdp, slots, kept, small, small_part, wqk, wv, first_part, locality, ff, images):
    b, d, _ = kept[0].shape
    heads = locality.shape[1]
    keys = kept[2].shape[2]
    n = images * PITCH
    _, split, rows = row_plan(ff // dp, d // dp)
    more = rows - split
    cores = 2 if dp % 2 == 0 else 1
    zs = dp // cores
    ys = max(v for v in range(1, fsdp + 1) if fsdp % v == 0 and v * v <= fsdp)
    xs = fsdp // ys
    copies = len(reducer_keys(zs, ys, xs, cores))
    rounds = cores + xs + ys + zs

    def whole(shape):
        return pl.BlockSpec(shape, lambda g: (0,) * len(shape), pipeline_mode=pl.Buffered(1))

    def per(shape):
        mode = pl.Buffered(1) if fsdp > 4 and shape[-1] == PITCH else None
        return pl.BlockSpec((images,) + shape, lambda g: (g,) + (0,) * len(shape), pipeline_mode=mode)

    scratch = [
        pltpu.VMEM((PITCH, PITCH), bf16),
        pltpu.VMEM((fsdp * 128, d), bf16),
        pltpu.VMEM((2 * d, 2 * d), bf16),
        pltpu.VMEM((more, fsdp * 128), f32),
        pltpu.VMEM((3, d, fsdp * 128) if fsdp <= 4 else (1, 8, 128), f32),
        pltpu.VMEM((2, d, 128), f32),
        pltpu.VMEM((d, 2 * d), f32),
        pltpu.VMEM((d, d), f32),
        pltpu.VMEM((2, d, 128), f32),
        pltpu.VMEM((heads, keys, PITCH), f32),
        pltpu.VMEM((-(-heads // 8) * 8, PITCH), f32),
        pltpu.VMEM((d, n), bf16),
        pltpu.VMEM((d, n), f32),
        pltpu.VMEM((8, n), f32),
        pltpu.VMEM((keys, d), bf16),
        pltpu.VMEM((heads, PITCH, PITCH), bf16),
        pltpu.VMEM((2, keys, PITCH), f32),
        pltpu.VMEM((heads, PITCH, PITCH), bf16),
        pltpu.VMEM((heads, PITCH, PITCH), bf16),
        pltpu.VMEM((3 * d, n), bf16),
        pltpu.VMEM((d, n), bf16),
        pltpu.VMEM((dp, fsdp, more, 128), bf16),
        pltpu.VMEM((zs, fsdp, split, 128), bf16),
        pltpu.VMEM((zs, fsdp, split, 128), bf16),
        *reducer_buffers(zs, ys, xs, split),
        pltpu.VMEM((zs, fsdp, more, 128), bf16),
        *reducer_buffers(zs, ys, xs, more),
        pltpu.VMEM((rounds,) + small.shape, f32),
        pltpu.VMEM((fsdp * dp, 8, 128), f32),
        pltpu.SemaphoreType.DMA((zs,)),
        pltpu.SemaphoreType.DMA((copies,)),
        pltpu.SemaphoreType.DMA((copies,)),
        pltpu.SemaphoreType.DMA((copies,)),
        pltpu.SemaphoreType.DMA((copies,)),
        pltpu.SemaphoreType.DMA((rounds,)),
        pltpu.SemaphoreType.DMA((rounds,)),
        pltpu.SemaphoreType.DMA((fsdp * dp,)),
        pltpu.SemaphoreType.DMA((fsdp * dp,)),
    ]
    return pl.pallas_call(
        partial(backward_kernel, images, slots, heads, dp, fsdp, ff, b // images),
        grid=(b // images,),
        out_shape=[
            jax.ShapeDtypeStruct((b, slots, d), bf16),
            jax.ShapeDtypeStruct((rows, 128), f32),
            jax.ShapeDtypeStruct(small.shape, f32),
            jax.ShapeDtypeStruct((8, 128), f32),
        ],
        in_specs=[pl.BlockSpec(memory_space=pltpu.SMEM)]
        + [per(v.shape[1:]) for v in kept]
        + [whole(small.shape), whole(small.shape), whole((2, d, d)), whole((d, d)), pl.BlockSpec(memory_space=pl.ANY)],
        out_specs=[per((slots, d)), whole((rows, 128)), whole(small.shape), whole((8, 128))],
        scratch_shapes=scratch,
        compiler_params=pltpu.CompilerParams(
            dimension_semantics=("arbitrary",),
            collective_id=1,
            has_side_effects=True,
            vmem_limit_bytes=63 * 1024 * 1024,
        ),
        cost_estimate=pl.CostEstimate(flops=25_000_000_000, bytes_accessed=70_000_000, transcendentals=0),
    )(locality, *kept, small, small_part, wqk, wv, first_part)


def adamw(parameter, moment_one, moment_two, gradient, rate, decay_rate):
    first_new = beta_one * moment_one + (1.0 - beta_one) * gradient
    second_new = beta_two * moment_two + (1.0 - beta_two) * gradient * gradient
    first_hat = first_new / (1.0 - beta_one**STEP)
    second_hat = second_new / (1.0 - beta_two**STEP)
    new_value = parameter - rate * (
        first_hat / (jnp.sqrt(second_hat) + adam_eps) + decay_rate * parameter
    )
    return (new_value, first_new, second_new)


def update_kernel(heads, *refs):
    grad_ref, small_ref, norm_ref = refs[0:3]
    states = [refs[3 + 3 * k : 6 + 3 * k] for k in range(8)]
    outs = refs[27:]
    small = small_ref[...]
    norm = jnp.sqrt(jnp.sum(norm_ref[...], keepdims=True) + jnp.sum(small * small, keepdims=True)[0])
    factor = clip_limit / jnp.maximum(norm, clip_limit)
    outs[0][...] = norm
    u, w = states[1][0].shape
    fu = states[3][0].shape[0]
    o_at, split, _ = row_plan(fu, u)
    starts = {1: split, 2: o_at, 3: 0, 4: up16(fu)}

    def matrix(k, state, gradient, place):
        new_value, first_new, second_new = adamw(
            state[0][place], state[1][place], state[2][place], gradient * factor, learn_rate, weight_decay
        )
        outs[1 + 4 * k][place] = new_value
        outs[2 + 4 * k][place] = new_value.astype(bf16)
        outs[3 + 4 * k][place] = first_new
        outs[4 + 4 * k][place] = second_new

    at = split + u
    gradient = jnp.concatenate([grad_ref[at : at + u, 0:w], grad_ref[at + u : at + 2 * u, 0:w]], axis=1)
    matrix(0, states[0], gradient, ...)
    for k in (1, 2, 3, 4):
        rows = states[k][0].shape[0]
        matrix(k, states[k], grad_ref[starts[k] : starts[k] + rows, 0:w], ...)
    mine = small_ref[lax.axis_index("fsdp")]
    share = states[6][0].shape[1] // w
    row = jnp.concatenate([mine[6 + r : 7 + r, 0:w] for r in range(share)], axis=1)
    gradients = (mine[0:6, 0:w], row, small_ref[0, 6 + share : 10 + share, 0:heads])
    for k in range(3):
        state = states[5 + k]
        new_value, first_new, second_new = adamw(
            state[0][...], state[1][...], state[2][...], gradients[k] * factor, small_rate, 0.0
        )
        outs[21 + 3 * k][...] = new_value
        outs[22 + 3 * k][...] = first_new
        outs[23 + 3 * k][...] = second_new


def update(heads, grad, small, norm, states):
    shapes = [jax.ShapeDtypeStruct((1, 1), f32)]
    for k in range(5):
        shape = states[3 * k].shape
        shapes += [jax.ShapeDtypeStruct(shape, kind) for kind in (f32, bf16, f32, f32)]
    for k in range(5, 8):
        shapes += [jax.ShapeDtypeStruct(states[3 * k].shape, f32)] * 3
    return pl.pallas_call(
        partial(update_kernel, heads),
        out_shape=shapes,
        in_specs=[pl.BlockSpec(memory_space=pltpu.VMEM)] * 27,
        out_specs=[pl.BlockSpec(memory_space=pltpu.VMEM)] * len(shapes),
        compiler_params=pltpu.CompilerParams(vmem_limit_bytes=62 * 1024 * 1024),
    )(grad, small, norm, *states)


def body(
    dp,
    fsdp,
    tokens,
    keep_mask,
    cotangent,
    qk_weight,
    qk_first,
    qk_second,
    value_weight,
    value_first,
    value_second,
    out_weight,
    out_first,
    out_second,
    up_weight,
    up_first,
    up_second,
    down_weight,
    down_first,
    down_second,
    vectors,
    vectors_first,
    vectors_second,
    up_bias,
    up_bias_first,
    up_bias_second,
    locality,
    locality_first,
    locality_second,
):
    d = tokens.shape[-1]
    heads = locality.shape[1]
    ff = up_bias.shape[0] * fsdp
    images = 2 if fsdp <= 4 else 1
    vis = jnp.pad(keep_mask.astype(f32), ((0, 0), (0, PITCH - tokens.shape[1])))[:, None, :]
    everything, small, tokens, cotangent = gather_all(
        dp,
        fsdp,
        up16(4 * d // dp),
        qk_weight,
        value_weight.T,
        out_weight.T,
        vectors,
        up_bias,
        tokens,
        cotangent,
    )
    xt, qkvt, *soft, mixture, wqk, wv, feed = run_attend(
        dp, fsdp, tokens, vis, everything, small, up_weight.T, down_weight, locality, images
    )
    result, mixture_grad, middle_grad, first_part, small_part = run_feed(
        dp, fsdp, cotangent, vis, xt, mixture, everything, feed, small, ff, images
    )
    kept = (xt, qkvt, *soft, mixture_grad, middle_grad)
    token_grad, grad, small_sum, norm = run_backward(
        dp, fsdp, tokens.shape[1], kept, small, small_part, wqk, wv, first_part, locality, ff, images
    )

    def flat(v):
        return v.reshape(1, -1)

    states = [qk_weight, qk_first, qk_second]
    states += [v.T for v in (value_weight, value_first, value_second, out_weight, out_first, out_second)]
    states += [v.T for v in (up_weight, up_first, up_second)]
    states += [down_weight, down_first, down_second, vectors, vectors_first, vectors_second]
    states += [flat(up_bias), flat(up_bias_first), flat(up_bias_second), locality, locality_first, locality_second]
    outs = list(update(heads, grad, small_sum, norm, states))
    for k in range(5, 17):
        outs[k] = outs[k].T
    for k in (24, 25, 26):
        outs[k] = outs[k].reshape(up_bias.shape)
    outs[0] = outs[0].reshape(())
    return (result, token_grad, *outs)


def solution(mesh):
    placed = (
        P(("dp", "fsdp"), None, None),
        P(("dp", "fsdp"), None),
        P(("dp", "fsdp"), None, None),
        P("dp", "fsdp"),
        P("dp", "fsdp"),
        P("dp", "fsdp"),
        P("fsdp", "dp"),
        P("fsdp", "dp"),
        P("fsdp", "dp"),
        P("fsdp", "dp"),
        P("fsdp", "dp"),
        P("fsdp", "dp"),
        P("fsdp", "dp"),
        P("fsdp", "dp"),
        P("fsdp", "dp"),
        P("dp", "fsdp"),
        P("dp", "fsdp"),
        P("dp", "fsdp"),
        P(None, "fsdp"),
        P(None, "fsdp"),
        P(None, "fsdp"),
        P("fsdp"),
        P("fsdp"),
        P("fsdp"),
        P(),
        P(),
        P(),
    )
    return jax.shard_map(
        partial(body, mesh.shape["dp"], mesh.shape["fsdp"]),
        mesh=mesh,
        in_specs=placed,
        out_specs=(
            P(("dp", "fsdp"), None, None),
            P(("dp", "fsdp"), None, None),
            P(),
            P("dp", "fsdp"),
            P("dp", "fsdp"),
            P("dp", "fsdp"),
            P("dp", "fsdp"),
            P("fsdp", "dp"),
            P("fsdp", "dp"),
            P("fsdp", "dp"),
            P("fsdp", "dp"),
            P("fsdp", "dp"),
            P("fsdp", "dp"),
            P("fsdp", "dp"),
            P("fsdp", "dp"),
            P("fsdp", "dp"),
            P("fsdp", "dp"),
            P("fsdp", "dp"),
            P("fsdp", "dp"),
            P("dp", "fsdp"),
            P("dp", "fsdp"),
            P("dp", "fsdp"),
            P("dp", "fsdp"),
            P(None, "fsdp"),
            P(None, "fsdp"),
            P(None, "fsdp"),
            P("fsdp"),
            P("fsdp"),
            P("fsdp"),
            P(),
            P(),
            P(),
        ),
        check_vma=False,
    )
```
